32 devices in a mesh: seq: 16 (over z, y, core), txt: 2 (over x).
Axes of the slice: x: 2, y: 2, z: 4, core: 2. Of those that a mesh axis runs over, the one named last changes fastest.
Arguments:
- video_tokens: bfloat16 [8192, 1536], P('seq'), may hold values from -6 to 6
- cotangent: bfloat16 [8192, 1536], P('seq'), may hold values from -6 to 6
- condition: bfloat16 [49, 1024], replicated, may hold values from -6 to 6
- captions: bfloat16 [48, 64, 4096], P('seq', 'txt'), may hold values from -6 to 6
- long_caption: bfloat16 [64, 4096], P('txt'), may hold values from -6 to 6
- null_embed: bfloat16 [64, 4096], P('txt'), may hold values from -6 to 6
- query_key_value: bfloat16 [1536, 3, 1536], P('seq', None, 'txt'), may hold values from -0.15625 to 0.15625
- out_weight: bfloat16 [1536, 1536], P('seq', 'txt'), may hold values from -0.15625 to 0.15625
- gate_weight: bfloat16 [1536, 4096], P('seq', 'txt'), may hold values from -0.15625 to 0.15625
- up_weight: bfloat16 [1536, 4096], P('seq', 'txt'), may hold values from -0.15625 to 0.15625
- down_weight: bfloat16 [1536, 4096], P('seq', 'txt'), may hold values from -0.09375 to 0.09375
- text_weight: bfloat16 [4096, 2, 1536], P('seq', None, 'txt'), may hold values from -0.09375 to 0.09375
- ada_weight: bfloat16 [1024, 6144], P(None, ('seq', 'txt')), may hold values from -0.1875 to 0.1875
- ada_bias: float32 [6144], P(('seq', 'txt')), may hold values from -1.75 to 1.75
- norm_gains: float32 [7, 1536], replicated, may hold values from 0.25 to 1.75
- head_gates: float32 [24], replicated, may hold values from -1.5 to 1.5
- clip_lengths: int32 [16, 3], P('seq'), may hold values from 1 to 224, 448 in all within a row
- null_mask: int32 [49], replicated, may hold values from 0 to 1, as said below
- text_lengths: int32 [49], replicated, may hold values from 16 to 64, as said below
Outputs:
- block_out: bfloat16 [8192, 1536], P('seq')
- video_grad: float32 [8192, 1536], P('seq')
- condition_grad: float32 [49, 1024], replicated
- query_key_value_grad: float32 [1536, 3, 1536], P('seq', None, 'txt')
- out_weight_grad: float32 [1536, 1536], P('seq', 'txt')
- gate_weight_grad: float32 [1536, 4096], P('seq', 'txt')
- up_weight_grad: float32 [1536, 4096], P('seq', 'txt')
- down_weight_grad: float32 [1536, 4096], P('seq', 'txt')
- text_weight_grad: float32 [4096, 2, 1536], P('seq', None, 'txt')
- ada_weight_grad: float32 [1024, 6144], P(None, ('seq', 'txt'))
- ada_bias_grad: float32 [6144], P(('seq', 'txt'))
- null_grad: float32 [64, 4096], replicated
- norm_gains_grad: float32 [7, 1536], replicated
- head_gates_grad: float32 [24], replicated
The draws below stay inside these ranges and needn't reach their ends.
Inputs may be any that keep to these rules, and one draw needn't show every extreme that they name: `clip_lengths`: row s lists, in order, the lengths of the 3 short clips that follow the 64 long-clip rows on index s of seq; each row sums to 448. `null_mask`: entry 48, that of the long clip, is 0; among the short clips both values occur. Clip c reads its caption's first text_lengths[c] tokens; entry 48 belongs to the long clip.
All inputs are finite; a program needn't handle non-finite values.
Results may differ from the reference program's by a relative error of at most 0.01615.
Values may be sent and summed in bfloat16 or wider, within the bound.
No kernel may reach another device: no remote copies, remote signals or barrier semaphores. Data moves between devices by JAX's collectives and lax.ppermute only.
A program may use at most 320 MiB of HBM per device.

```python
import math
from functools import partial
import jax
import jax.numpy as jnp
import numpy as np
from jax import lax

D = 1536
H = 24
HD = 64
FF = 4096
TD = 4096
CD = 1024
TXT_LEN = 64
LONG_DEV = 64
SHORT_DEV = 448
SHORTS = 3
TOK_DEV = 512
TOKENS = 8192
LONG = 1024
CAPS = 48
CLIPS = 49
N_SEQ = 16


def draw_null_mask(key, part):
    key = jax.random.fold_in(key, 11)
    first_key, second_key = jax.random.split(key)
    flags = (jax.random.randint(first_key, (CAPS,), 0, 4) == 0).astype(jnp.int32)
    order = jax.random.permutation(second_key, CAPS)
    places = jnp.arange(CAPS)
    flags = jnp.where(places == order[0], 1, flags)
    flags = jnp.where(places == order[1], 0, flags)
    return jnp.concatenate([flags, jnp.zeros((1,), jnp.int32)]).astype(jnp.int32)


def draw_text_lengths(key, part):
    key = jax.random.fold_in(key, 23)
    first_key, second_key = jax.random.split(key)
    lengths = jax.random.randint(first_key, (CLIPS,), TXT_LEN // 4, TXT_LEN + 1)
    order = jax.random.permutation(second_key, CLIPS)
    places = jnp.arange(CLIPS)
    lengths = jnp.where(places == order[0], TXT_LEN, lengths)
    lengths = jnp.where(places == order[1], TXT_LEN // 4, lengths)
    return lengths.astype(jnp.int32)


def steps_of(stream_key, shape, shards, least, high):
    loudness, own = 1.0, jax.random.fold_in(stream_key, 6)
    for dim, parts in shards:
        draws = jnp.exp(jax.random.uniform(jax.random.fold_in(own, dim), (parts,), jnp.float32, least / len(shards), high / len(shards)))
        loudness = loudness * jnp.repeat(draws, shape[dim] // parts).reshape([-1 if axis == dim else 1 for axis in range(len(shape))])
    return loudness


def profile(number_of, total, bound, skew):
    portions = [(1 << 20) // math.isqrt(rank ** skew) + 1 for rank in range(2, number_of + 1)]
    rest, given = total - bound - (number_of - 1), [1] * (number_of - 1)
    while rest > 0:
        movable = [i for i in range(number_of - 1) if given[i] < bound]
        whole, left = sum([portions[i] for i in movable]), rest
        for i in movable:
            addition = min(bound - given[i], max(1, left * portions[i] // whole), rest)
            given[i] = given[i] + addition
            rest = rest - addition
    return np.array([bound] + given)


def uneven_parts(stream_key, amount, total, reach, slope):
    if amount == 2:
        one = jax.random.randint(stream_key, (), max(1, total - reach), min(reach, total - 1) + 1)
        return jnp.stack([one, total - one])
    tallies = jnp.asarray(profile(amount, total, reach, slope), jnp.int32)
    twos = (amount - 1) // 2
    giver, receiver = tallies[1:1 + 2 * twos:2], tallies[2:2 + 2 * twos:2]
    room = jnp.minimum(giver - 1, reach - receiver)
    moved = jax.random.randint(jax.random.fold_in(stream_key, 1), (twos,), 0, 1 << 20) % (room + 1)
    tallies = tallies.at[1:1 + 2 * twos:2].set(giver - moved).at[2:2 + 2 * twos:2].set(receiver + moved)
    return tallies[jax.random.permutation(jax.random.fold_in(stream_key, 2), amount)]


def noise(rng, dims, width, limit, cuts=(), kind=jnp.bfloat16):
    values = width * jax.random.normal(rng, dims, jnp.float32)
    if cuts:
        values = values * steps_of(rng, dims, cuts, -0.22, 0.18)
    return jnp.clip(values, -limit, limit).astype(kind)


def setup_inputs(seed: int = 0) -> dict:
    splits = jax.random.split(jax.random.key(seed), 20)
    video_tokens = noise(splits[0], (TOKENS, D), 1.0, 6.0, ((0, 16),))
    cotangent = noise(splits[1], (TOKENS, D), 1.0, 6.0, ((0, 16),))
    condition = noise(splits[2], (CLIPS, CD), 1.0, 6.0)
    captions = noise(splits[3], (CAPS, TXT_LEN, TD), 1.0, 6.0, ((0, 16), (1, 2)))
    long_caption = noise(splits[4], (TXT_LEN, TD), 1.0, 6.0, ((0, 2),))
    null_embed = noise(splits[5], (TXT_LEN, TD), 1.0, 6.0, ((0, 2),))
    query_key_value = noise(splits[6], (D, 3, D), D ** -0.5, 0.15625, ((0, 16), (2, 2)))
    out_weight = noise(splits[7], (D, D), D ** -0.5, 0.15625, ((0, 16), (1, 2)))
    gate_weight = noise(splits[8], (D, FF), D ** -0.5, 0.15625, ((0, 16), (1, 2)))
    up_weight = noise(splits[9], (D, FF), D ** -0.5, 0.15625, ((0, 16), (1, 2)))
    down_weight = noise(splits[10], (D, FF), FF ** -0.5, 0.09375, ((0, 16), (1, 2)))
    text_weight = noise(splits[11], (TD, 2, D), TD ** -0.5, 0.09375, ((0, 16), (2, 2)))
    ada_weight = noise(splits[12], (CD, 4 * D), CD ** -0.5, 0.1875, ((1, 32),))
    ada_bias = noise(splits[13], (4 * D,), 0.3, 1.75, ((0, 32),), jnp.float32)
    norm_gains = jnp.clip(1.0 + 0.15 * jax.random.normal(splits[14], (7, D), jnp.float32), 0.25, 1.75)
    head_gates = jnp.clip(jax.random.uniform(splits[15], (H,), jnp.float32, -1.5, 1.5), -1.5, 1.5)
    clip_lengths = jax.vmap(lambda own: uneven_parts(own, SHORTS, SHORT_DEV, SHORT_DEV // 2, 2))(jax.random.split(splits[16], N_SEQ)).reshape((N_SEQ, SHORTS)).astype(jnp.int32)
    null_mask = draw_null_mask(jax.random.fold_in(splits[19], 71), 0)
    text_lengths = draw_text_lengths(jax.random.fold_in(splits[19], 71), 0)
    return dict(video_tokens=video_tokens, cotangent=cotangent, condition=condition, captions=captions, long_caption=long_caption, null_embed=null_embed, query_key_value=query_key_value, out_weight=out_weight, gate_weight=gate_weight, up_weight=up_weight, down_weight=down_weight, text_weight=text_weight, ada_weight=ada_weight, ada_bias=ada_bias, norm_gains=norm_gains, head_gates=head_gates, clip_lengths=clip_lengths, null_mask=null_mask, text_lengths=text_lengths)


epsilon = 1e-05
negative = -1e+30
highest = lax.Precision.HIGHEST

@jax.custom_vjp
def low(v):
    return lax.optimization_barrier(v.astype(jnp.bfloat16)).astype(jnp.float32)

@jax.custom_vjp
def low_back(v):
    return v

def low_keep(v):
    return (low(v), None)

def low_pass(kept, grad):
    return (grad,)

def back_keep(v):
    return (v, None)

def back_low(kept, grad):
    return (low(grad),)
low.defvjp(low_keep, low_pass)
low_back.defvjp(back_keep, back_low)

def layout(lengths_row, seq_index, long_rows, short_rows):
    clip_count = lengths_row.shape[0]
    clip_ends = jnp.cumsum(lengths_row).astype(jnp.int32)
    clip_starts = clip_ends - lengths_row
    row_ids = jnp.arange(short_rows, dtype=jnp.int32)
    local_clip = lax.optimization_barrier(jnp.sum((row_ids[:, None] >= clip_ends[None, :clip_count - 1]).astype(jnp.int32), axis=1))
    chosen = local_clip[:, None] == jnp.arange(clip_count, dtype=jnp.int32)[None, :]
    clip_begin = lax.optimization_barrier(jnp.sum(jnp.where(chosen, clip_starts[None, :], 0), axis=1)).astype(jnp.int32)
    clip_local = jnp.concatenate([jnp.full((long_rows,), clip_count, jnp.int32), local_clip])
    long_place = (seq_index * long_rows + jnp.arange(long_rows, dtype=jnp.int32)).astype(jnp.int32)
    position = jnp.concatenate([long_place, row_ids - clip_begin])
    return (clip_local, position)

def rotate(values, position):
    half_dim = values.shape[-1] // 2
    frequency = jnp.exp(jnp.arange(half_dim, dtype=jnp.float32) * (-math.log(10000.0) / half_dim))
    angles = position.astype(jnp.float32)[..., None] * frequency
    cosine = jnp.cos(angles)[..., None, :]
    sine_part = jnp.sin(angles)[..., None, :]
    front_part = values[..., :half_dim]
    back_part = values[..., half_dim:]
    return jnp.concatenate([front_part * cosine - back_part * sine_part, front_part * sine_part + back_part * cosine], axis=-1)

def rms_norm(values):
    return values * lax.rsqrt(lax.optimization_barrier(jnp.mean(values * values, axis=-1, keepdims=True)) + epsilon)

def head_norm(values, gain_row):
    shaped = values.reshape(values.shape[:-1] + (H, HD))
    return rms_norm(shaped) * gain_row.reshape(H, HD)

def attend(query_part, key_part, value_part, visible):
    scale_value = query_part.shape[-1] ** (-0.5)
    scores = low_back(jnp.einsum('qhe,khe->hqk', query_part, key_part, precision=highest) * scale_value)
    weights = jax.nn.softmax(jnp.where(visible[None], scores, negative), axis=-1)
    return jnp.einsum('hqk,khe->qhe', low(weights), value_part, precision=highest)

def block_forward(video_tokens, condition, null_embed, query_key_value, out_weight, gate_weight, up_weight, down_weight, text_weight, ada_weight, ada_bias, norm_gains, head_gates, captions, long_caption, clip_lengths, null_mask, text_lengths):
    shifted = low(jax.nn.silu(condition))
    modulation = jnp.dot(shifted, ada_weight, precision=highest) + ada_bias
    device_ids = jnp.arange(N_SEQ, dtype=jnp.int32)
    clip_local, position = jax.vmap(partial(layout, long_rows=LONG_DEV, short_rows=SHORT_DEV))(clip_lengths, device_ids)
    global_clip = jnp.where(clip_local == SHORTS, CAPS, device_ids[:, None] * SHORTS + clip_local)
    token_mod = jnp.take(modulation, global_clip, axis=0)
    scale_attn, gate_attn, scale_ffn, gate_ffn = jnp.split(token_mod, 4, axis=-1)
    hidden = video_tokens.reshape(N_SEQ, TOK_DEV, D)
    normed = low(rms_norm(hidden) * norm_gains[0] * (1.0 + scale_attn))
    projected = jnp.einsum('std,dke->stke', normed, query_key_value, precision=highest)
    queries = low(rotate(head_norm(low_back(projected[:, :, 0]), norm_gains[4]), position))
    keys_all = low(rotate(head_norm(low_back(projected[:, :, 1]), norm_gains[5]), position))
    values_all = low(low_back(projected[:, :, 2])).reshape(N_SEQ, TOK_DEV, H, HD)
    long_queries = queries[:, :LONG_DEV].reshape(LONG, H, HD)
    long_keys = keys_all[:, :LONG_DEV].reshape(LONG, H, HD)
    long_values = values_all[:, :LONG_DEV].reshape(LONG, H, HD)
    block_rows = math.gcd(LONG, 512)
    full_view = jnp.ones((block_rows, LONG), dtype=bool)

    def long_step(query_block):
        return jax.checkpoint(attend)(query_block, long_keys, long_values, full_view)
    long_out = lax.map(long_step, long_queries.reshape(LONG // block_rows, block_rows, H, HD))
    long_out = long_out.reshape(N_SEQ, LONG_DEV, H, HD)

    def short_step(pieces):
        query_part, key_part, value_part, clip_part = pieces
        visible = clip_part[:, None] == clip_part[None, :]
        return jax.checkpoint(attend)(query_part, key_part, value_part, visible)
    short_out = lax.map(short_step, (queries[:, LONG_DEV:], keys_all[:, LONG_DEV:], values_all[:, LONG_DEV:], clip_local[:, LONG_DEV:]))
    null_rows = null_mask[:CAPS, None, None] == 1
    short_feats = jnp.where(null_rows, null_embed[None], captions)
    long_feats = jnp.where(null_mask[CAPS] == 1, null_embed, long_caption)
    all_feats = jnp.concatenate([short_feats.reshape(CAPS * TXT_LEN, TD), long_feats], axis=0)
    text_proj = jnp.einsum('rt,tke->rke', all_feats, text_weight, precision=highest)
    text_keys = low(head_norm(low_back(text_proj[:, 0]), norm_gains[6]))
    text_values = low(low_back(text_proj[:, 1])).reshape(-1, H, HD)
    text_rows = (SHORTS + 1) * TXT_LEN
    key_clip = jnp.arange(text_rows, dtype=jnp.int32) // TXT_LEN
    key_place = jnp.arange(text_rows, dtype=jnp.int32) % TXT_LEN

    def cross_step(pieces):
        query_part, clip_part, device_id = pieces
        first_row = (device_id * (SHORTS * TXT_LEN)).astype(jnp.int32)
        key_part = jnp.concatenate([lax.dynamic_slice_in_dim(text_keys, first_row, SHORTS * TXT_LEN, 0), text_keys[CAPS * TXT_LEN:]], axis=0)
        value_part = jnp.concatenate([lax.dynamic_slice_in_dim(text_values, first_row, SHORTS * TXT_LEN, 0), text_values[CAPS * TXT_LEN:]], axis=0)
        limits = jnp.concatenate([lax.dynamic_slice_in_dim(text_lengths, (device_id * SHORTS).astype(jnp.int32), SHORTS, 0), text_lengths[CAPS:]])
        key_limit = jnp.take(limits, key_clip)
        visible = (clip_part[:, None] == key_clip[None, :]) & (key_place < key_limit)[None, :]
        return jax.checkpoint(attend)(query_part, key_part, value_part, visible)
    cross_out = lax.map(cross_step, (queries, clip_local, device_ids))
    attended = jnp.concatenate([long_out, short_out], axis=1)
    gate_tanh = jnp.tanh(head_gates)[:, None]
    combined = low(low_back(attended) + gate_tanh * low_back(cross_out)).reshape(N_SEQ, TOK_DEV, D)
    attn_out = low_back(jnp.einsum('std,ed->ste', combined, out_weight, precision=highest))
    residual = hidden + jnp.tanh(gate_attn) * rms_norm(attn_out) * norm_gains[1]
    ffn_in = low(rms_norm(residual) * norm_gains[2] * (1.0 + scale_ffn))
    gate_value = low_back(jnp.einsum('std,df->stf', ffn_in, gate_weight, precision=highest))
    up_value = low_back(jnp.einsum('std,df->stf', ffn_in, up_weight, precision=highest))
    inner = low(jax.nn.silu(gate_value) * up_value)
    ffn_out = low_back(jnp.einsum('stf,ef->ste', inner, down_weight, precision=highest))
    result = residual + jnp.tanh(gate_ffn) * rms_norm(ffn_out) * norm_gains[3]
    return result.reshape(TOKENS, D)

def reference(video_tokens, cotangent, condition, captions, long_caption, null_embed, query_key_value, out_weight, gate_weight, up_weight, down_weight, text_weight, ada_weight, ada_bias, norm_gains, head_gates, clip_lengths, null_mask, text_lengths):
    forward = partial(block_forward, captions=captions.astype(jnp.float32), long_caption=long_caption.astype(jnp.float32), clip_lengths=clip_lengths, null_mask=null_mask, text_lengths=text_lengths)
    result, pullback = jax.vjp(forward, video_tokens.astype(jnp.float32), condition.astype(jnp.float32), null_embed.astype(jnp.float32), query_key_value.astype(jnp.float32), out_weight.astype(jnp.float32), gate_weight.astype(jnp.float32), up_weight.astype(jnp.float32), down_weight.astype(jnp.float32), text_weight.astype(jnp.float32), ada_weight.astype(jnp.float32), ada_bias.astype(jnp.float32), norm_gains.astype(jnp.float32), head_gates.astype(jnp.float32))
    grads = pullback(cotangent.astype(jnp.float32))
    return (result.astype(jnp.bfloat16), grads[0], grads[1], grads[3], grads[4], grads[5], grads[6], grads[7], grads[8], grads[9], grads[10], grads[2], grads[11], grads[12])
```

```python
import functools
import math

import jax
import jax.numpy as jnp
from jax import lax
from jax.experimental import pallas as pl
from jax.experimental.pallas import tpu as pltpu
from jax.sharding import PartitionSpec as P

H = 24
HD = 64
TXT_LEN = 64
LONG_DEV = 64

epsilon = 1e-05
negative = -1e30
highest = lax.Precision.HIGHEST
bf16 = jnp.bfloat16
f32 = jnp.float32


def layout(lengths_row, seq_index, long_rows, short_rows):
    clip_count = lengths_row.shape[0]
    clip_ends = jnp.cumsum(lengths_row)
    clip_starts = clip_ends - lengths_row
    row_ids = jnp.arange(short_rows, dtype=jnp.int32)
    local_clip = jnp.sum(
        (row_ids[:, None] >= clip_ends[None, : clip_count - 1]).astype(jnp.int32), axis=1
    )
    chosen = local_clip[:, None] == jnp.arange(clip_count, dtype=jnp.int32)[None, :]
    clip_begin = jnp.sum(jnp.where(chosen, clip_starts[None, :], 0), axis=1)
    clip_local = jnp.concatenate([jnp.full((long_rows,), clip_count, jnp.int32), local_clip])
    long_place = seq_index * long_rows + jnp.arange(long_rows, dtype=jnp.int32)
    position = jnp.concatenate([long_place, row_ids - clip_begin])
    return (clip_local, position)


def rms_parts(values):
    inverse = lax.rsqrt(jnp.mean(values * values, axis=-1, keepdims=True) + epsilon)
    return (values * inverse, inverse)


def rms_back(grad_hat, normed, inverse):
    return inverse * (grad_hat - normed * jnp.mean(grad_hat * normed, axis=-1, keepdims=True))


def dot(left_side, right_side):
    return jnp.dot(left_side, right_side, preferred_element_type=f32)


def dot_pieces(left_side, pieces):
    depth = pieces[0].shape[0]
    total = 0.0
    for place, piece in enumerate(pieces):
        total = total + dot(left_side[:, place * depth : (place + 1) * depth], piece)
    return total


def contract_rows(left_side, right_side):
    return lax.dot_general(
        left_side, right_side, (((0,), (0,)), ((), ())), preferred_element_type=f32
    )


def contract_cols(left_side, right_side):
    return lax.dot_general(
        left_side, right_side, (((1,), (1,)), ((), ())), preferred_element_type=f32
    )


def swap_txt(values):
    return lax.ppermute(values, "txt", [(0, 1), (1, 0)])


def rounded(values):
    return lax.reduce_precision(values, exponent_bits=8, mantissa_bits=7)


def fence(*values):
    return lax.optimization_barrier(values)


class Grid:
    def __init__(self):
        self.count = lax.axis_size("seq")
        self.outer_count = 4
        self.inner_count = self.count // 8
        self.index = lax.axis_index("seq")
        self.core = self.index % 2
        self.inner = (self.index // 2) % self.inner_count
        self.outer = self.index // (2 * self.inner_count)

    def send(self, values, outer=0, inner=0, core=0):
        pairs = []
        for index in range(self.count):
            to_core = (index + core) % 2
            to_inner = (index // 2 + inner) % self.inner_count
            to_outer = (index // (2 * self.inner_count) + outer) % self.outer_count
            pairs.append((index, (to_outer * self.inner_count + to_inner) * 2 + to_core))
        return lax.ppermute(values, "seq", pairs)

    def lines(self):
        step = 2 * self.inner_count
        return [[first + step * k for k in range(self.outer_count)] for first in range(step)]

    def owners(self):
        place = jnp.arange(self.count, dtype=jnp.int32)
        outer = place % self.outer_count
        inner = (self.inner - (place // self.outer_count) % self.inner_count) % self.inner_count
        core = (self.core + place // (self.outer_count * self.inner_count)) % 2
        return (outer * self.inner_count + inner) * 2 + core


def gather_outer(grid, block):
    return lax.all_gather(block, "seq", axis=0, tiled=True, axis_index_groups=grid.lines())


def send_inner(grid, near):
    return [grid.send(near, inner=step) for step in range(1, grid.inner_count)]


def send_core(grid, pieces):
    return [grid.send(piece, core=1) for piece in pieces]


def stack(pieces):
    return jnp.concatenate(pieces, axis=0) if len(pieces) > 1 else pieces[0]


def add_blocks(*refs):
    *sources, target = refs
    total = sources[0][...].astype(f32)
    for source in sources[1:]:
        total = total + source[...].astype(f32)
    target[...] = total.astype(target.dtype)


def add_rows(arrays, starts, rows):
    cols = arrays[0].shape[1]
    block = 256 if rows % 256 == 0 else 128 if rows % 128 == 0 else rows

    def from_row(start):
        return pl.BlockSpec((block, cols), lambda i: (start // block + i, 0))

    return pl.pallas_call(
        add_blocks,
        grid=(rows // block,),
        in_specs=[from_row(start) for start in starts],
        out_specs=from_row(0),
        out_shape=jax.ShapeDtypeStruct((rows, cols), bf16),
        cost_estimate=pl.CostEstimate(flops=1, bytes_accessed=1, transcendentals=0),
        compiler_params=pltpu.CompilerParams(vmem_limit_bytes=48 * 1024 * 1024),
        name="add_rows",
    )(*arrays)


def core_away(grid, kept, moved):
    rows = kept.shape[0] // grid.inner_count
    return [
        add_rows([kept, moved], [step * rows] * 2, rows) for step in range(1, grid.inner_count)
    ]


def inner_total(grid, kept, moved, arrived):
    rows = kept.shape[0] // grid.inner_count
    return add_rows([kept, moved] + arrived, [0] * (2 + len(arrived)), rows)


def swap_inner(grid, away):
    return [grid.send(part, inner=-step) for step, part in enumerate(away, 1)]


def sum_outer(grid, total):
    return lax.psum_scatter(
        total, "seq", scatter_dimension=0, tiled=True, axis_index_groups=grid.lines()
    )


def pair_sum(grid, values, bit):
    pairs = [(index, index ^ bit) for index in range(grid.count)]
    return lax.ppermute(values, "seq", pairs)


def turn_stage(values, axis, size, own, send):
    moved = [lax.dynamic_index_in_dim(values, own, axis, keepdims=False)]
    for step in range(1, size):
        piece = lax.dynamic_index_in_dim(values, (own + step) % size, axis, keepdims=False)
        moved.append(send(piece, step))
    stacked = jnp.stack(moved, axis=axis)
    order = (own - jnp.arange(size, dtype=jnp.int32)) % size
    return jnp.take(stacked, order, axis=axis)


def turn_seq(grid, values):
    rest = values.shape[1:]
    values = values.reshape((grid.outer_count, grid.inner_count, 2) + rest)
    values = turn_stage(
        values, 0, grid.outer_count, grid.outer, lambda v, k: grid.send(v, outer=k)
    )
    values = turn_stage(
        values, 1, grid.inner_count, grid.inner, lambda v, k: grid.send(v, inner=k)
    )
    values = turn_stage(values, 2, 2, grid.core, lambda v, k: grid.send(v, core=k))
    return values.reshape((grid.count,) + rest)


def sum_seq(grid, values, bit):
    while bit < grid.count:
        values = values + pair_sum(grid, values, bit)
        bit *= 2
    return values


def copy_blocks(to_order, count, order_ref, source_ref, target_ref):
    width = source_ref.shape[1] // count
    for block in range(count):
        moved = pl.ds(pl.multiple_of(order_ref[block] * width, width), width)
        plain = pl.ds(block * width, width)
        if to_order:
            target_ref[:, plain] = source_ref[:, moved]
        else:
            target_ref[:, moved] = source_ref[:, plain]


def reorder_columns(values, order, to_order):
    rows, cols = values.shape
    count = order.shape[0]
    width = cols // count
    if width % 128:
        taken = order if to_order else jnp.argsort(order)
        return jnp.take(values.reshape(rows, count, width), taken, axis=1).reshape(rows, cols)
    return pl.pallas_call(
        functools.partial(copy_blocks, to_order, count),
        out_shape=jax.ShapeDtypeStruct(values.shape, values.dtype),
        in_specs=[
            pl.BlockSpec(memory_space=pltpu.SMEM),
            pl.BlockSpec(memory_space=pltpu.VMEM),
        ],
        out_specs=pl.BlockSpec(memory_space=pltpu.VMEM),
        name="reorder_columns",
    )(order, values)


def split_three(values):
    high = rounded(values)
    rest = values - high
    middle = rounded(rest)
    return high.astype(bf16), middle.astype(bf16), (rest - middle).astype(bf16)


def exact_dot(values, one_hot):
    rows = values.shape[0]
    parts = dot(jnp.concatenate(split_three(values), axis=0), one_hot)
    return parts[:rows] + parts[rows : 2 * rows] + parts[2 * rows :]


def choose(clip, rows):
    chosen = rows[-1:]
    for index in range(rows.shape[0] - 1):
        chosen = jnp.where(clip == index, rows[index : index + 1], chosen)
    return chosen


def add_clip_sums(clip, values, sums_ref):
    @pl.when(pl.program_id(0) == 0)
    def _():
        sums_ref[...] = jnp.zeros_like(sums_ref)

    for index in range(sums_ref.shape[0]):
        part = jnp.sum(jnp.where(clip == index, values, 0.0), axis=0, keepdims=True)
        sums_ref[index : index + 1, :] += part


def add_pair(own_ref, moved_ref):
    return own_ref[...].astype(f32) + moved_ref[...].astype(f32)


def enter_rows(clip_ref, hidden_ref, part_ref, moved_ref, tanh_ref, scale_ref, gains_ref, res_ref, in_ref):
    clip = clip_ref[...]
    attn_hat, _ = rms_parts(add_pair(part_ref, moved_ref))
    tanh_tok = choose(clip, tanh_ref[...])
    residual = hidden_ref[...].astype(f32) + tanh_tok * attn_hat * gains_ref[1:2]
    res_hat, _ = rms_parts(residual)
    res_ref[...] = residual
    in_ref[...] = (res_hat * gains_ref[2:3] * choose(clip, scale_ref[...])).astype(bf16)


def leave_rows(clip_ref, res_ref, part_ref, moved_ref, up_ref, tanh_ref, gains_ref, out_ref, grad_ref, sums_ref):
    clip = clip_ref[...]
    hat, inverse = rms_parts(add_pair(part_ref, moved_ref))
    upstream = up_ref[...].astype(f32)
    tanh_tok = choose(clip, tanh_ref[...])
    out_ref[...] = (res_ref[...] + tanh_tok * hat * gains_ref[3:4]).astype(bf16)
    grad_ref[...] = rms_back(upstream * tanh_tok * gains_ref[3:4], hat, inverse).astype(bf16)
    add_clip_sums(clip, upstream * hat, sums_ref)


def middle_rows(
    clip_ref, res_ref, grad_part_ref, grad_moved_ref, up_ref, part_ref, moved_ref, tanh_ref,
    scale_ref, gains_ref, grad_res_ref, grad_attn_ref, res_sums_ref, attn_sums_ref,
):
    clip = clip_ref[...]
    grad = add_pair(grad_part_ref, grad_moved_ref)
    hat, inverse = rms_parts(res_ref[...])
    add_clip_sums(clip, grad * hat, res_sums_ref)
    grad_hat = grad * gains_ref[2:3] * choose(clip, scale_ref[...])
    grad_res = up_ref[...].astype(f32) + rms_back(grad_hat, hat, inverse)
    grad_res_ref[...] = grad_res
    hat, inverse = rms_parts(add_pair(part_ref, moved_ref))
    add_clip_sums(clip, grad_res * hat, attn_sums_ref)
    grad_hat = grad_res * gains_ref[1:2] * choose(clip, tanh_ref[...])
    grad_attn_ref[...] = rms_back(grad_hat, hat, inverse).astype(bf16)


def last_rows(
    clip_ref, hidden_ref, part_ref, moved_ref, grad_res_ref, scale_ref, gains_ref, high_ref, low_ref,
    sums_ref,
):
    clip = clip_ref[...]
    grad = add_pair(part_ref, moved_ref)
    hat, inverse = rms_parts(hidden_ref[...].astype(f32))
    add_clip_sums(clip, grad * hat, sums_ref)
    grad_hat = grad * gains_ref[0:1] * choose(clip, scale_ref[...])
    total = grad_res_ref[...] + rms_back(grad_hat, hat, inverse)
    high = total.astype(bf16)
    high_ref[...] = high
    low_ref[...] = (total - high.astype(f32)).astype(bf16)


def row_call(body, name, arrays, tables, outs, sums):
    count, width = arrays[1].shape
    rows = count // 4

    def by_rows(array):
        return pl.BlockSpec((rows, array.shape[1]), lambda i: (i, 0))

    def whole(array):
        return pl.BlockSpec(array.shape, lambda i: (0, 0))

    out_shapes = [jax.ShapeDtypeStruct((count, width), kind) for kind in outs]
    sum_shapes = [jax.ShapeDtypeStruct((tables[0].shape[0], width), f32)] * sums
    return pl.pallas_call(
        body,
        grid=(4,),
        in_specs=[by_rows(array) for array in arrays] + [whole(table) for table in tables],
        out_specs=[by_rows(shape) for shape in out_shapes] + [whole(shape) for shape in sum_shapes],
        out_shape=out_shapes + sum_shapes,
        cost_estimate=pl.CostEstimate(flops=1, bytes_accessed=1, transcendentals=0),
        compiler_params=pltpu.CompilerParams(vmem_limit_bytes=48 * 1024 * 1024),
        name=name,
    )(*arrays, *tables)


def head_means(values):
    first = lax.broadcasted_iota(jnp.int32, values.shape, 1) < HD
    front = jnp.sum(jnp.where(first, values, 0.0), axis=1, keepdims=True)
    back = jnp.sum(jnp.where(first, 0.0, values), axis=1, keepdims=True)
    return jnp.where(first, front, back) * (1.0 / HD)


def turn_lanes(values, cosine, sine):
    lane = lax.broadcasted_iota(jnp.int32, values.shape, 1) % HD
    ahead = pltpu.roll(values, 2 * HD - HD // 2, 1)
    behind = pltpu.roll(values, HD // 2, 1)
    return values * cosine + jnp.where(lane < HD // 2, -ahead, behind) * sine


def norm_heads(values_ref, gain_ref, cos_ref, sin_ref, out_ref):
    cosine, sine = cos_ref[...], sin_ref[...]
    for start in range(0, out_ref.shape[1], 2 * HD):
        part = slice(start, start + 2 * HD)
        values = values_ref[:, part]
        hat = values * lax.rsqrt(head_means(values * values) + epsilon)
        out_ref[:, part] = turn_lanes(hat * gain_ref[:, part], cosine, sine).astype(bf16)


def norm_heads_back(*refs):
    values_ref, gain_ref, cos_ref, sin_ref, *grad_refs, out_ref, sums_ref = refs
    cosine, sine = cos_ref[...], sin_ref[...]

    @pl.when(pl.program_id(0) == 0)
    def _():
        sums_ref[...] = jnp.zeros_like(sums_ref)

    for start in range(0, out_ref.shape[1], 2 * HD):
        part = slice(start, start + 2 * HD)
        values = values_ref[:, part]
        inverse = lax.rsqrt(head_means(values * values) + epsilon)
        hat = values * inverse
        grad = grad_refs[0][:, part]
        for grad_ref in grad_refs[1:]:
            grad = grad + grad_ref[:, part]
        grad = turn_lanes(grad, cosine, -sine)
        sums_ref[:, part] += jnp.sum(grad * hat, axis=0, keepdims=True)
        grad = grad * gain_ref[:, part]
        out_ref[:, part] = (inverse * (grad - hat * head_means(grad * hat))).astype(bf16)


def head_call(body, name, values, column, gain, turns, grads=()):
    count, width = turns[0].shape[0], gain.shape[1]
    rows = count // 4
    by_rows = pl.BlockSpec((rows, width), lambda i: (i, 0))
    whole = pl.BlockSpec((1, width), lambda i: (0, 0))
    turn = pl.BlockSpec((rows, 2 * HD), lambda i: (i, 0))
    out_shape = [jax.ShapeDtypeStruct((count, width), bf16)]
    out_specs = [by_rows]
    if grads:
        out_shape.append(jax.ShapeDtypeStruct((1, width), f32))
        out_specs.append(whole)
    results = pl.pallas_call(
        body,
        grid=(4,),
        in_specs=[pl.BlockSpec((rows, width), lambda i: (i, column)), whole, turn, turn]
        + [by_rows] * len(grads),
        out_specs=out_specs,
        out_shape=out_shape,
        cost_estimate=pl.CostEstimate(flops=1, bytes_accessed=1, transcendentals=0),
        compiler_params=pltpu.CompilerParams(vmem_limit_bytes=48 * 1024 * 1024),
        name=name,
    )(values, gain, *turns, *grads)
    return results if grads else results[0]


def attend_heads(clip_ref, key_clip_ref, query_ref, key_ref, value_ref, out_ref, total_ref):
    visible = clip_ref[...] == key_clip_ref[...]
    for start in range(0, 2 * HD, HD):
        head = slice(start, start + HD)
        scores = contract_cols(query_ref[:, head], key_ref[:, head]) * HD ** (-0.5)
        scores = jnp.where(visible, scores, negative)
        peak = jnp.max(scores, axis=1, keepdims=True)
        exponent = jnp.exp(scores - peak)
        total = jnp.sum(exponent, axis=1, keepdims=True)
        out_ref[:, head] = dot((exponent / total).astype(bf16), value_ref[:, head])
        total_ref[:, head] = jnp.broadcast_to(peak + jnp.log(total), (total_ref.shape[0], HD))


def attend_heads_back(
    clip_ref, key_clip_ref, query_ref, key_ref, value_ref, grad_ref, out_ref, total_ref,
    grad_query_ref, grad_key_ref, grad_value_ref,
):
    visible = clip_ref[...] == key_clip_ref[...]
    for start in range(0, 2 * HD, HD):
        head = slice(start, start + HD)
        query, key = query_ref[:, head], key_ref[:, head]
        grad = grad_ref[:, head]
        scores = contract_cols(query, key) * HD ** (-0.5)
        weights = jnp.where(visible, jnp.exp(scores - total_ref[:, start : start + 1]), 0.0)
        delta = jnp.sum(grad.astype(f32) * out_ref[:, head], axis=1, keepdims=True)
        grad_scores = weights * (contract_cols(grad, value_ref[:, head]) - delta)
        grad_scores = grad_scores.astype(bf16)
        grad_query_ref[:, head] = dot(grad_scores, key) * HD ** (-0.5)
        grad_key = contract_rows(grad_scores, query) * HD ** (-0.5)
        grad_key_ref[:, head] = grad_key.astype(grad_key_ref.dtype)
        grad_value = contract_rows(weights.astype(bf16), grad)
        grad_value_ref[:, head] = grad_value.astype(grad_value_ref.dtype)


def attend_call(name, clips, key_clips, query, key, value, value_column=0, back=(), kind=f32):
    count, keys, width = query.shape[0], key.shape[0], query.shape[1]
    first = value_column // (2 * HD)
    queries = pl.BlockSpec((count, 2 * HD), lambda i: (0, i))
    seen = pl.BlockSpec((keys, 2 * HD), lambda i: (0, i))
    whole = [pl.BlockSpec(array.shape, lambda i: (0, 0)) for array in (clips, key_clips)]
    out_shape = [jax.ShapeDtypeStruct((count, width), f32)]
    if back:
        out_shape += [jax.ShapeDtypeStruct((keys, width), kind)] * 2
        out_specs = [queries, seen, seen]
    else:
        out_shape += out_shape
        out_specs = [queries, queries]
    return pl.pallas_call(
        attend_heads_back if back else attend_heads,
        grid=(width // (2 * HD),),
        in_specs=whole
        + [queries, seen, pl.BlockSpec((keys, 2 * HD), lambda i: (0, first + i))]
        + [queries] * len(back),
        out_specs=out_specs,
        out_shape=out_shape,
        cost_estimate=pl.CostEstimate(flops=1, bytes_accessed=1, transcendentals=0),
        compiler_params=pltpu.CompilerParams(vmem_limit_bytes=48 * 1024 * 1024),
        name=name,
    )(clips, key_clips, query, key, value, *back)


def local(
    video_tokens,
    cotangent,
    condition,
    captions,
    long_caption,
    null_embed,
    query_key_value,
    out_weight,
    gate_weight,
    up_weight,
    down_weight,
    text_weight,
    ada_weight,
    ada_bias,
    norm_gains,
    head_gates,
    clip_lengths,
    null_mask,
    text_lengths,
):
    grid = Grid()
    seq_index = grid.index
    seq_count = grid.count
    txt_index = lax.axis_index("txt")
    first_half = txt_index == 0
    token_count, model_width = video_tokens.shape
    depth = query_key_value.shape[0]
    text_depth, text_width = text_weight.shape[0], captions.shape[2]
    half_width = model_width // 2
    own_heads = query_key_value.shape[2] // HD
    own_width = own_heads * HD
    head_start = txt_index * own_heads
    clip_total = condition.shape[0]
    short_clips = clip_lengths.shape[1]
    clip_local, position = layout(clip_lengths[0], seq_index, LONG_DEV, token_count - LONG_DEV)
    owners = grid.owners()
    text_rows = (short_clips + 1) * TXT_LEN

    half_text = text_width // 2
    text_block = text_weight.reshape(text_depth, 2 * own_width)

    qkv_block, condition = fence(query_key_value.reshape(depth, 3 * own_width), condition)
    qkv_near = gather_outer(grid, qkv_block)
    shifted = jax.nn.silu(condition.astype(f32)).astype(bf16)
    mod_part = dot(shifted, ada_weight) + ada_bias
    short_part = mod_part[: clip_total - 1].reshape(seq_count, short_clips, mod_part.shape[1])
    long_part = jnp.broadcast_to(
        mod_part[clip_total - 1 :][None], (seq_count, 1, mod_part.shape[1])
    )
    own_part = turn_seq(grid, jnp.concatenate([short_part, long_part], axis=1))
    other_part = swap_txt(own_part)
    own_null = lax.dynamic_slice_in_dim(null_mask, seq_index * short_clips, short_clips, 0) == 1
    short_feats = jnp.where(own_null[:, None, None], null_embed[None], captions)
    long_feats = jnp.where(null_mask[clip_total - 1] == 1, null_embed, long_caption)
    own_feats = jnp.concatenate([short_feats, long_feats[None]], axis=0).reshape(-1, text_width)
    own_feats = reorder_columns(own_feats, owners, True)

    columns = jnp.arange(model_width, dtype=jnp.int32)
    column_order = jnp.repeat(owners, depth) * depth + columns % depth
    one_hot = (columns[:, None] == column_order[None, :]).astype(bf16)
    hidden = dot(video_tokens, one_hot).astype(bf16)
    hidden_hat, _ = rms_parts(hidden.astype(f32))
    clip_column = clip_local[:, None]
    tkey_block, tval_block = text_block[:, :own_width], text_block[:, own_width:]
    qkv_near, own_part, other_part, own_feats, tkey_block, tval_block, out_weight = fence(
        qkv_near, own_part, other_part, own_feats, tkey_block, tval_block, out_weight
    )

    qkv_y = send_inner(grid, qkv_near)
    qkv_near_core = send_core(grid, [qkv_near])
    tkey_near = gather_outer(grid, tkey_block)
    out_near = gather_outer(grid, out_weight)
    other_feats = swap_txt(own_feats)
    own_mod = jnp.stack(
        [jnp.where(first_half, own_part, other_part), jnp.where(first_half, other_part, own_part)],
        axis=1,
    )
    own_mod = jnp.transpose(own_mod, (2, 0, 1, 3)).reshape((short_clips + 1) * 4, model_width)
    rows = exact_dot(jnp.concatenate([own_mod, norm_gains[:4]], axis=0), one_hot)
    gains = rows[-4:]
    own_mod = rows[:-4].reshape(short_clips + 1, 4, model_width)
    own_scales = 1.0 + own_mod[:, 0], 1.0 + own_mod[:, 2]
    own_tanhs = jnp.tanh(own_mod[:, 1]), jnp.tanh(own_mod[:, 3])
    selector = clip_local[:, None] == jnp.arange(short_clips + 1, dtype=jnp.int32)[None, :]

    def per_token(rows):
        chosen = rows[short_clips:]
        for clip in range(short_clips):
            chosen = jnp.where(selector[:, clip : clip + 1], rows[clip : clip + 1], chosen)
        return chosen

    normed_in = (hidden_hat * gains[0] * per_token(own_scales[0])).astype(bf16)
    query_gain, key_gain, text_gain = [
        lax.dynamic_slice(norm_gains, (row, head_start * HD), (1, own_width)) for row in (4, 5, 6)
    ]
    frequency = jnp.exp(
        jnp.arange(HD // 2, dtype=f32) * (-math.log(10000.0) / (HD // 2))
    )
    angles = jnp.tile(position.astype(f32)[:, None] * frequency, (1, 4))
    turns = jnp.cos(angles), jnp.sin(angles)
    text_turns = jnp.ones((text_rows, 2 * HD), f32), jnp.zeros((text_rows, 2 * HD), f32)
    normed_in, other_feats, tkey_near, out_near, tval_block, qkv_near_core, qkv_y = fence(
        normed_in, other_feats, tkey_near, out_near, tval_block, qkv_near_core, qkv_y
    )

    tkey_y = send_inner(grid, tkey_near)
    tkey_near_core = send_core(grid, [tkey_near])
    out_near_core = send_core(grid, [out_near])
    tval_near = gather_outer(grid, tval_block)
    qkv_core, normed_in = fence(send_core(grid, qkv_y), normed_in)
    qkv_own, qkv_other = stack([qkv_near] + qkv_y), stack(qkv_near_core + qkv_core)
    projected = dot(normed_in[:, :half_width], qkv_own) + dot(normed_in[:, half_width:], qkv_other)
    query_bf = head_call(norm_heads, "norm_queries", projected, 0, query_gain, turns)
    key_bf = head_call(norm_heads, "norm_keys", projected, 1, key_gain, turns)
    value_bf = projected[:, 2 * own_width :].astype(bf16)
    long_block = jnp.concatenate([key_bf[:LONG_DEV], value_bf[:LONG_DEV]], axis=1)
    (
        query_bf, key_bf, value_bf, long_block, tkey_y, tkey_near_core, out_near, out_near_core,
        tval_near, gate_weight,
    ) = fence(
        query_bf, key_bf, value_bf, long_block, tkey_y, tkey_near_core, out_near, out_near_core,
        tval_near, gate_weight,
    )

    tail = long_block.size // gate_weight.shape[1]
    gate_near = gather_outer(
        grid, jnp.concatenate([gate_weight, long_block.reshape(tail, -1)], axis=0)
    )
    tval_y = send_inner(grid, tval_near)
    tval_near_core = send_core(grid, [tval_near])
    short_query = query_bf[LONG_DEV:]
    short_key = key_bf[LONG_DEV:]
    short_value = value_bf[LONG_DEV:]
    short_clip = clip_column[LONG_DEV:]
    short_seen = clip_local[LONG_DEV:][None, :]
    short_out, short_lse = attend_call(
        "attend_short", short_clip, short_seen, short_query, short_key, short_value
    )
    out_y = send_inner(grid, out_near)
    tkey_core = send_core(grid, tkey_y)
    feats = jnp.concatenate(
        [
            jnp.where(first_half, own_feats, other_feats).reshape(-1, TXT_LEN // 2, text_width),
            jnp.where(first_half, other_feats, own_feats).reshape(-1, TXT_LEN // 2, text_width),
        ],
        axis=1,
    ).reshape(text_rows, text_width)
    tval_y, tval_near_core, gate_near, tkey_core, out_y, up_weight, feats, short_out = fence(
        tval_y, tval_near_core, gate_near, tkey_core, out_y, up_weight, feats, short_out
    )

    gate_near = gate_near.reshape(grid.outer_count, depth + tail, -1)
    long_near = gate_near[:, depth:].reshape(-1, 2 * own_width)
    gate_near = gate_near[:, :depth].reshape(grid.outer_count * depth, -1)
    long_y = send_inner(grid, long_near)
    long_near_core = send_core(grid, [long_near])
    gate_y = send_inner(grid, gate_near)
    gate_near_core = send_core(grid, [gate_near])
    up_near = gather_outer(grid, up_weight)
    tval_core = send_core(grid, tval_y)
    long_core = send_core(grid, long_y)
    out_core = send_core(grid, out_y)
    tkey_pieces = [tkey_near] + tkey_y + tkey_near_core + tkey_core
    text_raw = dot_pieces(feats, tkey_pieces)
    text_key_bf = head_call(norm_heads, "norm_text", text_raw, 0, text_gain, text_turns)
    tval_core, out_core, long_core, long_near_core, long_y, text_key_bf, query_bf = fence(
        tval_core, out_core, long_core, long_near_core, long_y, text_key_bf, query_bf
    )

    out_own, out_other = stack([out_near] + out_y), stack(out_near_core + out_core)
    long_pairs = stack([long_near] + long_y + long_near_core + long_core)
    long_count = long_pairs.shape[0]
    long_query = query_bf[:LONG_DEV]
    long_clip = clip_column[:LONG_DEV]
    long_seen = jnp.full((1, long_count), short_clips, jnp.int32)
    long_out, long_lse = attend_call(
        "attend_long", long_clip, long_seen, long_query, long_pairs, long_pairs, own_width
    )
    tval_pieces = [tval_near] + tval_y + tval_near_core + tval_core
    text_value_bf = dot_pieces(feats, tval_pieces).astype(bf16)
    key_clip = jnp.arange(text_rows, dtype=jnp.int32) // TXT_LEN
    key_place = jnp.arange(text_rows, dtype=jnp.int32) % TXT_LEN
    limits = jnp.concatenate(
        [
            lax.dynamic_slice_in_dim(text_lengths, seq_index * short_clips, short_clips, 0),
            text_lengths[clip_total - 1 :],
        ]
    )
    clip_match = key_clip[:, None] == jnp.arange(short_clips + 1, dtype=jnp.int32)[None, :]
    key_limit = jnp.sum(jnp.where(clip_match, limits[None, :], 0), axis=1)
    cross_seen = jnp.where(key_place < key_limit, key_clip, -1)[None, :]
    cross_out, cross_lse = attend_call(
        "attend_cross", clip_column, cross_seen, query_bf, text_key_bf, text_value_bf
    )
    attended = jnp.concatenate([long_out, short_out], axis=0)
    own_gates = lax.dynamic_slice_in_dim(head_gates, head_start, own_heads, 0)
    gate_tanh = jnp.repeat(jnp.tanh(own_gates), HD)[None, :]
    combined_bf = (attended + gate_tanh * cross_out).astype(bf16)
    attn_part = rounded(
        jnp.concatenate(
            [contract_cols(combined_bf, out_own), contract_cols(combined_bf, out_other)], axis=1
        )
    ).astype(bf16)
    attn_part, gate_y, gate_near_core, up_near, down_weight = fence(
        attn_part, gate_y, gate_near_core, up_near, down_weight
    )

    attn_moved = swap_txt(attn_part)
    up_y = send_inner(grid, up_near)
    up_near_core = send_core(grid, [up_near])
    down_near = gather_outer(grid, down_weight)
    gate_core = send_core(grid, gate_y)
    attn_moved, up_y, up_near_core, down_near, gate_core = fence(
        attn_moved, up_y, up_near_core, down_near, gate_core
    )

    down_y = send_inner(grid, down_near)
    down_near_core = send_core(grid, [down_near])
    up_core = send_core(grid, up_y)
    gate_own, gate_other = stack([gate_near] + gate_y), stack(gate_near_core + gate_core)
    residual, ffn_in_bf = row_call(
        enter_rows,
        "enter_rows",
        [clip_column, hidden, attn_part, attn_moved],
        [own_tanhs[0], own_scales[1], gains],
        [f32, bf16],
        0,
    )
    gate_value = dot(ffn_in_bf[:, :half_width], gate_own) + dot(
        ffn_in_bf[:, half_width:], gate_other
    )
    up_core, gate_value = fence(up_core, gate_value)
    up_own, up_other = stack([up_near] + up_y), stack(up_near_core + up_core)
    up_value = dot(ffn_in_bf[:, :half_width], up_own) + dot(ffn_in_bf[:, half_width:], up_other)
    sigmoid_gate = jax.nn.sigmoid(gate_value)
    silu_gate = gate_value * sigmoid_gate
    inner_bf = (silu_gate * up_value).astype(bf16)
    inner_bf, down_y, down_near_core = fence(inner_bf, down_y, down_near_core)

    down_core = send_core(grid, down_y)
    upstream = dot(cotangent, one_hot).astype(bf16)
    down_core, inner_bf, upstream = fence(down_core, inner_bf, upstream)
    down_own, down_other = stack([down_near] + down_y), stack(down_near_core + down_core)
    ffn_part = rounded(
        jnp.concatenate(
            [contract_cols(inner_bf, down_own), contract_cols(inner_bf, down_other)], axis=1
        )
    ).astype(bf16)
    (ffn_part,) = fence(ffn_part)

    ffn_moved = swap_txt(ffn_part)
    ffn_moved, ffn_part = fence(ffn_moved, ffn_part)

    block_out, grad_ffn_out, ffn_sums = row_call(
        leave_rows,
        "leave_rows",
        [clip_column, residual, ffn_part, ffn_moved, upstream],
        [own_tanhs[1], gains],
        [bf16, bf16],
        1,
    )
    down_kept = contract_rows(grad_ffn_out[:, :half_width], inner_bf).astype(bf16)
    down_away = contract_rows(grad_ffn_out[:, half_width:], inner_bf).astype(bf16)
    grad_ffn_out, down_away, down_kept = fence(grad_ffn_out, down_away, down_kept)

    down_core = grid.send(down_away, core=1)
    grad_inner = dot(grad_ffn_out[:, :half_width], down_own) + dot(
        grad_ffn_out[:, half_width:], down_other
    )
    silu_slope = sigmoid_gate * (1.0 + gate_value * (1.0 - sigmoid_gate))
    grad_gate_bf = (grad_inner * up_value * silu_slope).astype(bf16)
    grad_up_bf = (grad_inner * silu_gate).astype(bf16)
    ffn_in_part = rounded(
        jnp.concatenate(
            [
                contract_cols(grad_gate_bf, gate_own) + contract_cols(grad_up_bf, up_own),
                contract_cols(grad_gate_bf, gate_other) + contract_cols(grad_up_bf, up_other),
            ],
            axis=1,
        )
    ).astype(bf16)
    gate_kept = contract_rows(ffn_in_bf[:, :half_width], grad_gate_bf).astype(bf16)
    gate_away = contract_rows(ffn_in_bf[:, half_width:], grad_gate_bf).astype(bf16)
    down_away = core_away(grid, down_kept, down_core)
    down_core, down_away, ffn_in_part, gate_kept, gate_away, grad_up_bf = fence(
        down_core, down_away, ffn_in_part, gate_kept, gate_away, grad_up_bf
    )

    ffn_in_moved = swap_txt(ffn_in_part)
    down_moved = swap_inner(grid, down_away)
    gate_core = grid.send(gate_away, core=1)
    up_kept = contract_rows(ffn_in_bf[:, :half_width], grad_up_bf).astype(bf16)
    up_away = contract_rows(ffn_in_bf[:, half_width:], grad_up_bf).astype(bf16)
    block_out = contract_cols(block_out, one_hot).astype(bf16)
    gate_away = core_away(grid, gate_kept, gate_core)
    block_out, ffn_in_moved, down_moved, up_kept = fence(
        block_out, ffn_in_moved, down_moved, up_kept
    )

    down_total = inner_total(grid, down_kept, down_core, down_moved)
    gate_moved = swap_inner(grid, gate_away)
    up_core = grid.send(up_away, core=1)
    ffn_in_moved, down_total = fence(ffn_in_moved, down_total)
    down_sum = sum_outer(grid, down_total)
    grad_residual, grad_attn_bf, res_sums, attn_sums = row_call(
        middle_rows,
        "middle_rows",
        [clip_column, residual, ffn_in_part, ffn_in_moved, upstream, attn_part, attn_moved],
        [own_tanhs[0], own_scales[1], gains],
        [f32, bf16],
        2,
    )
    grad_combined = dot(grad_attn_bf[:, :half_width], out_own) + dot(
        grad_attn_bf[:, half_width:], out_other
    )
    grad_attended_bf = grad_combined.astype(bf16)
    grad_long_bf = grad_attended_bf[:LONG_DEV]
    grad_long_q, *long_parts = attend_call(
        "attend_long_back", long_clip, long_seen, long_query, long_pairs, long_pairs, own_width,
        (grad_long_bf, long_out, long_lse), bf16,
    )
    long_terms = jnp.concatenate(long_parts, axis=1)
    long_kept, long_away = long_terms[: long_count // 2], long_terms[long_count // 2 :]
    out_kept = contract_rows(grad_attn_bf[:, :half_width], combined_bf).astype(bf16)
    out_away = contract_rows(grad_attn_bf[:, half_width:], combined_bf).astype(bf16)
    up_away = core_away(grid, up_kept, up_core)
    (
        grad_combined, grad_attended_bf, gate_moved, up_core, up_away, long_kept, long_away, out_kept,
        out_away, grad_long_q,
    ) = fence(
        grad_combined, grad_attended_bf, gate_moved, up_core, up_away, long_kept, long_away, out_kept,
        out_away, grad_long_q,
    )

    up_moved = swap_inner(grid, up_away)
    long_core = grid.send(long_away, core=1)
    out_core = grid.send(out_away, core=1)
    gate_total = inner_total(grid, gate_kept, gate_core, gate_moved)
    grad_combined, gate_total = fence(grad_combined, gate_total)
    gate_sum = sum_outer(grid, gate_total)
    grad_cross_bf = (gate_tanh * grad_combined).astype(bf16)
    own_gate_grad = jnp.sum(
        jnp.sum(grad_combined * cross_out, axis=0).reshape(own_heads, HD), axis=1
    ) * (1.0 - jnp.tanh(own_gates) ** 2)
    grad_query, grad_text_key, grad_text_value = attend_call(
        "attend_cross_back", clip_column, cross_seen, query_bf, text_key_bf, text_value_bf, 0,
        (grad_cross_bf, cross_out, cross_lse),
    )
    grad_tkey, text_gain_grad = head_call(
        norm_heads_back, "norm_text_back", text_raw, 0, text_gain, text_turns, (grad_text_key,)
    )
    grad_tval = grad_text_value.astype(bf16)
    tkey_kept = contract_rows(feats[:, :half_text], grad_tkey).astype(bf16)
    tkey_away = contract_rows(feats[:, half_text:], grad_tkey).astype(bf16)
    long_away = core_away(grid, long_kept, long_core)
    out_away = core_away(grid, out_kept, out_core)
    (
        gate_sum, down_sum, up_moved, long_core, long_away, out_core, out_away, grad_query, grad_tkey,
        grad_tval, tkey_kept, tkey_away, grad_attended_bf,
    ) = fence(
        gate_sum, down_sum, up_moved, long_core, long_away, out_core, out_away, grad_query, grad_tkey,
        grad_tval, tkey_kept, tkey_away, grad_attended_bf,
    )

    long_moved = swap_inner(grid, long_away)
    out_moved = swap_inner(grid, out_away)
    tkey_core = grid.send(tkey_away, core=1)
    down_grad = down_sum.astype(f32)
    gate_grad = gate_sum.astype(f32)
    up_total = inner_total(grid, up_kept, up_core, up_moved)
    grad_attended_bf, up_total = fence(grad_attended_bf, up_total)
    up_sum = sum_outer(grid, up_total)
    grad_short_bf = grad_attended_bf[LONG_DEV:]
    grad_short_q, grad_short_k, grad_short_v = attend_call(
        "attend_short_back", short_clip, short_seen, short_query, short_key, short_value, 0,
        (grad_short_bf, short_out, short_lse),
    )
    tval_kept = contract_rows(feats[:, :half_text], grad_tval).astype(bf16)
    tval_away = contract_rows(feats[:, half_text:], grad_tval).astype(bf16)
    null_flags = jnp.concatenate([own_null, null_mask[clip_total - 1 :] == 1]).astype(f32)
    row_ids = jnp.arange(text_rows, dtype=jnp.int32)
    null_chosen = jnp.where(
        row_ids[None, :] % TXT_LEN == jnp.arange(TXT_LEN, dtype=jnp.int32)[:, None],
        jnp.repeat(null_flags, TXT_LEN)[None, :],
        0.0,
    ).astype(bf16)
    null_rows = jnp.concatenate(
        [dot(null_chosen, grad_tkey), dot(null_chosen, grad_tval)], axis=1
    ).astype(bf16)
    tkey_away = core_away(grid, tkey_kept, tkey_core)
    (
        up_sum, long_moved, out_moved, tkey_core, tkey_away, tval_kept, tval_away, grad_short_q,
        grad_short_k, grad_short_v, null_rows,
    ) = fence(
        up_sum, long_moved, out_moved, tkey_core, tkey_away, tval_kept, tval_away, grad_short_q,
        grad_short_k, grad_short_v, null_rows,
    )

    tkey_moved = swap_inner(grid, tkey_away)
    tval_core = grid.send(tval_away, core=1)
    null_moved = pair_sum(grid, null_rows, 1)
    up_grad = up_sum.astype(f32)
    long_total = inner_total(grid, long_kept, long_core, long_moved)
    out_total = inner_total(grid, out_kept, out_core, out_moved)
    long_rows = LONG_DEV * 2
    both_total = jnp.concatenate(
        [
            long_total.reshape(grid.outer_count, long_rows, own_width),
            out_total.reshape(grid.outer_count, depth, own_width),
        ],
        axis=1,
    ).reshape(-1, own_width)
    both_sum = sum_outer(grid, both_total)
    grad_query_raw, query_gain_grad = head_call(
        norm_heads_back, "norm_queries_back", projected, 0, query_gain, turns,
        (grad_query, jnp.concatenate([grad_long_q, grad_short_q], axis=0)),
    )
    tval_away = core_away(grid, tval_kept, tval_core)
    (
        both_sum, tkey_moved, tval_core, tval_away, null_moved, grad_query_raw, grad_short_k,
        grad_short_v, query_gain_grad,
    ) = fence(
        both_sum, tkey_moved, tval_core, tval_away, null_moved, grad_query_raw, grad_short_k,
        grad_short_v, query_gain_grad,
    )

    tval_moved = swap_inner(grid, tval_away)
    null_rows = null_rows + null_moved
    null_moved = pair_sum(grid, null_rows, 2)
    out_grad = both_sum[long_rows:].astype(f32)
    tkey_total = inner_total(grid, tkey_kept, tkey_core, tkey_moved)
    both_sum, tkey_total = fence(both_sum, tkey_total)
    tkey_sum = sum_outer(grid, tkey_total)
    own_terms = both_sum[:long_rows].reshape(LONG_DEV, 2 * own_width).astype(f32)
    grad_key = jnp.concatenate([own_terms[:, :own_width], grad_short_k], axis=0)
    grad_value = jnp.concatenate([own_terms[:, own_width:], grad_short_v], axis=0)
    grad_key_raw, key_gain_grad = head_call(
        norm_heads_back, "norm_keys_back", projected, 1, key_gain, turns, (grad_key,)
    )
    grad_proj_bf = jnp.concatenate(
        [grad_query_raw, grad_key_raw, grad_value.astype(bf16)], axis=1
    )
    normed_part = rounded(
        jnp.concatenate(
            [contract_cols(grad_proj_bf, qkv_own), contract_cols(grad_proj_bf, qkv_other)], axis=1
        )
    ).astype(bf16)
    qkv_kept = contract_rows(normed_in[:, :half_width], grad_proj_bf).astype(bf16)
    qkv_away = contract_rows(normed_in[:, half_width:], grad_proj_bf).astype(bf16)
    first_rows = token_count // 2
    moved_first = swap_txt(normed_part[:first_rows])
    moved_last = swap_txt(normed_part[first_rows:])
    qkv_core = grid.send(qkv_away, core=1)
    qkv_away = core_away(grid, qkv_kept, qkv_core)
    (
        tkey_sum, tval_moved, null_moved, moved_first, qkv_kept, qkv_core, qkv_away, grad_residual,
    ) = fence(
        tkey_sum, tval_moved, null_moved, moved_first, qkv_kept, qkv_core, qkv_away, grad_residual,
    )

    qkv_moved = swap_inner(grid, qkv_away)
    null_rows = null_rows + null_moved
    tval_total = inner_total(grid, tval_kept, tval_core, tval_moved)
    tval_total, null_rows, moved_first, grad_residual = fence(
        tval_total, null_rows, moved_first, grad_residual
    )
    tval_sum = sum_outer(grid, tval_total)
    null_rows = null_rows + pair_sum(grid, null_rows, 4)
    null_moved = pair_sum(grid, null_rows, 8)
    normed_moved = jnp.concatenate([moved_first, moved_last], axis=0)
    video_high, video_low, hidden_sums = row_call(
        last_rows,
        "last_rows",
        [clip_column, hidden, normed_part, normed_moved, grad_residual],
        [own_scales[0], gains],
        [bf16, bf16],
        1,
    )
    hidden_sums, tval_sum, qkv_moved, null_rows, null_moved = fence(
        hidden_sums, tval_sum, qkv_moved, null_rows, null_moved
    )

    text_grad = jnp.stack([tkey_sum.astype(f32), tval_sum.astype(f32)], axis=1)
    qkv_total = inner_total(grid, qkv_kept, qkv_core, qkv_moved)
    hidden_sums, qkv_total = fence(hidden_sums, qkv_total)
    qkv_sum = sum_outer(grid, qkv_total)

    grad_mod = jnp.stack(
        [
            hidden_sums * gains[0],
            attn_sums * gains[1] * (1.0 - own_tanhs[0] * own_tanhs[0]),
            res_sums * gains[2],
            ffn_sums * gains[3] * (1.0 - own_tanhs[1] * own_tanhs[1]),
        ],
        axis=1,
    ).reshape(-1, model_width)
    gain_rows = jnp.stack(
        [
            jnp.sum(hidden_sums * own_scales[0], axis=0),
            jnp.sum(attn_sums * own_tanhs[0], axis=0),
            jnp.sum(res_sums * own_scales[1], axis=0),
            jnp.sum(ffn_sums * own_tanhs[1], axis=0),
        ],
        axis=0,
    )
    rows = contract_cols(
        jnp.concatenate(split_three(jnp.concatenate([grad_mod, gain_rows], axis=0)), axis=0),
        one_hot,
    )
    row_count = rows.shape[0] // 3
    rows = rows[:row_count] + rows[row_count : 2 * row_count] + rows[2 * row_count :]
    gain_rows = rows[-4:]
    own_grad_mod = rows[:-4].reshape(short_clips + 1, 4 * model_width)
    column_count = mod_part.shape[1]
    mod_blocks = lax.dynamic_index_in_dim(
        own_grad_mod.reshape(short_clips + 1, seq_count, 2, column_count),
        txt_index,
        2,
        keepdims=False,
    )
    mod_blocks = turn_seq(grid, jnp.transpose(mod_blocks, (1, 0, 2)))
    null_rows = sum_seq(grid, null_rows + null_moved, 16)
    null_part = jnp.concatenate(
        [
            contract_cols(null_rows[:, :own_width], key_piece)
            + contract_cols(null_rows[:, own_width:], value_piece)
            for key_piece, value_piece in zip(tkey_pieces, tval_pieces)
        ],
        axis=1,
    )
    null_part = rounded(null_part).astype(bf16)
    null_moved = swap_txt(null_part)
    video_grad = contract_cols(video_high, one_hot) + contract_cols(video_low, one_hot)
    slice_grad_mod = jnp.concatenate(
        [
            mod_blocks[:, :short_clips].reshape(clip_total - 1, column_count),
            jnp.sum(mod_blocks[:, short_clips], axis=0, keepdims=True),
        ],
        axis=0,
    )
    ada_weight_grad = lax.dot_general(
        shifted.astype(f32), slice_grad_mod, (((0,), (0,)), ((), ())), precision=highest
    )
    ada_bias_grad = jnp.sum(slice_grad_mod, axis=0)
    grad_shifted = lax.dot_general(
        slice_grad_mod, ada_weight.astype(f32), (((1,), (1,)), ((), ())), precision=highest
    )
    cond_value = condition.astype(f32)
    cond_sigmoid = jax.nn.sigmoid(cond_value)
    cond_part = grad_shifted * cond_sigmoid * (1.0 + cond_value * (1.0 - cond_sigmoid))

    head_rows = [
        lax.dynamic_update_slice(jnp.zeros((1, model_width), f32), rows, (0, head_start * HD))
        for rows in (query_gain_grad, key_gain_grad, text_gain_grad)
    ]
    gains_term = jnp.concatenate([jnp.where(first_half, gain_rows, 0.0)] + head_rows, axis=0)
    gates_term = lax.dynamic_update_slice_in_dim(jnp.zeros((H,), f32), own_gate_grad, head_start, 0)
    cond_count, gains_count = cond_part.size, gains_term.size
    packed = jnp.concatenate([cond_part.reshape(-1), gains_term.reshape(-1), gates_term])
    packed = jnp.pad(packed, (0, -packed.shape[0] % 1024)).reshape(-1, 1024)
    packed = packed + pair_sum(grid, packed, 1)
    packed = packed + pair_sum(grid, packed, 2)
    packed, qkv_sum = fence(packed, qkv_sum)
    packed = packed + pair_sum(grid, packed, 4)
    packed, null_moved = fence(packed, null_moved)
    null_grad = reorder_columns(
        null_part.astype(f32) + null_moved.astype(f32), owners, False
    )
    qkv_grad = qkv_sum.astype(f32).reshape(depth, 3, own_width)
    packed = sum_seq(grid, packed, 8)
    packed = (packed + swap_txt(packed)).reshape(-1)
    condition_grad = packed[:cond_count].reshape(cond_part.shape)
    norm_gains_grad = packed[cond_count : cond_count + gains_count].reshape(gains_term.shape)
    head_gates_grad = packed[cond_count + gains_count : cond_count + gains_count + H]
    return (
        block_out,
        video_grad,
        condition_grad,
        qkv_grad,
        out_grad,
        gate_grad,
        up_grad,
        down_grad,
        text_grad,
        ada_weight_grad,
        ada_bias_grad,
        null_grad,
        norm_gains_grad,
        head_gates_grad,
    )


def solution(mesh):
    placed = (
        P("seq", None),
        P("seq", None),
        P(),
        P("seq", "txt", None),
        P("txt", None),
        P("txt", None),
        P("seq", None, "txt"),
        P("seq", "txt"),
        P("seq", "txt"),
        P("seq", "txt"),
        P("seq", "txt"),
        P("seq", None, "txt"),
        P(None, ("seq", "txt")),
        P(("seq", "txt")),
        P(),
        P(),
        P("seq", None),
        P(),
        P(),
    )
    return jax.shard_map(
        local,
        mesh=mesh,
        in_specs=placed,
        out_specs=(
            P("seq", None),
            P("seq", None),
            P(),
            P("seq", None, "txt"),
            P("seq", "txt"),
            P("seq", "txt"),
            P("seq", "txt"),
            P("seq", "txt"),
            P("seq", None, "txt"),
            P(None, ("seq", "txt")),
            P(("seq", "txt")),
            P(),
            P(),
            P(),
        ),
        check_vma=False,
    )
```

```python
import functools
import math

import jax
import jax.numpy as jnp
from jax import lax
from jax.experimental import pallas as pl
from jax.experimental.pallas import tpu as pltpu
from jax.sharding import PartitionSpec as P

H = 24
HD = 64
TXT_LEN = 64
LONG_DEV = 64

epsilon = 1e-05
negative = -1e30
highest = lax.Precision.HIGHEST
bf16 = jnp.bfloat16
f32 = jnp.float32


def layout(lengths_row, seq_index, long_rows, short_rows):
    clip_count = lengths_row.shape[0]
    clip_ends = jnp.cumsum(lengths_row)
    clip_starts = clip_ends - lengths_row
    row_ids = jnp.arange(short_rows, dtype=jnp.int32)
    local_clip = jnp.sum(
        (row_ids[:, None] >= clip_ends[None, : clip_count - 1]).astype(jnp.int32), axis=1
    )
    chosen = local_clip[:, None] == jnp.arange(clip_count, dtype=jnp.int32)[None, :]
    clip_begin = jnp.sum(jnp.where(chosen, clip_starts[None, :], 0), axis=1)
    clip_local = jnp.concatenate([jnp.full((long_rows,), clip_count, jnp.int32), local_clip])
    long_place = seq_index * long_rows + jnp.arange(long_rows, dtype=jnp.int32)
    position = jnp.concatenate([long_place, row_ids - clip_begin])
    return (clip_local, position)


def rms_parts(values):
    inverse = lax.rsqrt(jnp.mean(values * values, axis=-1, keepdims=True) + epsilon)
    return (values * inverse, inverse)


def rms_back(grad_hat, normed, inverse):
    return inverse * (grad_hat - normed * jnp.mean(grad_hat * normed, axis=-1, keepdims=True))


def dot(left_side, right_side):
    return jnp.dot(left_side, right_side, preferred_element_type=f32)


def dot_pieces(left_side, pieces):
    depth = pieces[0].shape[0]
    total = 0.0
    for place, piece in enumerate(pieces):
        total = total + dot(left_side[:, place * depth : (place + 1) * depth], piece)
    return total


def contract_rows(left_side, right_side):
    return lax.dot_general(
        left_side, right_side, (((0,), (0,)), ((), ())), preferred_element_type=f32
    )


def contract_cols(left_side, right_side):
    return lax.dot_general(
        left_side, right_side, (((1,), (1,)), ((), ())), preferred_element_type=f32
    )


def swap_txt(values):
    return lax.ppermute(values, "txt", [(0, 1), (1, 0)])


def rounded(values):
    return lax.reduce_precision(values, exponent_bits=8, mantissa_bits=7)


def fence(*values):
    return lax.optimization_barrier(values)


class Grid:
    def __init__(self):
        self.count = lax.axis_size("seq")
        self.outer_count = 4
        self.inner_count = self.count // 8
        self.index = lax.axis_index("seq")
        self.core = self.index % 2
        self.inner = (self.index // 2) % self.inner_count
        self.outer = self.index // (2 * self.inner_count)

    def send(self, values, outer=0, inner=0, core=0):
        pairs = []
        for index in range(self.count):
            to_core = (index + core) % 2
            to_inner = (index // 2 + inner) % self.inner_count
            to_outer = (index // (2 * self.inner_count) + outer) % self.outer_count
            pairs.append((index, (to_outer * self.inner_count + to_inner) * 2 + to_core))
        return lax.ppermute(values, "seq", pairs)

    def lines(self):
        step = 2 * self.inner_count
        return [[first + step * k for k in range(self.outer_count)] for first in range(step)]

    def owners(self):
        place = jnp.arange(self.count, dtype=jnp.int32)
        outer = place % self.outer_count
        inner = (self.inner - (place // self.outer_count) % self.inner_count) % self.inner_count
        core = (self.core + place // (self.outer_count * self.inner_count)) % 2
        return (outer * self.inner_count + inner) * 2 + core


def gather_outer(grid, block):
    return lax.all_gather(block, "seq", axis=0, tiled=True, axis_index_groups=grid.lines())


def send_inner(grid, near):
    return [grid.send(near, inner=step) for step in range(1, grid.inner_count)]


def send_core(grid, pieces):
    return [grid.send(piece, core=1) for piece in pieces]


def stack(pieces):
    return jnp.concatenate(pieces, axis=0) if len(pieces) > 1 else pieces[0]


def add_blocks(*refs):
    *sources, target = refs
    total = sources[0][...].astype(f32)
    for source in sources[1:]:
        total = total + source[...].astype(f32)
    target[...] = total.astype(target.dtype)


def add_rows(arrays, starts, rows):
    cols = arrays[0].shape[1]
    block = 256 if rows % 256 == 0 else 128 if rows % 128 == 0 else rows

    def from_row(start):
        return pl.BlockSpec((block, cols), lambda i: (start // block + i, 0))

    return pl.pallas_call(
        add_blocks,
        grid=(rows // block,),
        in_specs=[from_row(start) for start in starts],
        out_specs=from_row(0),
        out_shape=jax.ShapeDtypeStruct((rows, cols), bf16),
        cost_estimate=pl.CostEstimate(flops=1, bytes_accessed=1, transcendentals=0),
        compiler_params=pltpu.CompilerParams(vmem_limit_bytes=48 * 1024 * 1024),
        name="add_rows",
    )(*arrays)


def join_blocks(*refs):
    *sources, target = refs
    half = len(sources) // 2
    totals = []
    for part in (sources[:half], sources[half:]):
        total = part[0][...].astype(f32)
        for source in part[1:]:
            total = total + source[...].astype(f32)
        totals.append(total.astype(bf16))
    rows, width = totals[0].shape[0], totals[1].shape[1]
    target[0, :rows, :] = totals[0][:, :width]
    target[0, rows : 2 * rows, :] = totals[0][:, width:]
    target[0, 2 * rows :, :] = totals[1]


def join_sums(grid, long_parts, out_parts, long_rows, out_rows):
    width = out_parts[0].shape[1]
    rows = 2 * long_rows + out_rows
    long_spec = pl.BlockSpec((long_rows, 2 * width), lambda i: (i, 0))
    out_spec = pl.BlockSpec((out_rows, width), lambda i: (i, 0))
    joined = pl.pallas_call(
        join_blocks,
        grid=(grid.outer_count,),
        in_specs=[long_spec] * len(long_parts) + [out_spec] * len(out_parts),
        out_specs=pl.BlockSpec((1, rows, width), lambda i: (i, 0, 0)),
        out_shape=jax.ShapeDtypeStruct((grid.outer_count, rows, width), bf16),
        cost_estimate=pl.CostEstimate(flops=1, bytes_accessed=1, transcendentals=0),
        name="join_sums",
    )(*long_parts, *out_parts)
    return joined.reshape(grid.outer_count * rows, width)


def core_away(grid, kept, moved):
    rows = kept.shape[0] // grid.inner_count
    return [
        add_rows([kept, moved], [step * rows] * 2, rows) for step in range(1, grid.inner_count)
    ]


def inner_total(grid, kept, moved, arrived):
    rows = kept.shape[0] // grid.inner_count
    return add_rows([kept, moved] + arrived, [0] * (2 + len(arrived)), rows)


def swap_inner(grid, away):
    return [grid.send(part, inner=-step) for step, part in enumerate(away, 1)]


def sum_outer(grid, total):
    return lax.psum_scatter(
        total, "seq", scatter_dimension=0, tiled=True, axis_index_groups=grid.lines()
    )


def pair_sum(grid, values, bit):
    pairs = [(index, index ^ bit) for index in range(grid.count)]
    return lax.ppermute(values, "seq", pairs)


def turn_stage(values, axis, size, own, send):
    moved = [lax.dynamic_index_in_dim(values, own, axis, keepdims=False)]
    for step in range(1, size):
        piece = lax.dynamic_index_in_dim(values, (own + step) % size, axis, keepdims=False)
        moved.append(send(piece, step))
    stacked = jnp.stack(moved, axis=axis)
    order = (own - jnp.arange(size, dtype=jnp.int32)) % size
    return jnp.take(stacked, order, axis=axis)


def turn_seq(grid, values):
    rest = values.shape[1:]
    values = values.reshape((grid.outer_count, grid.inner_count, 2) + rest)
    values = turn_stage(
        values, 0, grid.outer_count, grid.outer, lambda v, k: grid.send(v, outer=k)
    )
    values = turn_stage(
        values, 1, grid.inner_count, grid.inner, lambda v, k: grid.send(v, inner=k)
    )
    values = turn_stage(values, 2, 2, grid.core, lambda v, k: grid.send(v, core=k))
    return values.reshape((grid.count,) + rest)


def sum_seq(grid, values, bit):
    while bit < grid.count:
        values = values + pair_sum(grid, values, bit)
        bit *= 2
    return values


def copy_blocks(to_order, count, order_ref, source_ref, target_ref):
    width = source_ref.shape[1] // count
    for block in range(count):
        moved = pl.ds(pl.multiple_of(order_ref[block] * width, width), width)
        plain = pl.ds(block * width, width)
        if to_order:
            target_ref[:, plain] = source_ref[:, moved]
        else:
            target_ref[:, moved] = source_ref[:, plain]


def reorder_columns(values, order, to_order):
    rows, cols = values.shape
    count = order.shape[0]
    width = cols // count
    if width % 128:
        taken = order if to_order else jnp.argsort(order)
        return jnp.take(values.reshape(rows, count, width), taken, axis=1).reshape(rows, cols)
    return pl.pallas_call(
        functools.partial(copy_blocks, to_order, count),
        out_shape=jax.ShapeDtypeStruct(values.shape, values.dtype),
        in_specs=[
            pl.BlockSpec(memory_space=pltpu.SMEM),
            pl.BlockSpec(memory_space=pltpu.VMEM),
        ],
        out_specs=pl.BlockSpec(memory_space=pltpu.VMEM),
        name="reorder_columns",
    )(order, values)


def split_three(values):
    high = rounded(values)
    rest = values - high
    middle = rounded(rest)
    return high.astype(bf16), middle.astype(bf16), (rest - middle).astype(bf16)


def exact_dot(values, one_hot):
    rows = values.shape[0]
    parts = dot(jnp.concatenate(split_three(values), axis=0), one_hot)
    return parts[:rows] + parts[rows : 2 * rows] + parts[2 * rows :]


def choose(clip, rows):
    chosen = rows[-1:]
    for index in range(rows.shape[0] - 1):
        chosen = jnp.where(clip == index, rows[index : index + 1], chosen)
    return chosen


def add_clip_sums(clip, values, sums_ref):
    @pl.when(pl.program_id(0) == 0)
    def _():
        sums_ref[...] = jnp.zeros_like(sums_ref)

    for index in range(sums_ref.shape[0]):
        part = jnp.sum(jnp.where(clip == index, values, 0.0), axis=0, keepdims=True)
        sums_ref[index : index + 1, :] += part


def add_pair(own_ref, moved_ref):
    return own_ref[...].astype(f32) + moved_ref[...].astype(f32)


def enter_rows(clip_ref, hidden_ref, part_ref, moved_ref, tanh_ref, scale_ref, gains_ref, res_ref, in_ref):
    clip = clip_ref[...]
    attn_hat, _ = rms_parts(add_pair(part_ref, moved_ref))
    tanh_tok = choose(clip, tanh_ref[...])
    residual = hidden_ref[...].astype(f32) + tanh_tok * attn_hat * gains_ref[1:2]
    res_hat, _ = rms_parts(residual)
    res_ref[...] = residual
    in_ref[...] = (res_hat * gains_ref[2:3] * choose(clip, scale_ref[...])).astype(bf16)


def leave_rows(clip_ref, res_ref, part_ref, moved_ref, up_ref, tanh_ref, gains_ref, out_ref, grad_ref, sums_ref):
    clip = clip_ref[...]
    hat, inverse = rms_parts(add_pair(part_ref, moved_ref))
    upstream = up_ref[...].astype(f32)
    tanh_tok = choose(clip, tanh_ref[...])
    out_ref[...] = (res_ref[...] + tanh_tok * hat * gains_ref[3:4]).astype(bf16)
    grad_ref[...] = rms_back(upstream * tanh_tok * gains_ref[3:4], hat, inverse).astype(bf16)
    add_clip_sums(clip, upstream * hat, sums_ref)


def middle_rows(
    clip_ref, res_ref, grad_part_ref, grad_moved_ref, up_ref, part_ref, moved_ref, tanh_ref,
    scale_ref, gains_ref, grad_res_ref, grad_attn_ref, res_sums_ref, attn_sums_ref,
):
    clip = clip_ref[...]
    grad = add_pair(grad_part_ref, grad_moved_ref)
    hat, inverse = rms_parts(res_ref[...])
    add_clip_sums(clip, grad * hat, res_sums_ref)
    grad_hat = grad * gains_ref[2:3] * choose(clip, scale_ref[...])
    grad_res = up_ref[...].astype(f32) + rms_back(grad_hat, hat, inverse)
    grad_res_ref[...] = grad_res
    hat, inverse = rms_parts(add_pair(part_ref, moved_ref))
    add_clip_sums(clip, grad_res * hat, attn_sums_ref)
    grad_hat = grad_res * gains_ref[1:2] * choose(clip, tanh_ref[...])
    grad_attn_ref[...] = rms_back(grad_hat, hat, inverse).astype(bf16)


def last_rows(
    clip_ref, hidden_ref, part_ref, moved_ref, grad_res_ref, scale_ref, gains_ref, high_ref, low_ref,
    sums_ref,
):
    clip = clip_ref[...]
    grad = add_pair(part_ref, moved_ref)
    hat, inverse = rms_parts(hidden_ref[...].astype(f32))
    add_clip_sums(clip, grad * hat, sums_ref)
    grad_hat = grad * gains_ref[0:1] * choose(clip, scale_ref[...])
    total = grad_res_ref[...] + rms_back(grad_hat, hat, inverse)
    high = total.astype(bf16)
    high_ref[...] = high
    low_ref[...] = (total - high.astype(f32)).astype(bf16)


def row_call(body, name, arrays, tables, outs, sums):
    count, width = arrays[1].shape
    rows = count // 4

    def by_rows(array):
        return pl.BlockSpec((rows, array.shape[1]), lambda i: (i, 0))

    def whole(array):
        return pl.BlockSpec(array.shape, lambda i: (0, 0))

    out_shapes = [jax.ShapeDtypeStruct((count, width), kind) for kind in outs]
    sum_shapes = [jax.ShapeDtypeStruct((tables[0].shape[0], width), f32)] * sums
    return pl.pallas_call(
        body,
        grid=(4,),
        in_specs=[by_rows(array) for array in arrays] + [whole(table) for table in tables],
        out_specs=[by_rows(shape) for shape in out_shapes] + [whole(shape) for shape in sum_shapes],
        out_shape=out_shapes + sum_shapes,
        cost_estimate=pl.CostEstimate(flops=1, bytes_accessed=1, transcendentals=0),
        compiler_params=pltpu.CompilerParams(vmem_limit_bytes=48 * 1024 * 1024),
        name=name,
    )(*arrays, *tables)


def head_means(values):
    first = lax.broadcasted_iota(jnp.int32, values.shape, 1) < HD
    front = jnp.sum(jnp.where(first, values, 0.0), axis=1, keepdims=True)
    back = jnp.sum(jnp.where(first, 0.0, values), axis=1, keepdims=True)
    return jnp.where(first, front, back) * (1.0 / HD)


def turn_lanes(values, cosine, sine):
    lane = lax.broadcasted_iota(jnp.int32, values.shape, 1) % HD
    ahead = pltpu.roll(values, 2 * HD - HD // 2, 1)
    behind = pltpu.roll(values, HD // 2, 1)
    return values * cosine + jnp.where(lane < HD // 2, -ahead, behind) * sine


def norm_heads(values_ref, gain_ref, cos_ref, sin_ref, out_ref):
    cosine, sine = cos_ref[...], sin_ref[...]
    for start in range(0, out_ref.shape[1], 2 * HD):
        part = slice(start, start + 2 * HD)
        values = values_ref[:, part]
        hat = values * lax.rsqrt(head_means(values * values) + epsilon)
        out_ref[:, part] = turn_lanes(hat * gain_ref[:, part], cosine, sine).astype(bf16)


def norm_heads_back(*refs):
    values_ref, gain_ref, cos_ref, sin_ref, *grad_refs, out_ref, sums_ref = refs
    cosine, sine = cos_ref[...], sin_ref[...]

    @pl.when(pl.program_id(0) == 0)
    def _():
        sums_ref[...] = jnp.zeros_like(sums_ref)

    for start in range(0, out_ref.shape[1], 2 * HD):
        part = slice(start, start + 2 * HD)
        values = values_ref[:, part]
        inverse = lax.rsqrt(head_means(values * values) + epsilon)
        hat = values * inverse
        grad = grad_refs[0][:, part]
        for grad_ref in grad_refs[1:]:
            grad = grad + grad_ref[:, part]
        grad = turn_lanes(grad, cosine, -sine)
        sums_ref[:, part] += jnp.sum(grad * hat, axis=0, keepdims=True)
        grad = grad * gain_ref[:, part]
        out_ref[:, part] = (inverse * (grad - hat * head_means(grad * hat))).astype(bf16)


def head_call(body, name, values, column, gain, turns, grads=()):
    count, width = turns[0].shape[0], gain.shape[1]
    rows = count // 4
    by_rows = pl.BlockSpec((rows, width), lambda i: (i, 0))
    whole = pl.BlockSpec((1, width), lambda i: (0, 0))
    turn = pl.BlockSpec((rows, 2 * HD), lambda i: (i, 0))
    out_shape = [jax.ShapeDtypeStruct((count, width), bf16)]
    out_specs = [by_rows]
    if grads:
        out_shape.append(jax.ShapeDtypeStruct((1, width), f32))
        out_specs.append(whole)
    results = pl.pallas_call(
        body,
        grid=(4,),
        in_specs=[pl.BlockSpec((rows, width), lambda i: (i, column)), whole, turn, turn]
        + [by_rows] * len(grads),
        out_specs=out_specs,
        out_shape=out_shape,
        cost_estimate=pl.CostEstimate(flops=1, bytes_accessed=1, transcendentals=0),
        compiler_params=pltpu.CompilerParams(vmem_limit_bytes=48 * 1024 * 1024),
        name=name,
    )(values, gain, *turns, *grads)
    return results if grads else results[0]


def attend_heads(clip_ref, key_clip_ref, query_ref, key_ref, value_ref, out_ref, total_ref):
    visible = clip_ref[...] == key_clip_ref[...]
    for start in range(0, 2 * HD, HD):
        head = slice(start, start + HD)
        scores = contract_cols(query_ref[:, head], key_ref[:, head]) * HD ** (-0.5)
        scores = jnp.where(visible, scores, negative)
        peak = jnp.max(scores, axis=1, keepdims=True)
        exponent = jnp.exp(scores - peak)
        total = jnp.sum(exponent, axis=1, keepdims=True)
        out_ref[:, head] = dot((exponent / total).astype(bf16), value_ref[:, head])
        total_ref[:, head] = jnp.broadcast_to(peak + jnp.log(total), (total_ref.shape[0], HD))


def attend_heads_back(
    clip_ref, key_clip_ref, query_ref, key_ref, value_ref, grad_ref, out_ref, total_ref,
    grad_query_ref, grad_key_ref, grad_value_ref,
):
    visible = clip_ref[...] == key_clip_ref[...]
    for start in range(0, 2 * HD, HD):
        head = slice(start, start + HD)
        query, key = query_ref[:, head], key_ref[:, head]
        grad = grad_ref[:, head]
        scores = contract_cols(query, key) * HD ** (-0.5)
        weights = jnp.where(visible, jnp.exp(scores - total_ref[:, start : start + 1]), 0.0)
        delta = jnp.sum(grad.astype(f32) * out_ref[:, head], axis=1, keepdims=True)
        grad_scores = weights * (contract_cols(grad, value_ref[:, head]) - delta)
        grad_scores = grad_scores.astype(bf16)
        grad_query_ref[:, head] = dot(grad_scores, key) * HD ** (-0.5)
        grad_key = contract_rows(grad_scores, query) * HD ** (-0.5)
        grad_key_ref[:, head] = grad_key.astype(grad_key_ref.dtype)
        grad_value = contract_rows(weights.astype(bf16), grad)
        grad_value_ref[:, head] = grad_value.astype(grad_value_ref.dtype)


def attend_call(name, clips, key_clips, query, key, value, value_column=0, back=(), kind=f32):
    count, keys, width = query.shape[0], key.shape[0], query.shape[1]
    first = value_column // (2 * HD)
    queries = pl.BlockSpec((count, 2 * HD), lambda i: (0, i))
    seen = pl.BlockSpec((keys, 2 * HD), lambda i: (0, i))
    whole = [pl.BlockSpec(array.shape, lambda i: (0, 0)) for array in (clips, key_clips)]
    out_shape = [jax.ShapeDtypeStruct((count, width), f32)]
    if back:
        out_shape += [jax.ShapeDtypeStruct((keys, width), kind)] * 2
        out_specs = [queries, seen, seen]
    else:
        out_shape += out_shape
        out_specs = [queries, queries]
    return pl.pallas_call(
        attend_heads_back if back else attend_heads,
        grid=(width // (2 * HD),),
        in_specs=whole
        + [queries, seen, pl.BlockSpec((keys, 2 * HD), lambda i: (0, first + i))]
        + [queries] * len(back),
        out_specs=out_specs,
        out_shape=out_shape,
        cost_estimate=pl.CostEstimate(flops=1, bytes_accessed=1, transcendentals=0),
        compiler_params=pltpu.CompilerParams(vmem_limit_bytes=48 * 1024 * 1024),
        name=name,
    )(clips, key_clips, query, key, value, *back)


def local(
    video_tokens,
    cotangent,
    condition,
    captions,
    long_caption,
    null_embed,
    query_key_value,
    out_weight,
    gate_weight,
    up_weight,
    down_weight,
    text_weight,
    ada_weight,
    ada_bias,
    norm_gains,
    head_gates,
    clip_lengths,
    null_mask,
    text_lengths,
):
    grid = Grid()
    seq_index = grid.index
    seq_count = grid.count
    txt_index = lax.axis_index("txt")
    first_half = txt_index == 0
    token_count, model_width = video_tokens.shape
    depth = query_key_value.shape[0]
    text_depth, text_width = text_weight.shape[0], captions.shape[2]
    half_width = model_width // 2
    own_heads = query_key_value.shape[2] // HD
    own_width = own_heads * HD
    head_start = txt_index * own_heads
    clip_total = condition.shape[0]
    short_clips = clip_lengths.shape[1]
    clip_local, position = layout(clip_lengths[0], seq_index, LONG_DEV, token_count - LONG_DEV)
    owners = grid.owners()
    text_rows = (short_clips + 1) * TXT_LEN

    half_text = text_width // 2
    text_block = text_weight.reshape(text_depth, 2 * own_width)

    qkv_block, condition = fence(query_key_value.reshape(depth, 3 * own_width), condition)
    qkv_near = gather_outer(grid, qkv_block)
    shifted = jax.nn.silu(condition.astype(f32)).astype(bf16)
    mod_part = dot(shifted, ada_weight) + ada_bias
    short_part = mod_part[: clip_total - 1].reshape(seq_count, short_clips, mod_part.shape[1])
    long_part = jnp.broadcast_to(
        mod_part[clip_total - 1 :][None], (seq_count, 1, mod_part.shape[1])
    )
    own_part = turn_seq(grid, jnp.concatenate([short_part, long_part], axis=1))
    other_part = swap_txt(own_part)
    own_null = lax.dynamic_slice_in_dim(null_mask, seq_index * short_clips, short_clips, 0) == 1
    short_feats = jnp.where(own_null[:, None, None], null_embed[None], captions)
    long_feats = jnp.where(null_mask[clip_total - 1] == 1, null_embed, long_caption)
    own_feats = jnp.concatenate([short_feats, long_feats[None]], axis=0).reshape(-1, text_width)
    own_feats = reorder_columns(own_feats, owners, True)

    columns = jnp.arange(model_width, dtype=jnp.int32)
    column_order = jnp.repeat(owners, depth) * depth + columns % depth
    one_hot = (columns[:, None] == column_order[None, :]).astype(bf16)
    hidden = dot(video_tokens, one_hot).astype(bf16)
    hidden_hat, _ = rms_parts(hidden.astype(f32))
    clip_column = clip_local[:, None]
    tkey_block, tval_block = text_block[:, :own_width], text_block[:, own_width:]
    qkv_near, own_part, other_part, own_feats, tkey_block, tval_block, out_weight = fence(
        qkv_near, own_part, other_part, own_feats, tkey_block, tval_block, out_weight
    )

    qkv_y = send_inner(grid, qkv_near)
    qkv_near_core = send_core(grid, [qkv_near])
    tkey_near = gather_outer(grid, tkey_block)
    out_near = gather_outer(grid, out_weight)
    other_feats = swap_txt(own_feats)
    own_mod = jnp.stack(
        [jnp.where(first_half, own_part, other_part), jnp.where(first_half, other_part, own_part)],
        axis=1,
    )
    own_mod = jnp.transpose(own_mod, (2, 0, 1, 3)).reshape((short_clips + 1) * 4, model_width)
    rows = exact_dot(jnp.concatenate([own_mod, norm_gains[:4]], axis=0), one_hot)
    gains = rows[-4:]
    own_mod = rows[:-4].reshape(short_clips + 1, 4, model_width)
    own_scales = 1.0 + own_mod[:, 0], 1.0 + own_mod[:, 2]
    own_tanhs = jnp.tanh(own_mod[:, 1]), jnp.tanh(own_mod[:, 3])
    selector = clip_local[:, None] == jnp.arange(short_clips + 1, dtype=jnp.int32)[None, :]

    def per_token(rows):
        chosen = rows[short_clips:]
        for clip in range(short_clips):
            chosen = jnp.where(selector[:, clip : clip + 1], rows[clip : clip + 1], chosen)
        return chosen

    normed_in = (hidden_hat * gains[0] * per_token(own_scales[0])).astype(bf16)
    query_gain, key_gain, text_gain = [
        lax.dynamic_slice(norm_gains, (row, head_start * HD), (1, own_width)) for row in (4, 5, 6)
    ]
    frequency = jnp.exp(
        jnp.arange(HD // 2, dtype=f32) * (-math.log(10000.0) / (HD // 2))
    )
    angles = jnp.tile(position.astype(f32)[:, None] * frequency, (1, 4))
    turns = jnp.cos(angles), jnp.sin(angles)
    text_turns = jnp.ones((text_rows, 2 * HD), f32), jnp.zeros((text_rows, 2 * HD), f32)
    normed_in, other_feats, tkey_near, out_near, tval_block, qkv_near_core, qkv_y = fence(
        normed_in, other_feats, tkey_near, out_near, tval_block, qkv_near_core, qkv_y
    )

    tkey_y = send_inner(grid, tkey_near)
    tkey_near_core = send_core(grid, [tkey_near])
    out_near_core = send_core(grid, [out_near])
    tval_near = gather_outer(grid, tval_block)
    qkv_core, normed_in = fence(send_core(grid, qkv_y), normed_in)
    qkv_own, qkv_other = stack([qkv_near] + qkv_y), stack(qkv_near_core + qkv_core)
    projected = dot(normed_in[:, :half_width], qkv_own) + dot(normed_in[:, half_width:], qkv_other)
    query_bf = head_call(norm_heads, "norm_queries", projected, 0, query_gain, turns)
    key_bf = head_call(norm_heads, "norm_keys", projected, 1, key_gain, turns)
    value_bf = projected[:, 2 * own_width :].astype(bf16)
    long_block = jnp.concatenate([key_bf[:LONG_DEV], value_bf[:LONG_DEV]], axis=1)
    (
        query_bf, key_bf, value_bf, long_block, tkey_y, tkey_near_core, out_near, out_near_core,
        tval_near, gate_weight,
    ) = fence(
        query_bf, key_bf, value_bf, long_block, tkey_y, tkey_near_core, out_near, out_near_core,
        tval_near, gate_weight,
    )

    tail = long_block.size // gate_weight.shape[1]
    gate_near = gather_outer(
        grid, jnp.concatenate([gate_weight, long_block.reshape(tail, -1)], axis=0)
    )
    tval_y = send_inner(grid, tval_near)
    tval_near_core = send_core(grid, [tval_near])
    short_query = query_bf[LONG_DEV:]
    short_key = key_bf[LONG_DEV:]
    short_value = value_bf[LONG_DEV:]
    short_clip = clip_column[LONG_DEV:]
    short_seen = clip_local[LONG_DEV:][None, :]
    short_out, short_lse = attend_call(
        "attend_short", short_clip, short_seen, short_query, short_key, short_value
    )
    out_y = send_inner(grid, out_near)
    tkey_core = send_core(grid, tkey_y)
    feats = jnp.concatenate(
        [
            jnp.where(first_half, own_feats, other_feats).reshape(-1, TXT_LEN // 2, text_width),
            jnp.where(first_half, other_feats, own_feats).reshape(-1, TXT_LEN // 2, text_width),
        ],
        axis=1,
    ).reshape(text_rows, text_width)
    tval_y, tval_near_core, gate_near, tkey_core, out_y, up_weight, feats, short_out = fence(
        tval_y, tval_near_core, gate_near, tkey_core, out_y, up_weight, feats, short_out
    )

    gate_near = gate_near.reshape(grid.outer_count, depth + tail, -1)
    long_near = gate_near[:, depth:].reshape(-1, 2 * own_width)
    gate_near = gate_near[:, :depth].reshape(grid.outer_count * depth, -1)
    long_y = send_inner(grid, long_near)
    long_near_core = send_core(grid, [long_near])
    gate_y = send_inner(grid, gate_near)
    gate_near_core = send_core(grid, [gate_near])
    up_near = gather_outer(grid, up_weight)
    tval_core = send_core(grid, tval_y)
    long_core = send_core(grid, long_y)
    out_core = send_core(grid, out_y)
    tkey_pieces = [tkey_near] + tkey_y + tkey_near_core + tkey_core
    text_raw = dot_pieces(feats, tkey_pieces)
    text_key_bf = head_call(norm_heads, "norm_text", text_raw, 0, text_gain, text_turns)

    out_own, out_other = stack([out_near] + out_y), stack(out_near_core + out_core)
    long_pairs = stack([long_near] + long_y + long_near_core + long_core)
    long_count = long_pairs.shape[0]
    long_query = query_bf[:LONG_DEV]
    long_clip = clip_column[:LONG_DEV]
    long_seen = jnp.full((1, long_count), short_clips, jnp.int32)
    long_out, long_lse = attend_call(
        "attend_long", long_clip, long_seen, long_query, long_pairs, long_pairs, own_width
    )
    tval_pieces = [tval_near] + tval_y + tval_near_core + tval_core
    text_value_bf = dot_pieces(feats, tval_pieces).astype(bf16)
    key_clip = jnp.arange(text_rows, dtype=jnp.int32) // TXT_LEN
    key_place = jnp.arange(text_rows, dtype=jnp.int32) % TXT_LEN
    limits = jnp.concatenate(
        [
            lax.dynamic_slice_in_dim(text_lengths, seq_index * short_clips, short_clips, 0),
            text_lengths[clip_total - 1 :],
        ]
    )
    clip_match = key_clip[:, None] == jnp.arange(short_clips + 1, dtype=jnp.int32)[None, :]
    key_limit = jnp.sum(jnp.where(clip_match, limits[None, :], 0), axis=1)
    cross_seen = jnp.where(key_place < key_limit, key_clip, -1)[None, :]
    cross_out, cross_lse = attend_call(
        "attend_cross", clip_column, cross_seen, query_bf, text_key_bf, text_value_bf
    )
    attended = jnp.concatenate([long_out, short_out], axis=0)
    own_gates = lax.dynamic_slice_in_dim(head_gates, head_start, own_heads, 0)
    gate_tanh = jnp.repeat(jnp.tanh(own_gates), HD)[None, :]
    combined_bf = (attended + gate_tanh * cross_out).astype(bf16)
    attn_part = rounded(
        jnp.concatenate(
            [contract_cols(combined_bf, out_own), contract_cols(combined_bf, out_other)], axis=1
        )
    ).astype(bf16)
    attn_part, gate_y, gate_near_core, up_near, down_weight = fence(
        attn_part, gate_y, gate_near_core, up_near, down_weight
    )

    attn_moved = swap_txt(attn_part)
    up_y = send_inner(grid, up_near)
    up_near_core = send_core(grid, [up_near])
    down_near = gather_outer(grid, down_weight)
    gate_core = send_core(grid, gate_y)
    attn_moved, up_y, up_near_core, down_near, gate_core = fence(
        attn_moved, up_y, up_near_core, down_near, gate_core
    )

    down_y = send_inner(grid, down_near)
    down_near_core = send_core(grid, [down_near])
    up_core = send_core(grid, up_y)
    gate_own, gate_other = stack([gate_near] + gate_y), stack(gate_near_core + gate_core)
    residual, ffn_in_bf = row_call(
        enter_rows,
        "enter_rows",
        [clip_column, hidden, attn_part, attn_moved],
        [own_tanhs[0], own_scales[1], gains],
        [f32, bf16],
        0,
    )
    gate_value = dot(ffn_in_bf[:, :half_width], gate_own) + dot(
        ffn_in_bf[:, half_width:], gate_other
    )
    up_core, gate_value = fence(up_core, gate_value)
    up_own, up_other = stack([up_near] + up_y), stack(up_near_core + up_core)
    up_value = dot(ffn_in_bf[:, :half_width], up_own) + dot(ffn_in_bf[:, half_width:], up_other)
    sigmoid_gate = jax.nn.sigmoid(gate_value)
    silu_gate = gate_value * sigmoid_gate
    inner_bf = (silu_gate * up_value).astype(bf16)
    inner_bf, down_y, down_near_core = fence(inner_bf, down_y, down_near_core)

    down_core = send_core(grid, down_y)
    upstream = dot(cotangent, one_hot).astype(bf16)
    down_core, inner_bf, upstream = fence(down_core, inner_bf, upstream)
    down_own, down_other = stack([down_near] + down_y), stack(down_near_core + down_core)
    ffn_part = rounded(
        jnp.concatenate(
            [contract_cols(inner_bf, down_own), contract_cols(inner_bf, down_other)], axis=1
        )
    ).astype(bf16)
    (ffn_part,) = fence(ffn_part)

    ffn_moved = swap_txt(ffn_part)
    ffn_moved, ffn_part = fence(ffn_moved, ffn_part)

    block_out, grad_ffn_out, ffn_sums = row_call(
        leave_rows,
        "leave_rows",
        [clip_column, residual, ffn_part, ffn_moved, upstream],
        [own_tanhs[1], gains],
        [bf16, bf16],
        1,
    )
    down_kept = contract_rows(grad_ffn_out[:, :half_width], inner_bf).astype(bf16)
    down_away = contract_rows(grad_ffn_out[:, half_width:], inner_bf).astype(bf16)
    grad_ffn_out, down_away, down_kept = fence(grad_ffn_out, down_away, down_kept)

    down_core = grid.send(down_away, core=1)
    grad_inner = dot(grad_ffn_out[:, :half_width], down_own) + dot(
        grad_ffn_out[:, half_width:], down_other
    )
    silu_slope = sigmoid_gate * (1.0 + gate_value * (1.0 - sigmoid_gate))
    grad_gate_bf = (grad_inner * up_value * silu_slope).astype(bf16)
    grad_up_bf = (grad_inner * silu_gate).astype(bf16)
    ffn_in_part = rounded(
        jnp.concatenate(
            [
                contract_cols(grad_gate_bf, gate_own) + contract_cols(grad_up_bf, up_own),
                contract_cols(grad_gate_bf, gate_other) + contract_cols(grad_up_bf, up_other),
            ],
            axis=1,
        )
    ).astype(bf16)
    gate_away = contract_rows(ffn_in_bf[:, half_width:], grad_gate_bf).astype(bf16)
    down_away = core_away(grid, down_kept, down_core)
    down_core, down_away, ffn_in_part, gate_away, grad_gate_bf, grad_up_bf = fence(
        down_core, down_away, ffn_in_part, gate_away, grad_gate_bf, grad_up_bf
    )

    ffn_in_moved = swap_txt(ffn_in_part)
    down_moved = swap_inner(grid, down_away)
    gate_core = grid.send(gate_away, core=1)
    gate_kept = contract_rows(ffn_in_bf[:, :half_width], grad_gate_bf).astype(bf16)
    up_kept = contract_rows(ffn_in_bf[:, :half_width], grad_up_bf).astype(bf16)
    up_away = contract_rows(ffn_in_bf[:, half_width:], grad_up_bf).astype(bf16)
    block_out = contract_cols(block_out, one_hot).astype(bf16)
    gate_away = core_away(grid, gate_kept, gate_core)
    block_out, ffn_in_moved, down_moved, up_kept = fence(
        block_out, ffn_in_moved, down_moved, up_kept
    )

    down_total = inner_total(grid, down_kept, down_core, down_moved)
    gate_moved = swap_inner(grid, gate_away)
    up_core = grid.send(up_away, core=1)
    ffn_in_moved, down_total = fence(ffn_in_moved, down_total)
    down_sum = sum_outer(grid, down_total)
    grad_residual, grad_attn_bf, res_sums, attn_sums = row_call(
        middle_rows,
        "middle_rows",
        [clip_column, residual, ffn_in_part, ffn_in_moved, upstream, attn_part, attn_moved],
        [own_tanhs[0], own_scales[1], gains],
        [f32, bf16],
        2,
    )
    grad_combined = dot(grad_attn_bf[:, :half_width], out_own) + dot(
        grad_attn_bf[:, half_width:], out_other
    )
    grad_attended_bf = grad_combined.astype(bf16)
    grad_long_bf = grad_attended_bf[:LONG_DEV]
    grad_long_q, *long_parts = attend_call(
        "attend_long_back", long_clip, long_seen, long_query, long_pairs, long_pairs, own_width,
        (grad_long_bf, long_out, long_lse), bf16,
    )
    long_terms = jnp.concatenate(long_parts, axis=1)
    long_kept, long_away = long_terms[: long_count // 2], long_terms[long_count // 2 :]
    out_kept = contract_rows(grad_attn_bf[:, :half_width], combined_bf).astype(bf16)
    out_away = contract_rows(grad_attn_bf[:, half_width:], combined_bf).astype(bf16)
    up_away = core_away(grid, up_kept, up_core)
    (
        grad_combined, grad_attended_bf, gate_moved, up_core, up_away, long_kept, long_away, out_kept,
        out_away, grad_long_q,
    ) = fence(
        grad_combined, grad_attended_bf, gate_moved, up_core, up_away, long_kept, long_away, out_kept,
        out_away, grad_long_q,
    )

    up_moved = swap_inner(grid, up_away)
    long_core = grid.send(long_away, core=1)
    out_core = grid.send(out_away, core=1)
    gate_total = inner_total(grid, gate_kept, gate_core, gate_moved)
    grad_combined, gate_total = fence(grad_combined, gate_total)
    gate_sum = sum_outer(grid, gate_total)
    grad_cross_bf = (gate_tanh * grad_combined).astype(bf16)
    own_gate_grad = jnp.sum(
        jnp.sum(grad_combined * cross_out, axis=0).reshape(own_heads, HD), axis=1
    ) * (1.0 - jnp.tanh(own_gates) ** 2)
    grad_query, grad_text_key, grad_text_value = attend_call(
        "attend_cross_back", clip_column, cross_seen, query_bf, text_key_bf, text_value_bf, 0,
        (grad_cross_bf, cross_out, cross_lse),
    )
    grad_tkey, text_gain_grad = head_call(
        norm_heads_back, "norm_text_back", text_raw, 0, text_gain, text_turns, (grad_text_key,)
    )
    grad_tval = grad_text_value.astype(bf16)
    tkey_kept = contract_rows(feats[:, :half_text], grad_tkey).astype(bf16)
    tkey_away = contract_rows(feats[:, half_text:], grad_tkey).astype(bf16)
    long_away = core_away(grid, long_kept, long_core)
    out_away = core_away(grid, out_kept, out_core)
    (
        gate_sum, down_sum, up_moved, long_core, long_away, out_core, out_away, grad_query, grad_tkey,
        grad_tval, tkey_kept, tkey_away, grad_attended_bf,
    ) = fence(
        gate_sum, down_sum, up_moved, long_core, long_away, out_core, out_away, grad_query, grad_tkey,
        grad_tval, tkey_kept, tkey_away, grad_attended_bf,
    )

    long_moved = swap_inner(grid, long_away)
    out_moved = swap_inner(grid, out_away)
    tkey_core = grid.send(tkey_away, core=1)
    down_grad = down_sum.astype(f32)
    gate_grad = gate_sum.astype(f32)
    up_total = inner_total(grid, up_kept, up_core, up_moved)
    grad_attended_bf, up_total = fence(grad_attended_bf, up_total)
    up_sum = sum_outer(grid, up_total)
    grad_short_bf = grad_attended_bf[LONG_DEV:]
    grad_short_q, grad_short_k, grad_short_v = attend_call(
        "attend_short_back", short_clip, short_seen, short_query, short_key, short_value, 0,
        (grad_short_bf, short_out, short_lse),
    )
    tval_kept = contract_rows(feats[:, :half_text], grad_tval).astype(bf16)
    tval_away = contract_rows(feats[:, half_text:], grad_tval).astype(bf16)
    null_flags = jnp.concatenate([own_null, null_mask[clip_total - 1 :] == 1]).astype(f32)
    row_ids = jnp.arange(text_rows, dtype=jnp.int32)
    null_chosen = jnp.where(
        row_ids[None, :] % TXT_LEN == jnp.arange(TXT_LEN, dtype=jnp.int32)[:, None],
        jnp.repeat(null_flags, TXT_LEN)[None, :],
        0.0,
    ).astype(bf16)
    null_rows = jnp.concatenate(
        [dot(null_chosen, grad_tkey), dot(null_chosen, grad_tval)], axis=1
    ).astype(bf16)
    tkey_away = core_away(grid, tkey_kept, tkey_core)
    (
        up_sum, long_moved, out_moved, tkey_core, tkey_away, tval_kept, tval_away, grad_short_q,
        grad_short_k, grad_short_v, null_rows,
    ) = fence(
        up_sum, long_moved, out_moved, tkey_core, tkey_away, tval_kept, tval_away, grad_short_q,
        grad_short_k, grad_short_v, null_rows,
    )

    tkey_moved = swap_inner(grid, tkey_away)
    tval_core = grid.send(tval_away, core=1)
    null_moved = pair_sum(grid, null_rows, 1)
    up_grad = up_sum.astype(f32)
    both_total = join_sums(
        grid,
        [long_kept, long_core] + long_moved,
        [out_kept, out_core] + out_moved,
        LONG_DEV,
        depth,
    )
    both_sum = sum_outer(grid, both_total)
    grad_query_raw, query_gain_grad = head_call(
        norm_heads_back, "norm_queries_back", projected, 0, query_gain, turns,
        (grad_query, jnp.concatenate([grad_long_q, grad_short_q], axis=0)),
    )
    tval_away = core_away(grid, tval_kept, tval_core)
    (
        both_sum, tkey_moved, tval_core, tval_away, null_moved, grad_query_raw, grad_short_k,
        grad_short_v, query_gain_grad,
    ) = fence(
        both_sum, tkey_moved, tval_core, tval_away, null_moved, grad_query_raw, grad_short_k,
        grad_short_v, query_gain_grad,
    )

    tval_moved = swap_inner(grid, tval_away)
    null_rows = null_rows + null_moved
    null_moved = pair_sum(grid, null_rows, 2)
    out_grad = both_sum[2 * LONG_DEV :].astype(f32)
    tkey_total = inner_total(grid, tkey_kept, tkey_core, tkey_moved)
    both_sum, tkey_total = fence(both_sum, tkey_total)
    tkey_sum = sum_outer(grid, tkey_total)
    own_terms = both_sum[: 2 * LONG_DEV].astype(f32)
    grad_key = jnp.concatenate([own_terms[:LONG_DEV], grad_short_k], axis=0)
    grad_value = jnp.concatenate([own_terms[LONG_DEV:], grad_short_v], axis=0)
    grad_key_raw, key_gain_grad = head_call(
        norm_heads_back, "norm_keys_back", projected, 1, key_gain, turns, (grad_key,)
    )
    grad_proj_bf = jnp.concatenate(
        [grad_query_raw, grad_key_raw, grad_value.astype(bf16)], axis=1
    )
    normed_part = rounded(
        jnp.concatenate(
            [contract_cols(grad_proj_bf, qkv_own), contract_cols(grad_proj_bf, qkv_other)], axis=1
        )
    ).astype(bf16)
    qkv_kept = contract_rows(normed_in[:, :half_width], grad_proj_bf).astype(bf16)
    qkv_away = contract_rows(normed_in[:, half_width:], grad_proj_bf).astype(bf16)
    first_rows = token_count // 2
    moved_first = swap_txt(normed_part[:first_rows])
    moved_last = swap_txt(normed_part[first_rows:])
    qkv_core = grid.send(qkv_away, core=1)
    qkv_away = core_away(grid, qkv_kept, qkv_core)
    (
        tkey_sum, tval_moved, null_moved, moved_first, qkv_kept, qkv_core, qkv_away, grad_residual,
    ) = fence(
        tkey_sum, tval_moved, null_moved, moved_first, qkv_kept, qkv_core, qkv_away, grad_residual,
    )

    qkv_moved = swap_inner(grid, qkv_away)
    null_rows = null_rows + null_moved
    tval_total = inner_total(grid, tval_kept, tval_core, tval_moved)
    tval_total, null_rows, moved_first, grad_residual = fence(
        tval_total, null_rows, moved_first, grad_residual
    )
    tval_sum = sum_outer(grid, tval_total)
    null_rows = null_rows + pair_sum(grid, null_rows, 4)
    null_moved = pair_sum(grid, null_rows, 8)
    normed_moved = jnp.concatenate([moved_first, moved_last], axis=0)
    video_high, video_low, hidden_sums = row_call(
        last_rows,
        "last_rows",
        [clip_column, hidden, normed_part, normed_moved, grad_residual],
        [own_scales[0], gains],
        [bf16, bf16],
        1,
    )
    hidden_sums, tval_sum, qkv_moved, null_rows, null_moved = fence(
        hidden_sums, tval_sum, qkv_moved, null_rows, null_moved
    )

    text_grad = jnp.stack([tkey_sum.astype(f32), tval_sum.astype(f32)], axis=1)
    qkv_total = inner_total(grid, qkv_kept, qkv_core, qkv_moved)
    hidden_sums, qkv_total = fence(hidden_sums, qkv_total)
    qkv_sum = sum_outer(grid, qkv_total)

    grad_mod = jnp.stack(
        [
            hidden_sums * gains[0],
            attn_sums * gains[1] * (1.0 - own_tanhs[0] * own_tanhs[0]),
            res_sums * gains[2],
            ffn_sums * gains[3] * (1.0 - own_tanhs[1] * own_tanhs[1]),
        ],
        axis=1,
    ).reshape(-1, model_width)
    gain_rows = jnp.stack(
        [
            jnp.sum(hidden_sums * own_scales[0], axis=0),
            jnp.sum(attn_sums * own_tanhs[0], axis=0),
            jnp.sum(res_sums * own_scales[1], axis=0),
            jnp.sum(ffn_sums * own_tanhs[1], axis=0),
        ],
        axis=0,
    )
    rows = contract_cols(
        jnp.concatenate(split_three(jnp.concatenate([grad_mod, gain_rows], axis=0)), axis=0),
        one_hot,
    )
    row_count = rows.shape[0] // 3
    rows = rows[:row_count] + rows[row_count : 2 * row_count] + rows[2 * row_count :]
    gain_rows = rows[-4:]
    own_grad_mod = rows[:-4].reshape(short_clips + 1, 4 * model_width)
    column_count = mod_part.shape[1]
    mod_blocks = lax.dynamic_index_in_dim(
        own_grad_mod.reshape(short_clips + 1, seq_count, 2, column_count),
        txt_index,
        2,
        keepdims=False,
    )
    mod_blocks = turn_seq(grid, jnp.transpose(mod_blocks, (1, 0, 2)))
    null_rows = sum_seq(grid, null_rows + null_moved, 16)
    null_part = jnp.concatenate(
        [
            contract_cols(null_rows[:, :own_width], key_piece)
            + contract_cols(null_rows[:, own_width:], value_piece)
            for key_piece, value_piece in zip(tkey_pieces, tval_pieces)
        ],
        axis=1,
    )
    null_part = rounded(null_part).astype(bf16)
    null_moved = swap_txt(null_part)
    video_grad = contract_cols(video_high, one_hot) + contract_cols(video_low, one_hot)
    slice_grad_mod = jnp.concatenate(
        [
            mod_blocks[:, :short_clips].reshape(clip_total - 1, column_count),
            jnp.sum(mod_blocks[:, short_clips], axis=0, keepdims=True),
        ],
        axis=0,
    )
    ada_weight_grad = lax.dot_general(
        shifted.astype(f32), slice_grad_mod, (((0,), (0,)), ((), ())), precision=highest
    )
    ada_bias_grad = jnp.sum(slice_grad_mod, axis=0)
    grad_shifted = lax.dot_general(
        slice_grad_mod, ada_weight.astype(f32), (((1,), (1,)), ((), ())), precision=highest
    )
    cond_value = condition.astype(f32)
    cond_sigmoid = jax.nn.sigmoid(cond_value)
    cond_part = grad_shifted * cond_sigmoid * (1.0 + cond_value * (1.0 - cond_sigmoid))

    head_rows = [
        lax.dynamic_update_slice(jnp.zeros((1, model_width), f32), rows, (0, head_start * HD))
        for rows in (query_gain_grad, key_gain_grad, text_gain_grad)
    ]
    gains_term = jnp.concatenate([jnp.where(first_half, gain_rows, 0.0)] + head_rows, axis=0)
    gates_term = lax.dynamic_update_slice_in_dim(jnp.zeros((H,), f32), own_gate_grad, head_start, 0)
    cond_count, gains_count = cond_part.size, gains_term.size
    packed = jnp.concatenate([cond_part.reshape(-1), gains_term.reshape(-1), gates_term])
    packed = jnp.pad(packed, (0, -packed.shape[0] % 1024)).reshape(-1, 1024)
    packed = packed + pair_sum(grid, packed, 1)
    packed = packed + pair_sum(grid, packed, 2)
    packed, qkv_sum = fence(packed, qkv_sum)
    packed = packed + pair_sum(grid, packed, 4)
    packed, null_moved = fence(packed, null_moved)
    null_grad = reorder_columns(
        null_part.astype(f32) + null_moved.astype(f32), owners, False
    )
    qkv_grad = qkv_sum.astype(f32).reshape(depth, 3, own_width)
    packed = sum_seq(grid, packed, 8)
    packed = (packed + swap_txt(packed)).reshape(-1)
    condition_grad = packed[:cond_count].reshape(cond_part.shape)
    norm_gains_grad = packed[cond_count : cond_count + gains_count].reshape(gains_term.shape)
    head_gates_grad = packed[cond_count + gains_count : cond_count + gains_count + H]
    return (
        block_out,
        video_grad,
        condition_grad,
        qkv_grad,
        out_grad,
        gate_grad,
        up_grad,
        down_grad,
        text_grad,
        ada_weight_grad,
        ada_bias_grad,
        null_grad,
        norm_gains_grad,
        head_gates_grad,
    )


def solution(mesh):
    placed = (
        P("seq", None),
        P("seq", None),
        P(),
        P("seq", "txt", None),
        P("txt", None),
        P("txt", None),
        P("seq", None, "txt"),
        P("seq", "txt"),
        P("seq", "txt"),
        P("seq", "txt"),
        P("seq", "txt"),
        P("seq", None, "txt"),
        P(None, ("seq", "txt")),
        P(("seq", "txt")),
        P(),
        P(),
        P("seq", None),
        P(),
        P(),
    )
    return jax.shard_map(
        local,
        mesh=mesh,
        in_specs=placed,
        out_specs=(
            P("seq", None),
            P("seq", None),
            P(),
            P("seq", None, "txt"),
            P("seq", "txt"),
            P("seq", "txt"),
            P("seq", "txt"),
            P("seq", "txt"),
            P("seq", None, "txt"),
            P(None, ("seq", "txt")),
            P(("seq", "txt")),
            P(),
            P(),
            P(),
        ),
        check_vma=False,
    )
```

```python
import functools
import math

import jax
import jax.numpy as jnp
from jax import lax
from jax.experimental import pallas as pl
from jax.experimental.pallas import tpu as pltpu
from jax.sharding import PartitionSpec as P

H = 24
HD = 64
TXT_LEN = 64
LONG_DEV = 64

epsilon = 1e-05
negative = -1e30
highest = lax.Precision.HIGHEST
bf16 = jnp.bfloat16
f32 = jnp.float32


def layout(lengths_row, seq_index, long_rows, short_rows):
    clip_count = lengths_row.shape[0]
    clip_ends = jnp.cumsum(lengths_row)
    clip_starts = clip_ends - lengths_row
    row_ids = jnp.arange(short_rows, dtype=jnp.int32)
    local_clip = jnp.sum(
        (row_ids[:, None] >= clip_ends[None, : clip_count - 1]).astype(jnp.int32), axis=1
    )
    chosen = local_clip[:, None] == jnp.arange(clip_count, dtype=jnp.int32)[None, :]
    clip_begin = jnp.sum(jnp.where(chosen, clip_starts[None, :], 0), axis=1)
    clip_local = jnp.concatenate([jnp.full((long_rows,), clip_count, jnp.int32), local_clip])
    long_place = seq_index * long_rows + jnp.arange(long_rows, dtype=jnp.int32)
    position = jnp.concatenate([long_place, row_ids - clip_begin])
    return (clip_local, position)


def rms_parts(values):
    inverse = lax.rsqrt(jnp.mean(values * values, axis=-1, keepdims=True) + epsilon)
    return (values * inverse, inverse)


def rms_back(grad_hat, normed, inverse):
    return inverse * (grad_hat - normed * jnp.mean(grad_hat * normed, axis=-1, keepdims=True))


def dot(left_side, right_side):
    return jnp.dot(left_side, right_side, preferred_element_type=f32)


def dot_pieces(left_side, pieces):
    depth = pieces[0].shape[0]
    total = 0.0
    for place, piece in enumerate(pieces):
        total = total + dot(left_side[:, place * depth : (place + 1) * depth], piece)
    return total


def contract_rows(left_side, right_side):
    return lax.dot_general(
        left_side, right_side, (((0,), (0,)), ((), ())), preferred_element_type=f32
    )


def contract_cols(left_side, right_side):
    return lax.dot_general(
        left_side, right_side, (((1,), (1,)), ((), ())), preferred_element_type=f32
    )


def swap_txt(values):
    return lax.ppermute(values, "txt", [(0, 1), (1, 0)])


def rounded(values):
    return lax.reduce_precision(values, exponent_bits=8, mantissa_bits=7)


def fence(*values):
    return lax.optimization_barrier(values)


class Grid:
    def __init__(self):
        self.count = lax.axis_size("seq")
        self.outer_count = 4
        self.inner_count = self.count // 8
        self.index = lax.axis_index("seq")
        self.core = self.index % 2
        self.inner = (self.index // 2) % self.inner_count
        self.outer = self.index // (2 * self.inner_count)

    def send(self, values, outer=0, inner=0, core=0):
        pairs = []
        for index in range(self.count):
            to_core = (index + core) % 2
            to_inner = (index // 2 + inner) % self.inner_count
            to_outer = (index // (2 * self.inner_count) + outer) % self.outer_count
            pairs.append((index, (to_outer * self.inner_count + to_inner) * 2 + to_core))
        return lax.ppermute(values, "seq", pairs)

    def lines(self):
        step = 2 * self.inner_count
        return [[first + step * k for k in range(self.outer_count)] for first in range(step)]

    def owners(self):
        place = jnp.arange(self.count, dtype=jnp.int32)
        outer = place % self.outer_count
        inner = (self.inner - (place // self.outer_count) % self.inner_count) % self.inner_count
        core = (self.core + place // (self.outer_count * self.inner_count)) % 2
        return (outer * self.inner_count + inner) * 2 + core


def gather_outer(grid, block):
    return lax.all_gather(block, "seq", axis=0, tiled=True, axis_index_groups=grid.lines())


def send_inner(grid, near):
    return [grid.send(near, inner=step) for step in range(1, grid.inner_count)]


def send_core(grid, pieces):
    return [grid.send(piece, core=1) for piece in pieces]


def stack(pieces):
    return jnp.concatenate(pieces, axis=0) if len(pieces) > 1 else pieces[0]


def add_blocks(*refs):
    *sources, target = refs
    total = sources[0][...].astype(f32)
    for source in sources[1:]:
        total = total + source[...].astype(f32)
    target[...] = total.astype(target.dtype)


def add_rows(arrays, starts, rows):
    cols = arrays[0].shape[1]
    block = 256 if rows % 256 == 0 else 128 if rows % 128 == 0 else rows

    def from_row(start):
        return pl.BlockSpec((block, cols), lambda i: (start // block + i, 0))

    return pl.pallas_call(
        add_blocks,
        grid=(rows // block,),
        in_specs=[from_row(start) for start in starts],
        out_specs=from_row(0),
        out_shape=jax.ShapeDtypeStruct((rows, cols), bf16),
        cost_estimate=pl.CostEstimate(flops=1, bytes_accessed=1, transcendentals=0),
        compiler_params=pltpu.CompilerParams(vmem_limit_bytes=48 * 1024 * 1024),
        name="add_rows",
    )(*arrays)


def join_blocks(*refs):
    *sources, target = refs
    half = len(sources) // 2
    totals = []
    for part in (sources[:half], sources[half:]):
        total = part[0][...].astype(f32)
        for source in part[1:]:
            total = total + source[...].astype(f32)
        totals.append(total.astype(bf16))
    rows, width = totals[0].shape[0], totals[1].shape[1]
    target[0, :rows, :] = totals[0][:, :width]
    target[0, rows : 2 * rows, :] = totals[0][:, width:]
    target[0, 2 * rows :, :] = totals[1]


def join_sums(grid, long_parts, out_parts, long_rows, out_rows):
    width = out_parts[0].shape[1]
    rows = 2 * long_rows + out_rows
    long_spec = pl.BlockSpec((long_rows, 2 * width), lambda i: (i, 0))
    out_spec = pl.BlockSpec((out_rows, width), lambda i: (i, 0))
    joined = pl.pallas_call(
        join_blocks,
        grid=(grid.outer_count,),
        in_specs=[long_spec] * len(long_parts) + [out_spec] * len(out_parts),
        out_specs=pl.BlockSpec((1, rows, width), lambda i: (i, 0, 0)),
        out_shape=jax.ShapeDtypeStruct((grid.outer_count, rows, width), bf16),
        cost_estimate=pl.CostEstimate(flops=1, bytes_accessed=1, transcendentals=0),
        name="join_sums",
    )(*long_parts, *out_parts)
    return joined.reshape(grid.outer_count * rows, width)


def core_away(grid, kept, moved):
    rows = kept.shape[0] // grid.inner_count
    return [
        add_rows([kept, moved], [step * rows] * 2, rows) for step in range(1, grid.inner_count)
    ]


def inner_total(grid, kept, moved, arrived):
    rows = kept.shape[0] // grid.inner_count
    return add_rows([kept, moved] + arrived, [0] * (2 + len(arrived)), rows)


def swap_inner(grid, away):
    return [grid.send(part, inner=-step) for step, part in enumerate(away, 1)]


def sum_outer(grid, total):
    return lax.psum_scatter(
        total, "seq", scatter_dimension=0, tiled=True, axis_index_groups=grid.lines()
    )


def pair_sum(grid, values, bit):
    pairs = [(index, index ^ bit) for index in range(grid.count)]
    return lax.ppermute(values, "seq", pairs)


def turn_stage(values, axis, size, own, send):
    moved = [lax.dynamic_index_in_dim(values, own, axis, keepdims=False)]
    for step in range(1, size):
        piece = lax.dynamic_index_in_dim(values, (own + step) % size, axis, keepdims=False)
        moved.append(send(piece, step))
    stacked = jnp.stack(moved, axis=axis)
    order = (own - jnp.arange(size, dtype=jnp.int32)) % size
    return jnp.take(stacked, order, axis=axis)


def turn_seq(grid, values):
    rest = values.shape[1:]
    values = values.reshape((grid.outer_count, grid.inner_count, 2) + rest)
    values = turn_stage(
        values, 0, grid.outer_count, grid.outer, lambda v, k: grid.send(v, outer=k)
    )
    values = turn_stage(
        values, 1, grid.inner_count, grid.inner, lambda v, k: grid.send(v, inner=k)
    )
    values = turn_stage(values, 2, 2, grid.core, lambda v, k: grid.send(v, core=k))
    return values.reshape((grid.count,) + rest)


def sum_seq(grid, values, bit):
    while bit < grid.count:
        values = values + pair_sum(grid, values, bit)
        bit *= 2
    return values


def copy_blocks(to_order, count, order_ref, source_ref, target_ref):
    width = source_ref.shape[1] // count
    for block in range(count):
        moved = pl.ds(pl.multiple_of(order_ref[block] * width, width), width)
        plain = pl.ds(block * width, width)
        if to_order:
            target_ref[:, plain] = source_ref[:, moved]
        else:
            target_ref[:, moved] = source_ref[:, plain]


def reorder_columns(values, order, to_order):
    rows, cols = values.shape
    count = order.shape[0]
    width = cols // count
    if width % 128:
        taken = order if to_order else jnp.argsort(order)
        return jnp.take(values.reshape(rows, count, width), taken, axis=1).reshape(rows, cols)
    return pl.pallas_call(
        functools.partial(copy_blocks, to_order, count),
        out_shape=jax.ShapeDtypeStruct(values.shape, values.dtype),
        in_specs=[
            pl.BlockSpec(memory_space=pltpu.SMEM),
            pl.BlockSpec(memory_space=pltpu.VMEM),
        ],
        out_specs=pl.BlockSpec(memory_space=pltpu.VMEM),
        name="reorder_columns",
    )(order, values)


def split_three(values):
    high = rounded(values)
    rest = values - high
    middle = rounded(rest)
    return high.astype(bf16), middle.astype(bf16), (rest - middle).astype(bf16)


def exact_dot(values, one_hot):
    rows = values.shape[0]
    parts = dot(jnp.concatenate(split_three(values), axis=0), one_hot)
    return parts[:rows] + parts[rows : 2 * rows] + parts[2 * rows :]


def choose(clip, rows):
    chosen = rows[-1:]
    for index in range(rows.shape[0] - 1):
        chosen = jnp.where(clip == index, rows[index : index + 1], chosen)
    return chosen


def add_clip_sums(clip, values, sums_ref):
    @pl.when(pl.program_id(0) == 0)
    def _():
        sums_ref[...] = jnp.zeros_like(sums_ref)

    for index in range(sums_ref.shape[0]):
        part = jnp.sum(jnp.where(clip == index, values, 0.0), axis=0, keepdims=True)
        sums_ref[index : index + 1, :] += part


def add_pair(own_ref, moved_ref):
    return own_ref[...].astype(f32) + moved_ref[...].astype(f32)


def enter_rows(clip_ref, hidden_ref, part_ref, moved_ref, tanh_ref, scale_ref, gains_ref, res_ref, in_ref):
    clip = clip_ref[...]
    attn_hat, _ = rms_parts(add_pair(part_ref, moved_ref))
    tanh_tok = choose(clip, tanh_ref[...])
    residual = hidden_ref[...].astype(f32) + tanh_tok * attn_hat * gains_ref[1:2]
    res_hat, _ = rms_parts(residual)
    res_ref[...] = residual
    in_ref[...] = (res_hat * gains_ref[2:3] * choose(clip, scale_ref[...])).astype(bf16)


def leave_rows(clip_ref, res_ref, part_ref, moved_ref, up_ref, tanh_ref, gains_ref, out_ref, grad_ref, sums_ref):
    clip = clip_ref[...]
    hat, inverse = rms_parts(add_pair(part_ref, moved_ref))
    upstream = up_ref[...].astype(f32)
    tanh_tok = choose(clip, tanh_ref[...])
    out_ref[...] = (res_ref[...] + tanh_tok * hat * gains_ref[3:4]).astype(bf16)
    grad_ref[...] = rms_back(upstream * tanh_tok * gains_ref[3:4], hat, inverse).astype(bf16)
    add_clip_sums(clip, upstream * hat, sums_ref)


def middle_rows(
    clip_ref, res_ref, grad_part_ref, grad_moved_ref, up_ref, part_ref, moved_ref, tanh_ref,
    scale_ref, gains_ref, grad_res_ref, grad_attn_ref, res_sums_ref, attn_sums_ref,
):
    clip = clip_ref[...]
    grad = add_pair(grad_part_ref, grad_moved_ref)
    hat, inverse = rms_parts(res_ref[...])
    add_clip_sums(clip, grad * hat, res_sums_ref)
    grad_hat = grad * gains_ref[2:3] * choose(clip, scale_ref[...])
    grad_res = up_ref[...].astype(f32) + rms_back(grad_hat, hat, inverse)
    grad_res_ref[...] = grad_res
    hat, inverse = rms_parts(add_pair(part_ref, moved_ref))
    add_clip_sums(clip, grad_res * hat, attn_sums_ref)
    grad_hat = grad_res * gains_ref[1:2] * choose(clip, tanh_ref[...])
    grad_attn_ref[...] = rms_back(grad_hat, hat, inverse).astype(bf16)


def last_rows(
    clip_ref, hidden_ref, part_ref, moved_ref, grad_res_ref, scale_ref, gains_ref, high_ref, low_ref,
    sums_ref,
):
    clip = clip_ref[...]
    grad = add_pair(part_ref, moved_ref)
    hat, inverse = rms_parts(hidden_ref[...].astype(f32))
    add_clip_sums(clip, grad * hat, sums_ref)
    grad_hat = grad * gains_ref[0:1] * choose(clip, scale_ref[...])
    total = grad_res_ref[...] + rms_back(grad_hat, hat, inverse)
    high = total.astype(bf16)
    high_ref[...] = high
    low_ref[...] = (total - high.astype(f32)).astype(bf16)


def row_call(body, name, arrays, tables, outs, sums):
    count, width = arrays[1].shape
    rows = count // 4

    def by_rows(array):
        return pl.BlockSpec((rows, array.shape[1]), lambda i: (i, 0))

    def whole(array):
        return pl.BlockSpec(array.shape, lambda i: (0, 0))

    out_shapes = [jax.ShapeDtypeStruct((count, width), kind) for kind in outs]
    sum_shapes = [jax.ShapeDtypeStruct((tables[0].shape[0], width), f32)] * sums
    return pl.pallas_call(
        body,
        grid=(4,),
        in_specs=[by_rows(array) for array in arrays] + [whole(table) for table in tables],
        out_specs=[by_rows(shape) for shape in out_shapes] + [whole(shape) for shape in sum_shapes],
        out_shape=out_shapes + sum_shapes,
        cost_estimate=pl.CostEstimate(flops=1, bytes_accessed=1, transcendentals=0),
        compiler_params=pltpu.CompilerParams(vmem_limit_bytes=48 * 1024 * 1024),
        name=name,
    )(*arrays, *tables)


def head_means(values):
    first = lax.broadcasted_iota(jnp.int32, values.shape, 1) < HD
    front = jnp.sum(jnp.where(first, values, 0.0), axis=1, keepdims=True)
    back = jnp.sum(jnp.where(first, 0.0, values), axis=1, keepdims=True)
    return jnp.where(first, front, back) * (1.0 / HD)


def turn_lanes(values, cosine, sine):
    lane = lax.broadcasted_iota(jnp.int32, values.shape, 1) % HD
    ahead = pltpu.roll(values, 2 * HD - HD // 2, 1)
    behind = pltpu.roll(values, HD // 2, 1)
    return values * cosine + jnp.where(lane < HD // 2, -ahead, behind) * sine


def norm_heads(values_ref, gain_ref, cos_ref, sin_ref, out_ref):
    cosine, sine = cos_ref[...], sin_ref[...]
    for start in range(0, out_ref.shape[1], 2 * HD):
        part = slice(start, start + 2 * HD)
        values = values_ref[:, part]
        hat = values * lax.rsqrt(head_means(values * values) + epsilon)
        out_ref[:, part] = turn_lanes(hat * gain_ref[:, part], cosine, sine).astype(bf16)


def norm_heads_back(*refs):
    values_ref, gain_ref, cos_ref, sin_ref, *grad_refs, out_ref, sums_ref = refs
    cosine, sine = cos_ref[...], sin_ref[...]

    @pl.when(pl.program_id(0) == 0)
    def _():
        sums_ref[...] = jnp.zeros_like(sums_ref)

    for start in range(0, out_ref.shape[1], 2 * HD):
        part = slice(start, start + 2 * HD)
        values = values_ref[:, part]
        inverse = lax.rsqrt(head_means(values * values) + epsilon)
        hat = values * inverse
        grad = grad_refs[0][:, part]
        for grad_ref in grad_refs[1:]:
            grad = grad + grad_ref[:, part]
        grad = turn_lanes(grad, cosine, -sine)
        sums_ref[:, part] += jnp.sum(grad * hat, axis=0, keepdims=True)
        grad = grad * gain_ref[:, part]
        out_ref[:, part] = (inverse * (grad - hat * head_means(grad * hat))).astype(bf16)


def head_call(body, name, values, column, gain, turns, grads=()):
    count, width = turns[0].shape[0], gain.shape[1]
    rows = count // 4
    by_rows = pl.BlockSpec((rows, width), lambda i: (i, 0))
    whole = pl.BlockSpec((1, width), lambda i: (0, 0))
    turn = pl.BlockSpec((rows, 2 * HD), lambda i: (i, 0))
    out_shape = [jax.ShapeDtypeStruct((count, width), bf16)]
    out_specs = [by_rows]
    if grads:
        out_shape.append(jax.ShapeDtypeStruct((1, width), f32))
        out_specs.append(whole)
    results = pl.pallas_call(
        body,
        grid=(4,),
        in_specs=[pl.BlockSpec((rows, width), lambda i: (i, column)), whole, turn, turn]
        + [by_rows] * len(grads),
        out_specs=out_specs,
        out_shape=out_shape,
        cost_estimate=pl.CostEstimate(flops=1, bytes_accessed=1, transcendentals=0),
        compiler_params=pltpu.CompilerParams(vmem_limit_bytes=48 * 1024 * 1024),
        name=name,
    )(values, gain, *turns, *grads)
    return results if grads else results[0]


def attend_heads(clip_ref, key_clip_ref, query_ref, key_ref, value_ref, out_ref, total_ref):
    visible = clip_ref[...] == key_clip_ref[...]
    for start in range(0, 2 * HD, HD):
        head = slice(start, start + HD)
        scores = contract_cols(query_ref[:, head], key_ref[:, head]) * HD ** (-0.5)
        scores = jnp.where(visible, scores, negative)
        peak = jnp.max(scores, axis=1, keepdims=True)
        exponent = jnp.exp(scores - peak)
        total = jnp.sum(exponent, axis=1, keepdims=True)
        out_ref[:, head] = dot((exponent / total).astype(bf16), value_ref[:, head])
        total_ref[:, head] = jnp.broadcast_to(peak + jnp.log(total), (total_ref.shape[0], HD))


def attend_heads_back(
    clip_ref, key_clip_ref, query_ref, key_ref, value_ref, grad_ref, out_ref, total_ref,
    grad_query_ref, grad_key_ref, grad_value_ref,
):
    visible = clip_ref[...] == key_clip_ref[...]
    for start in range(0, 2 * HD, HD):
        head = slice(start, start + HD)
        query, key = query_ref[:, head], key_ref[:, head]
        grad = grad_ref[:, head]
        scores = contract_cols(query, key) * HD ** (-0.5)
        weights = jnp.where(visible, jnp.exp(scores - total_ref[:, start : start + 1]), 0.0)
        delta = jnp.sum(grad.astype(f32) * out_ref[:, head], axis=1, keepdims=True)
        grad_scores = weights * (contract_cols(grad, value_ref[:, head]) - delta)
        grad_scores = grad_scores.astype(bf16)
        grad_query_ref[:, head] = dot(grad_scores, key) * HD ** (-0.5)
        grad_key = contract_rows(grad_scores, query) * HD ** (-0.5)
        grad_key_ref[:, head] = grad_key.astype(grad_key_ref.dtype)
        grad_value = contract_rows(weights.astype(bf16), grad)
        grad_value_ref[:, head] = grad_value.astype(grad_value_ref.dtype)


def attend_call(name, clips, key_clips, query, key, value, value_column=0, back=(), kind=f32):
    count, keys, width = query.shape[0], key.shape[0], query.shape[1]
    first = value_column // (2 * HD)
    queries = pl.BlockSpec((count, 2 * HD), lambda i: (0, i))
    seen = pl.BlockSpec((keys, 2 * HD), lambda i: (0, i))
    whole = [pl.BlockSpec(array.shape, lambda i: (0, 0)) for array in (clips, key_clips)]
    out_shape = [jax.ShapeDtypeStruct((count, width), f32)]
    if back:
        out_shape += [jax.ShapeDtypeStruct((keys, width), kind)] * 2
        out_specs = [queries, seen, seen]
    else:
        out_shape += out_shape
        out_specs = [queries, queries]
    return pl.pallas_call(
        attend_heads_back if back else attend_heads,
        grid=(width // (2 * HD),),
        in_specs=whole
        + [queries, seen, pl.BlockSpec((keys, 2 * HD), lambda i: (0, first + i))]
        + [queries] * len(back),
        out_specs=out_specs,
        out_shape=out_shape,
        cost_estimate=pl.CostEstimate(flops=1, bytes_accessed=1, transcendentals=0),
        compiler_params=pltpu.CompilerParams(vmem_limit_bytes=48 * 1024 * 1024),
        name=name,
    )(clips, key_clips, query, key, value, *back)


def local(
    video_tokens,
    cotangent,
    condition,
    captions,
    long_caption,
    null_embed,
    query_key_value,
    out_weight,
    gate_weight,
    up_weight,
    down_weight,
    text_weight,
    ada_weight,
    ada_bias,
    norm_gains,
    head_gates,
    clip_lengths,
    null_mask,
    text_lengths,
):
    grid = Grid()
    seq_index = grid.index
    seq_count = grid.count
    txt_index = lax.axis_index("txt")
    first_half = txt_index == 0
    token_count, model_width = video_tokens.shape
    depth = query_key_value.shape[0]
    text_depth, text_width = text_weight.shape[0], captions.shape[2]
    half_width = model_width // 2
    own_heads = query_key_value.shape[2] // HD
    own_width = own_heads * HD
    head_start = txt_index * own_heads
    clip_total = condition.shape[0]
    short_clips = clip_lengths.shape[1]
    clip_local, position = layout(clip_lengths[0], seq_index, LONG_DEV, token_count - LONG_DEV)
    owners = grid.owners()
    text_rows = (short_clips + 1) * TXT_LEN

    half_text = text_width // 2
    text_block = text_weight.reshape(text_depth, 2 * own_width)

    qkv_block, condition = fence(query_key_value.reshape(depth, 3 * own_width), condition)
    qkv_near = gather_outer(grid, qkv_block)
    shifted = jax.nn.silu(condition.astype(f32)).astype(bf16)
    mod_part = dot(shifted, ada_weight) + ada_bias
    short_part = mod_part[: clip_total - 1].reshape(seq_count, short_clips, mod_part.shape[1])
    long_part = jnp.broadcast_to(
        mod_part[clip_total - 1 :][None], (seq_count, 1, mod_part.shape[1])
    )
    own_part = turn_seq(grid, jnp.concatenate([short_part, long_part], axis=1))
    other_part = swap_txt(own_part)
    own_null = lax.dynamic_slice_in_dim(null_mask, seq_index * short_clips, short_clips, 0) == 1
    short_feats = jnp.where(own_null[:, None, None], null_embed[None], captions)
    long_feats = jnp.where(null_mask[clip_total - 1] == 1, null_embed, long_caption)
    own_feats = jnp.concatenate([short_feats, long_feats[None]], axis=0).reshape(-1, text_width)
    own_feats = reorder_columns(own_feats, owners, True)

    columns = jnp.arange(model_width, dtype=jnp.int32)
    column_order = jnp.repeat(owners, depth) * depth + columns % depth
    one_hot = (columns[:, None] == column_order[None, :]).astype(bf16)
    hidden = dot(video_tokens, one_hot).astype(bf16)
    hidden_hat, _ = rms_parts(hidden.astype(f32))
    clip_column = clip_local[:, None]
    tkey_block, tval_block = text_block[:, :own_width], text_block[:, own_width:]
    qkv_near, own_part, other_part, own_feats, tkey_block, tval_block, out_weight = fence(
        qkv_near, own_part, other_part, own_feats, tkey_block, tval_block, out_weight
    )

    qkv_y = send_inner(grid, qkv_near)
    qkv_near_core = send_core(grid, [qkv_near])
    tkey_near = gather_outer(grid, tkey_block)
    out_near = gather_outer(grid, out_weight)
    other_feats = swap_txt(own_feats)
    own_mod = jnp.stack(
        [jnp.where(first_half, own_part, other_part), jnp.where(first_half, other_part, own_part)],
        axis=1,
    )
    own_mod = jnp.transpose(own_mod, (2, 0, 1, 3)).reshape((short_clips + 1) * 4, model_width)
    rows = exact_dot(jnp.concatenate([own_mod, norm_gains[:4]], axis=0), one_hot)
    gains = rows[-4:]
    own_mod = rows[:-4].reshape(short_clips + 1, 4, model_width)
    own_scales = 1.0 + own_mod[:, 0], 1.0 + own_mod[:, 2]
    own_tanhs = jnp.tanh(own_mod[:, 1]), jnp.tanh(own_mod[:, 3])
    selector = clip_local[:, None] == jnp.arange(short_clips + 1, dtype=jnp.int32)[None, :]

    def per_token(rows):
        chosen = rows[short_clips:]
        for clip in range(short_clips):
            chosen = jnp.where(selector[:, clip : clip + 1], rows[clip : clip + 1], chosen)
        return chosen

    normed_in = (hidden_hat * gains[0] * per_token(own_scales[0])).astype(bf16)
    query_gain, key_gain, text_gain = [
        lax.dynamic_slice(norm_gains, (row, head_start * HD), (1, own_width)) for row in (4, 5, 6)
    ]
    frequency = jnp.exp(
        jnp.arange(HD // 2, dtype=f32) * (-math.log(10000.0) / (HD // 2))
    )
    angles = jnp.tile(position.astype(f32)[:, None] * frequency, (1, 4))
    turns = jnp.cos(angles), jnp.sin(angles)
    text_turns = jnp.ones((text_rows, 2 * HD), f32), jnp.zeros((text_rows, 2 * HD), f32)
    normed_in, other_feats, tkey_near, out_near, tval_block, qkv_near_core, qkv_y = fence(
        normed_in, other_feats, tkey_near, out_near, tval_block, qkv_near_core, qkv_y
    )

    tkey_y = send_inner(grid, tkey_near)
    tkey_near_core = send_core(grid, [tkey_near])
    out_near_core = send_core(grid, [out_near])
    tval_near = gather_outer(grid, tval_block)
    qkv_core, normed_in = fence(send_core(grid, qkv_y), normed_in)
    qkv_own, qkv_other = stack([qkv_near] + qkv_y), stack(qkv_near_core + qkv_core)
    projected = dot(normed_in[:, :half_width], qkv_own) + dot(normed_in[:, half_width:], qkv_other)
    query_bf = head_call(norm_heads, "norm_queries", projected, 0, query_gain, turns)
    key_bf = head_call(norm_heads, "norm_keys", projected, 1, key_gain, turns)
    value_bf = projected[:, 2 * own_width :].astype(bf16)
    long_block = jnp.concatenate([key_bf[:LONG_DEV], value_bf[:LONG_DEV]], axis=1)
    (
        query_bf, key_bf, value_bf, long_block, tkey_y, tkey_near_core, out_near, out_near_core,
        tval_near, gate_weight,
    ) = fence(
        query_bf, key_bf, value_bf, long_block, tkey_y, tkey_near_core, out_near, out_near_core,
        tval_near, gate_weight,
    )

    tail = long_block.size // gate_weight.shape[1]
    gate_near = gather_outer(
        grid, jnp.concatenate([gate_weight, long_block.reshape(tail, -1)], axis=0)
    )
    tval_y = send_inner(grid, tval_near)
    tval_near_core = send_core(grid, [tval_near])
    short_query = query_bf[LONG_DEV:]
    short_key = key_bf[LONG_DEV:]
    short_value = value_bf[LONG_DEV:]
    short_clip = clip_column[LONG_DEV:]
    short_seen = clip_local[LONG_DEV:][None, :]
    short_out, short_lse = attend_call(
        "attend_short", short_clip, short_seen, short_query, short_key, short_value
    )
    out_y = send_inner(grid, out_near)
    tkey_core = send_core(grid, tkey_y)
    feats = jnp.concatenate(
        [
            jnp.where(first_half, own_feats, other_feats).reshape(-1, TXT_LEN // 2, text_width),
            jnp.where(first_half, other_feats, own_feats).reshape(-1, TXT_LEN // 2, text_width),
        ],
        axis=1,
    ).reshape(text_rows, text_width)
    tval_y, tval_near_core, gate_near, tkey_core, out_y, up_weight, feats, short_out = fence(
        tval_y, tval_near_core, gate_near, tkey_core, out_y, up_weight, feats, short_out
    )

    gate_near = gate_near.reshape(grid.outer_count, depth + tail, -1)
    long_near = gate_near[:, depth:].reshape(-1, 2 * own_width)
    gate_near = gate_near[:, :depth].reshape(grid.outer_count * depth, -1)
    long_y = send_inner(grid, long_near)
    long_near_core = send_core(grid, [long_near])
    gate_y = send_inner(grid, gate_near)
    gate_near_core = send_core(grid, [gate_near])
    up_near = gather_outer(grid, up_weight)
    tval_core = send_core(grid, tval_y)
    long_core = send_core(grid, long_y)
    out_core = send_core(grid, out_y)
    tkey_pieces = [tkey_near] + tkey_y + tkey_near_core + tkey_core
    text_raw = dot_pieces(feats, tkey_pieces)
    text_key_bf = head_call(norm_heads, "norm_text", text_raw, 0, text_gain, text_turns)

    out_own, out_other = stack([out_near] + out_y), stack(out_near_core + out_core)
    long_pairs = stack([long_near] + long_y + long_near_core + long_core)
    long_count = long_pairs.shape[0]
    long_query = query_bf[:LONG_DEV]
    long_clip = clip_column[:LONG_DEV]
    long_seen = jnp.full((1, long_count), short_clips, jnp.int32)
    long_out, long_lse = attend_call(
        "attend_long", long_clip, long_seen, long_query, long_pairs, long_pairs, own_width
    )
    tval_pieces = [tval_near] + tval_y + tval_near_core + tval_core
    text_value_bf = dot_pieces(feats, tval_pieces).astype(bf16)
    key_clip = jnp.arange(text_rows, dtype=jnp.int32) // TXT_LEN
    key_place = jnp.arange(text_rows, dtype=jnp.int32) % TXT_LEN
    limits = jnp.concatenate(
        [
            lax.dynamic_slice_in_dim(text_lengths, seq_index * short_clips, short_clips, 0),
            text_lengths[clip_total - 1 :],
        ]
    )
    clip_match = key_clip[:, None] == jnp.arange(short_clips + 1, dtype=jnp.int32)[None, :]
    key_limit = jnp.sum(jnp.where(clip_match, limits[None, :], 0), axis=1)
    cross_seen = jnp.where(key_place < key_limit, key_clip, -1)[None, :]
    cross_out, cross_lse = attend_call(
        "attend_cross", clip_column, cross_seen, query_bf, text_key_bf, text_value_bf
    )
    attended = jnp.concatenate([long_out, short_out], axis=0)
    own_gates = lax.dynamic_slice_in_dim(head_gates, head_start, own_heads, 0)
    gate_tanh = jnp.repeat(jnp.tanh(own_gates), HD)[None, :]
    combined_bf = (attended + gate_tanh * cross_out).astype(bf16)
    attn_part = rounded(
        jnp.concatenate(
            [contract_cols(combined_bf, out_own), contract_cols(combined_bf, out_other)], axis=1
        )
    ).astype(bf16)
    attn_part, gate_y, gate_near_core, up_near, down_weight = fence(
        attn_part, gate_y, gate_near_core, up_near, down_weight
    )

    attn_moved = swap_txt(attn_part)
    up_y = send_inner(grid, up_near)
    up_near_core = send_core(grid, [up_near])
    down_near = gather_outer(grid, down_weight)
    gate_core = send_core(grid, gate_y)
    attn_moved, up_y, up_near_core, down_near, gate_core = fence(
        attn_moved, up_y, up_near_core, down_near, gate_core
    )

    down_y = send_inner(grid, down_near)
    down_near_core = send_core(grid, [down_near])
    up_core = send_core(grid, up_y)
    gate_own, gate_other = stack([gate_near] + gate_y), stack(gate_near_core + gate_core)
    residual, ffn_in_bf = row_call(
        enter_rows,
        "enter_rows",
        [clip_column, hidden, attn_part, attn_moved],
        [own_tanhs[0], own_scales[1], gains],
        [f32, bf16],
        0,
    )
    gate_value = dot(ffn_in_bf[:, :half_width], gate_own) + dot(
        ffn_in_bf[:, half_width:], gate_other
    )
    up_core, gate_value = fence(up_core, gate_value)
    up_own, up_other = stack([up_near] + up_y), stack(up_near_core + up_core)
    up_value = dot(ffn_in_bf[:, :half_width], up_own) + dot(ffn_in_bf[:, half_width:], up_other)
    sigmoid_gate = jax.nn.sigmoid(gate_value)
    silu_gate = gate_value * sigmoid_gate
    inner_bf = (silu_gate * up_value).astype(bf16)
    inner_bf, down_y, down_near_core = fence(inner_bf, down_y, down_near_core)

    down_core = send_core(grid, down_y)
    upstream = dot(cotangent, one_hot).astype(bf16)
    down_core, inner_bf, upstream = fence(down_core, inner_bf, upstream)
    down_own, down_other = stack([down_near] + down_y), stack(down_near_core + down_core)
    ffn_part = rounded(
        jnp.concatenate(
            [contract_cols(inner_bf, down_own), contract_cols(inner_bf, down_other)], axis=1
        )
    ).astype(bf16)
    (ffn_part,) = fence(ffn_part)

    ffn_moved = swap_txt(ffn_part)
    ffn_moved, ffn_part = fence(ffn_moved, ffn_part)

    block_out, grad_ffn_out, ffn_sums = row_call(
        leave_rows,
        "leave_rows",
        [clip_column, residual, ffn_part, ffn_moved, upstream],
        [own_tanhs[1], gains],
        [bf16, bf16],
        1,
    )
    down_kept = contract_rows(grad_ffn_out[:, :half_width], inner_bf).astype(bf16)
    down_away = contract_rows(grad_ffn_out[:, half_width:], inner_bf).astype(bf16)
    grad_ffn_out, down_away, down_kept = fence(grad_ffn_out, down_away, down_kept)

    down_core = grid.send(down_away, core=1)
    grad_inner = dot(grad_ffn_out[:, :half_width], down_own) + dot(
        grad_ffn_out[:, half_width:], down_other
    )
    silu_slope = sigmoid_gate * (1.0 + gate_value * (1.0 - sigmoid_gate))
    grad_gate_bf = (grad_inner * up_value * silu_slope).astype(bf16)
    grad_up_bf = (grad_inner * silu_gate).astype(bf16)
    ffn_in_part = rounded(
        jnp.concatenate(
            [
                contract_cols(grad_gate_bf, gate_own) + contract_cols(grad_up_bf, up_own),
                contract_cols(grad_gate_bf, gate_other) + contract_cols(grad_up_bf, up_other),
            ],
            axis=1,
        )
    ).astype(bf16)
    gate_away = contract_rows(ffn_in_bf[:, half_width:], grad_gate_bf).astype(bf16)
    down_away = core_away(grid, down_kept, down_core)
    down_core, down_away, ffn_in_part, gate_away, grad_gate_bf, grad_up_bf = fence(
        down_core, down_away, ffn_in_part, gate_away, grad_gate_bf, grad_up_bf
    )

    ffn_in_moved = swap_txt(ffn_in_part)
    down_moved = swap_inner(grid, down_away)
    gate_core = grid.send(gate_away, core=1)
    gate_kept = contract_rows(ffn_in_bf[:, :half_width], grad_gate_bf).astype(bf16)
    up_kept = contract_rows(ffn_in_bf[:, :half_width], grad_up_bf).astype(bf16)
    up_away = contract_rows(ffn_in_bf[:, half_width:], grad_up_bf).astype(bf16)
    block_out = contract_cols(block_out, one_hot).astype(bf16)
    gate_away = core_away(grid, gate_kept, gate_core)
    block_out, ffn_in_moved, down_moved, up_kept, gate_kept, gate_away = fence(
        block_out, ffn_in_moved, down_moved, up_kept, gate_kept, gate_away
    )

    down_total = inner_total(grid, down_kept, down_core, down_moved)
    gate_moved = swap_inner(grid, gate_away)
    up_core = grid.send(up_away, core=1)
    ffn_in_moved, down_total = fence(ffn_in_moved, down_total)
    down_sum = sum_outer(grid, down_total)
    grad_residual, grad_attn_bf, res_sums, attn_sums = row_call(
        middle_rows,
        "middle_rows",
        [clip_column, residual, ffn_in_part, ffn_in_moved, upstream, attn_part, attn_moved],
        [own_tanhs[0], own_scales[1], gains],
        [f32, bf16],
        2,
    )
    grad_combined = dot(grad_attn_bf[:, :half_width], out_own) + dot(
        grad_attn_bf[:, half_width:], out_other
    )
    grad_attended_bf = grad_combined.astype(bf16)
    grad_long_bf = grad_attended_bf[:LONG_DEV]
    grad_long_q, *long_parts = attend_call(
        "attend_long_back", long_clip, long_seen, long_query, long_pairs, long_pairs, own_width,
        (grad_long_bf, long_out, long_lse), bf16,
    )
    long_terms = jnp.concatenate(long_parts, axis=1)
    long_kept, long_away = long_terms[: long_count // 2], long_terms[long_count // 2 :]
    out_kept = contract_rows(grad_attn_bf[:, :half_width], combined_bf).astype(bf16)
    out_away = contract_rows(grad_attn_bf[:, half_width:], combined_bf).astype(bf16)
    up_away = core_away(grid, up_kept, up_core)
    (
        grad_combined, grad_attended_bf, gate_moved, up_core, up_away, long_kept, long_away, out_kept,
        out_away, grad_long_q,
    ) = fence(
        grad_combined, grad_attended_bf, gate_moved, up_core, up_away, long_kept, long_away, out_kept,
        out_away, grad_long_q,
    )

    up_moved = swap_inner(grid, up_away)
    long_core = grid.send(long_away, core=1)
    out_core = grid.send(out_away, core=1)
    gate_total = inner_total(grid, gate_kept, gate_core, gate_moved)
    grad_combined, gate_total = fence(grad_combined, gate_total)
    gate_sum = sum_outer(grid, gate_total)
    grad_cross_bf = (gate_tanh * grad_combined).astype(bf16)
    own_gate_grad = jnp.sum(
        jnp.sum(grad_combined * cross_out, axis=0).reshape(own_heads, HD), axis=1
    ) * (1.0 - jnp.tanh(own_gates) ** 2)
    grad_query, grad_text_key, grad_text_value = attend_call(
        "attend_cross_back", clip_column, cross_seen, query_bf, text_key_bf, text_value_bf, 0,
        (grad_cross_bf, cross_out, cross_lse),
    )
    grad_tkey, text_gain_grad = head_call(
        norm_heads_back, "norm_text_back", text_raw, 0, text_gain, text_turns, (grad_text_key,)
    )
    grad_tval = grad_text_value.astype(bf16)
    tkey_kept = contract_rows(feats[:, :half_text], grad_tkey).astype(bf16)
    tkey_away = contract_rows(feats[:, half_text:], grad_tkey).astype(bf16)
    long_away = core_away(grid, long_kept, long_core)
    out_away = core_away(grid, out_kept, out_core)
    (
        gate_sum, down_sum, up_moved, long_core, long_away, out_core, out_away, grad_query, grad_tkey,
        grad_tval, tkey_kept, tkey_away, grad_attended_bf,
    ) = fence(
        gate_sum, down_sum, up_moved, long_core, long_away, out_core, out_away, grad_query, grad_tkey,
        grad_tval, tkey_kept, tkey_away, grad_attended_bf,
    )

    long_moved = swap_inner(grid, long_away)
    out_moved = swap_inner(grid, out_away)
    tkey_core = grid.send(tkey_away, core=1)
    down_grad = down_sum.astype(f32)
    gate_grad = gate_sum.astype(f32)
    up_total = inner_total(grid, up_kept, up_core, up_moved)
    grad_attended_bf, up_total = fence(grad_attended_bf, up_total)
    up_sum = sum_outer(grid, up_total)
    grad_short_bf = grad_attended_bf[LONG_DEV:]
    grad_short_q, grad_short_k, grad_short_v = attend_call(
        "attend_short_back", short_clip, short_seen, short_query, short_key, short_value, 0,
        (grad_short_bf, short_out, short_lse),
    )
    tval_kept = contract_rows(feats[:, :half_text], grad_tval).astype(bf16)
    tval_away = contract_rows(feats[:, half_text:], grad_tval).astype(bf16)
    null_flags = jnp.concatenate([own_null, null_mask[clip_total - 1 :] == 1]).astype(f32)
    row_ids = jnp.arange(text_rows, dtype=jnp.int32)
    null_chosen = jnp.where(
        row_ids[None, :] % TXT_LEN == jnp.arange(TXT_LEN, dtype=jnp.int32)[:, None],
        jnp.repeat(null_flags, TXT_LEN)[None, :],
        0.0,
    ).astype(bf16)
    null_rows = jnp.concatenate(
        [dot(null_chosen, grad_tkey), dot(null_chosen, grad_tval)], axis=1
    ).astype(bf16)
    tkey_away = core_away(grid, tkey_kept, tkey_core)
    (
        up_sum, long_moved, out_moved, tkey_core, tkey_away, tval_kept, tval_away, grad_short_q,
        grad_short_k, grad_short_v, null_rows,
    ) = fence(
        up_sum, long_moved, out_moved, tkey_core, tkey_away, tval_kept, tval_away, grad_short_q,
        grad_short_k, grad_short_v, null_rows,
    )

    tkey_moved = swap_inner(grid, tkey_away)
    tval_core = grid.send(tval_away, core=1)
    null_moved = pair_sum(grid, null_rows, 1)
    up_grad = up_sum.astype(f32)
    both_total = join_sums(
        grid,
        [long_kept, long_core] + long_moved,
        [out_kept, out_core] + out_moved,
        LONG_DEV,
        depth,
    )
    both_sum = sum_outer(grid, both_total)
    grad_query_raw, query_gain_grad = head_call(
        norm_heads_back, "norm_queries_back", projected, 0, query_gain, turns,
        (grad_query, jnp.concatenate([grad_long_q, grad_short_q], axis=0)),
    )
    tval_away = core_away(grid, tval_kept, tval_core)
    (
        both_sum, tkey_moved, tval_core, tval_away, null_moved, grad_query_raw, grad_short_k,
        grad_short_v, query_gain_grad,
    ) = fence(
        both_sum, tkey_moved, tval_core, tval_away, null_moved, grad_query_raw, grad_short_k,
        grad_short_v, query_gain_grad,
    )

    tval_moved = swap_inner(grid, tval_away)
    null_rows = null_rows + null_moved
    null_moved = pair_sum(grid, null_rows, 2)
    out_grad = both_sum[2 * LONG_DEV :].astype(f32)
    tkey_total = inner_total(grid, tkey_kept, tkey_core, tkey_moved)
    both_sum, tkey_total = fence(both_sum, tkey_total)
    tkey_sum = sum_outer(grid, tkey_total)
    own_terms = both_sum[: 2 * LONG_DEV].astype(f32)
    grad_key = jnp.concatenate([own_terms[:LONG_DEV], grad_short_k], axis=0)
    grad_value = jnp.concatenate([own_terms[LONG_DEV:], grad_short_v], axis=0)
    grad_key_raw, key_gain_grad = head_call(
        norm_heads_back, "norm_keys_back", projected, 1, key_gain, turns, (grad_key,)
    )
    grad_proj_bf = jnp.concatenate(
        [grad_query_raw, grad_key_raw, grad_value.astype(bf16)], axis=1
    )
    normed_part = rounded(
        jnp.concatenate(
            [contract_cols(grad_proj_bf, qkv_own), contract_cols(grad_proj_bf, qkv_other)], axis=1
        )
    ).astype(bf16)
    qkv_kept = contract_rows(normed_in[:, :half_width], grad_proj_bf).astype(bf16)
    qkv_away = contract_rows(normed_in[:, half_width:], grad_proj_bf).astype(bf16)
    first_rows = token_count // 2
    moved_first = swap_txt(normed_part[:first_rows])
    moved_last = swap_txt(normed_part[first_rows:])
    qkv_core = grid.send(qkv_away, core=1)
    qkv_away = core_away(grid, qkv_kept, qkv_core)
    (
        tkey_sum, tval_moved, null_moved, moved_first, qkv_kept, qkv_core, qkv_away, grad_residual,
    ) = fence(
        tkey_sum, tval_moved, null_moved, moved_first, qkv_kept, qkv_core, qkv_away, grad_residual,
    )

    qkv_moved = swap_inner(grid, qkv_away)
    null_rows = null_rows + null_moved
    tval_total = inner_total(grid, tval_kept, tval_core, tval_moved)
    tval_total, null_rows, moved_first, grad_residual = fence(
        tval_total, null_rows, moved_first, grad_residual
    )
    tval_sum = sum_outer(grid, tval_total)
    null_rows = null_rows + pair_sum(grid, null_rows, 4)
    null_moved = pair_sum(grid, null_rows, 8)
    normed_moved = jnp.concatenate([moved_first, moved_last], axis=0)
    video_high, video_low, hidden_sums = row_call(
        last_rows,
        "last_rows",
        [clip_column, hidden, normed_part, normed_moved, grad_residual],
        [own_scales[0], gains],
        [bf16, bf16],
        1,
    )
    hidden_sums, tval_sum, qkv_moved, null_rows, null_moved = fence(
        hidden_sums, tval_sum, qkv_moved, null_rows, null_moved
    )

    text_grad = jnp.stack([tkey_sum.astype(f32), tval_sum.astype(f32)], axis=1)
    qkv_total = inner_total(grid, qkv_kept, qkv_core, qkv_moved)
    hidden_sums, qkv_total = fence(hidden_sums, qkv_total)
    qkv_sum = sum_outer(grid, qkv_total)

    grad_mod = jnp.stack(
        [
            hidden_sums * gains[0],
            attn_sums * gains[1] * (1.0 - own_tanhs[0] * own_tanhs[0]),
            res_sums * gains[2],
            ffn_sums * gains[3] * (1.0 - own_tanhs[1] * own_tanhs[1]),
        ],
        axis=1,
    ).reshape(-1, model_width)
    gain_rows = jnp.stack(
        [
            jnp.sum(hidden_sums * own_scales[0], axis=0),
            jnp.sum(attn_sums * own_tanhs[0], axis=0),
            jnp.sum(res_sums * own_scales[1], axis=0),
            jnp.sum(ffn_sums * own_tanhs[1], axis=0),
        ],
        axis=0,
    )
    rows = contract_cols(
        jnp.concatenate(split_three(jnp.concatenate([grad_mod, gain_rows], axis=0)), axis=0),
        one_hot,
    )
    row_count = rows.shape[0] // 3
    rows = rows[:row_count] + rows[row_count : 2 * row_count] + rows[2 * row_count :]
    gain_rows = rows[-4:]
    own_grad_mod = rows[:-4].reshape(short_clips + 1, 4 * model_width)
    column_count = mod_part.shape[1]
    mod_blocks = lax.dynamic_index_in_dim(
        own_grad_mod.reshape(short_clips + 1, seq_count, 2, column_count),
        txt_index,
        2,
        keepdims=False,
    )
    mod_blocks = turn_seq(grid, jnp.transpose(mod_blocks, (1, 0, 2)))
    null_rows = sum_seq(grid, null_rows + null_moved, 16)
    null_part = jnp.concatenate(
        [
            contract_cols(null_rows[:, :own_width], key_piece)
            + contract_cols(null_rows[:, own_width:], value_piece)
            for key_piece, value_piece in zip(tkey_pieces, tval_pieces)
        ],
        axis=1,
    )
    null_part = rounded(null_part).astype(bf16)
    null_moved = swap_txt(null_part)
    video_grad = contract_cols(video_high, one_hot) + contract_cols(video_low, one_hot)
    slice_grad_mod = jnp.concatenate(
        [
            mod_blocks[:, :short_clips].reshape(clip_total - 1, column_count),
            jnp.sum(mod_blocks[:, short_clips], axis=0, keepdims=True),
        ],
        axis=0,
    )
    ada_weight_grad = lax.dot_general(
        shifted.astype(f32), slice_grad_mod, (((0,), (0,)), ((), ())), precision=highest
    )
    ada_bias_grad = jnp.sum(slice_grad_mod, axis=0)
    grad_shifted = lax.dot_general(
        slice_grad_mod, ada_weight.astype(f32), (((1,), (1,)), ((), ())), precision=highest
    )
    cond_value = condition.astype(f32)
    cond_sigmoid = jax.nn.sigmoid(cond_value)
    cond_part = grad_shifted * cond_sigmoid * (1.0 + cond_value * (1.0 - cond_sigmoid))

    head_rows = [
        lax.dynamic_update_slice(jnp.zeros((1, model_width), f32), rows, (0, head_start * HD))
        for rows in (query_gain_grad, key_gain_grad, text_gain_grad)
    ]
    gains_term = jnp.concatenate([jnp.where(first_half, gain_rows, 0.0)] + head_rows, axis=0)
    gates_term = lax.dynamic_update_slice_in_dim(jnp.zeros((H,), f32), own_gate_grad, head_start, 0)
    cond_count, gains_count = cond_part.size, gains_term.size
    packed = jnp.concatenate([cond_part.reshape(-1), gains_term.reshape(-1), gates_term])
    packed = jnp.pad(packed, (0, -packed.shape[0] % 1024)).reshape(-1, 1024)
    packed = packed + pair_sum(grid, packed, 1)
    packed = packed + pair_sum(grid, packed, 2)
    packed = packed + swap_txt(packed)
    packed, qkv_sum = fence(packed, qkv_sum)
    packed = packed + pair_sum(grid, packed, 4)
    packed, null_moved = fence(packed, null_moved)
    null_grad = reorder_columns(
        null_part.astype(f32) + null_moved.astype(f32), owners, False
    )
    qkv_grad = qkv_sum.astype(f32).reshape(depth, 3, own_width)
    packed = sum_seq(grid, packed, 8)
    packed = packed.reshape(-1)
    condition_grad = packed[:cond_count].reshape(cond_part.shape)
    norm_gains_grad = packed[cond_count : cond_count + gains_count].reshape(gains_term.shape)
    head_gates_grad = packed[cond_count + gains_count : cond_count + gains_count + H]
    return (
        block_out,
        video_grad,
        condition_grad,
        qkv_grad,
        out_grad,
        gate_grad,
        up_grad,
        down_grad,
        text_grad,
        ada_weight_grad,
        ada_bias_grad,
        null_grad,
        norm_gains_grad,
        head_gates_grad,
    )


def solution(mesh):
    placed = (
        P("seq", None),
        P("seq", None),
        P(),
        P("seq", "txt", None),
        P("txt", None),
        P("txt", None),
        P("seq", None, "txt"),
        P("seq", "txt"),
        P("seq", "txt"),
        P("seq", "txt"),
        P("seq", "txt"),
        P("seq", None, "txt"),
        P(None, ("seq", "txt")),
        P(("seq", "txt")),
        P(),
        P(),
        P("seq", None),
        P(),
        P(),
    )
    return jax.shard_map(
        local,
        mesh=mesh,
        in_specs=placed,
        out_specs=(
            P("seq", None),
            P("seq", None),
            P(),
            P("seq", None, "txt"),
            P("seq", "txt"),
            P("seq", "txt"),
            P("seq", "txt"),
            P("seq", "txt"),
            P("seq", None, "txt"),
            P(None, ("seq", "txt")),
            P(("seq", "txt")),
            P(),
            P(),
            P(),
        ),
        check_vma=False,
    )
```

```python
import functools
import math

import jax
import jax.numpy as jnp
from jax import lax
from jax.experimental import pallas as pl
from jax.experimental.pallas import tpu as pltpu
from jax.sharding import PartitionSpec as P

H = 24
HD = 64
TXT_LEN = 64
LONG_DEV = 64

epsilon = 1e-05
negative = -1e30
highest = lax.Precision.HIGHEST
bf16 = jnp.bfloat16
f32 = jnp.float32


def layout(lengths_row, seq_index, long_rows, short_rows):
    clip_count = lengths_row.shape[0]
    clip_ends = jnp.cumsum(lengths_row)
    clip_starts = clip_ends - lengths_row
    row_ids = jnp.arange(short_rows, dtype=jnp.int32)
    local_clip = jnp.sum(
        (row_ids[:, None] >= clip_ends[None, : clip_count - 1]).astype(jnp.int32), axis=1
    )
    chosen = local_clip[:, None] == jnp.arange(clip_count, dtype=jnp.int32)[None, :]
    clip_begin = jnp.sum(jnp.where(chosen, clip_starts[None, :], 0), axis=1)
    clip_local = jnp.concatenate([jnp.full((long_rows,), clip_count, jnp.int32), local_clip])
    long_place = seq_index * long_rows + jnp.arange(long_rows, dtype=jnp.int32)
    position = jnp.concatenate([long_place, row_ids - clip_begin])
    return (clip_local, position)


def rms_parts(values):
    inverse = lax.rsqrt(jnp.mean(values * values, axis=-1, keepdims=True) + epsilon)
    return (values * inverse, inverse)


def rms_back(grad_hat, normed, inverse):
    return inverse * (grad_hat - normed * jnp.mean(grad_hat * normed, axis=-1, keepdims=True))


def dot(left_side, right_side):
    return jnp.dot(left_side, right_side, preferred_element_type=f32)


def dot_pieces(left_side, pieces):
    depth = pieces[0].shape[0]
    total = 0.0
    for place, piece in enumerate(pieces):
        total = total + dot(left_side[:, place * depth : (place + 1) * depth], piece)
    return total


def contract_rows(left_side, right_side):
    return lax.dot_general(
        left_side, right_side, (((0,), (0,)), ((), ())), preferred_element_type=f32
    )


def contract_cols(left_side, right_side):
    return lax.dot_general(
        left_side, right_side, (((1,), (1,)), ((), ())), preferred_element_type=f32
    )


def swap_txt(values):
    return lax.ppermute(values, "txt", [(0, 1), (1, 0)])


def rounded(values):
    return lax.reduce_precision(values, exponent_bits=8, mantissa_bits=7)


def fence(*values):
    return lax.optimization_barrier(values)


class Grid:
    def __init__(self):
        self.count = lax.axis_size("seq")
        self.outer_count = 4
        self.inner_count = self.count // 8
        self.index = lax.axis_index("seq")
        self.core = self.index % 2
        self.inner = (self.index // 2) % self.inner_count
        self.outer = self.index // (2 * self.inner_count)

    def send(self, values, outer=0, inner=0, core=0):
        pairs = []
        for index in range(self.count):
            to_core = (index + core) % 2
            to_inner = (index // 2 + inner) % self.inner_count
            to_outer = (index // (2 * self.inner_count) + outer) % self.outer_count
            pairs.append((index, (to_outer * self.inner_count + to_inner) * 2 + to_core))
        return lax.ppermute(values, "seq", pairs)

    def lines(self):
        step = 2 * self.inner_count
        return [[first + step * k for k in range(self.outer_count)] for first in range(step)]

    def owners(self):
        place = jnp.arange(self.count, dtype=jnp.int32)
        outer = place % self.outer_count
        inner = (self.inner - (place // self.outer_count) % self.inner_count) % self.inner_count
        core = (self.core + place // (self.outer_count * self.inner_count)) % 2
        return (outer * self.inner_count + inner) * 2 + core


def gather_outer(grid, block):
    return lax.all_gather(block, "seq", axis=0, tiled=True, axis_index_groups=grid.lines())


def send_inner(grid, near):
    return [grid.send(near, inner=step) for step in range(1, grid.inner_count)]


def send_core(grid, pieces):
    return [grid.send(piece, core=1) for piece in pieces]


def stack(pieces):
    return jnp.concatenate(pieces, axis=0) if len(pieces) > 1 else pieces[0]


def add_blocks(*refs):
    *sources, target = refs
    total = sources[0][...].astype(f32)
    for source in sources[1:]:
        total = total + source[...].astype(f32)
    target[...] = total.astype(target.dtype)


def add_rows(arrays, starts, rows):
    cols = arrays[0].shape[1]
    block = 256 if rows % 256 == 0 else 128 if rows % 128 == 0 else rows

    def from_row(start):
        return pl.BlockSpec((block, cols), lambda i: (start // block + i, 0))

    return pl.pallas_call(
        add_blocks,
        grid=(rows // block,),
        in_specs=[from_row(start) for start in starts],
        out_specs=from_row(0),
        out_shape=jax.ShapeDtypeStruct((rows, cols), bf16),
        cost_estimate=pl.CostEstimate(flops=1, bytes_accessed=1, transcendentals=0),
        compiler_params=pltpu.CompilerParams(vmem_limit_bytes=48 * 1024 * 1024),
        name="add_rows",
    )(*arrays)


def join_blocks(*refs):
    *sources, target = refs
    half = len(sources) // 2
    totals = []
    for part in (sources[:half], sources[half:]):
        total = part[0][...].astype(f32)
        for source in part[1:]:
            total = total + source[...].astype(f32)
        totals.append(total.astype(bf16))
    rows, width = totals[0].shape[0], totals[1].shape[1]
    target[0, :rows, :] = totals[0][:, :width]
    target[0, rows : 2 * rows, :] = totals[0][:, width:]
    target[0, 2 * rows :, :] = totals[1]


def join_sums(grid, long_parts, out_parts, long_rows, out_rows):
    width = out_parts[0].shape[1]
    rows = 2 * long_rows + out_rows
    long_spec = pl.BlockSpec((long_rows, 2 * width), lambda i: (i, 0))
    out_spec = pl.BlockSpec((out_rows, width), lambda i: (i, 0))
    joined = pl.pallas_call(
        join_blocks,
        grid=(grid.outer_count,),
        in_specs=[long_spec] * len(long_parts) + [out_spec] * len(out_parts),
        out_specs=pl.BlockSpec((1, rows, width), lambda i: (i, 0, 0)),
        out_shape=jax.ShapeDtypeStruct((grid.outer_count, rows, width), bf16),
        cost_estimate=pl.CostEstimate(flops=1, bytes_accessed=1, transcendentals=0),
        name="join_sums",
    )(*long_parts, *out_parts)
    return joined.reshape(grid.outer_count * rows, width)


def core_away(grid, kept, moved):
    rows = kept.shape[0] // grid.inner_count
    return [
        add_rows([kept, moved], [step * rows] * 2, rows) for step in range(1, grid.inner_count)
    ]


def inner_total(grid, kept, moved, arrived):
    rows = kept.shape[0] // grid.inner_count
    return add_rows([kept, moved] + arrived, [0] * (2 + len(arrived)), rows)


def swap_inner(grid, away):
    return [grid.send(part, inner=-step) for step, part in enumerate(away, 1)]


def sum_outer(grid, total):
    return lax.psum_scatter(
        total, "seq", scatter_dimension=0, tiled=True, axis_index_groups=grid.lines()
    )


def pair_sum(grid, values, bit):
    pairs = [(index, index ^ bit) for index in range(grid.count)]
    return lax.ppermute(values, "seq", pairs)


def turn_stage(values, axis, size, own, send):
    moved = [lax.dynamic_index_in_dim(values, own, axis, keepdims=False)]
    for step in range(1, size):
        piece = lax.dynamic_index_in_dim(values, (own + step) % size, axis, keepdims=False)
        moved.append(send(piece, step))
    stacked = jnp.stack(moved, axis=axis)
    order = (own - jnp.arange(size, dtype=jnp.int32)) % size
    return jnp.take(stacked, order, axis=axis)


def turn_seq(grid, values):
    rest = values.shape[1:]
    values = values.reshape((grid.outer_count, grid.inner_count, 2) + rest)
    values = turn_stage(
        values, 0, grid.outer_count, grid.outer, lambda v, k: grid.send(v, outer=k)
    )
    values = turn_stage(
        values, 1, grid.inner_count, grid.inner, lambda v, k: grid.send(v, inner=k)
    )
    values = turn_stage(values, 2, 2, grid.core, lambda v, k: grid.send(v, core=k))
    return values.reshape((grid.count,) + rest)


def sum_seq(grid, values, bit):
    while bit < grid.count:
        values = values + pair_sum(grid, values, bit)
        bit *= 2
    return values


def copy_blocks(to_order, count, order_ref, source_ref, target_ref):
    width = source_ref.shape[1] // count
    for block in range(count):
        moved = pl.ds(pl.multiple_of(order_ref[block] * width, width), width)
        plain = pl.ds(block * width, width)
        if to_order:
            target_ref[:, plain] = source_ref[:, moved]
        else:
            target_ref[:, moved] = source_ref[:, plain]


def reorder_columns(values, order, to_order):
    rows, cols = values.shape
    count = order.shape[0]
    width = cols // count
    if width % 128:
        taken = order if to_order else jnp.argsort(order)
        return jnp.take(values.reshape(rows, count, width), taken, axis=1).reshape(rows, cols)
    return pl.pallas_call(
        functools.partial(copy_blocks, to_order, count),
        out_shape=jax.ShapeDtypeStruct(values.shape, values.dtype),
        in_specs=[
            pl.BlockSpec(memory_space=pltpu.SMEM),
            pl.BlockSpec(memory_space=pltpu.VMEM),
        ],
        out_specs=pl.BlockSpec(memory_space=pltpu.VMEM),
        name="reorder_columns",
    )(order, values)


def split_three(values):
    high = rounded(values)
    rest = values - high
    middle = rounded(rest)
    return high.astype(bf16), middle.astype(bf16), (rest - middle).astype(bf16)


def exact_dot(values, one_hot):
    rows = values.shape[0]
    parts = dot(jnp.concatenate(split_three(values), axis=0), one_hot)
    return parts[:rows] + parts[rows : 2 * rows] + parts[2 * rows :]


def choose(clip, rows):
    chosen = rows[-1:]
    for index in range(rows.shape[0] - 1):
        chosen = jnp.where(clip == index, rows[index : index + 1], chosen)
    return chosen


def add_clip_sums(clip, values, sums_ref):
    @pl.when(pl.program_id(0) == 0)
    def _():
        sums_ref[...] = jnp.zeros_like(sums_ref)

    for index in range(sums_ref.shape[0]):
        part = jnp.sum(jnp.where(clip == index, values, 0.0), axis=0, keepdims=True)
        sums_ref[index : index + 1, :] += part


def add_pair(own_ref, moved_ref):
    return own_ref[...].astype(f32) + moved_ref[...].astype(f32)


def enter_rows(clip_ref, hidden_ref, part_ref, moved_ref, tanh_ref, scale_ref, gains_ref, res_ref, in_ref):
    clip = clip_ref[...]
    attn_hat, _ = rms_parts(add_pair(part_ref, moved_ref))
    tanh_tok = choose(clip, tanh_ref[...])
    residual = hidden_ref[...].astype(f32) + tanh_tok * attn_hat * gains_ref[1:2]
    res_hat, _ = rms_parts(residual)
    res_ref[...] = residual
    in_ref[...] = (res_hat * gains_ref[2:3] * choose(clip, scale_ref[...])).astype(bf16)


def leave_rows(clip_ref, part_ref, moved_ref, up_ref, tanh_ref, gains_ref, grad_ref):
    hat, inverse = rms_parts(add_pair(part_ref, moved_ref))
    grad_hat = up_ref[...].astype(f32) * choose(clip_ref[...], tanh_ref[...]) * gains_ref[3:4]
    grad_ref[...] = rms_back(grad_hat, hat, inverse).astype(bf16)


def block_rows(clip_ref, res_ref, part_ref, moved_ref, up_ref, tanh_ref, gains_ref, out_ref, sums_ref):
    clip = clip_ref[...]
    hat, _ = rms_parts(add_pair(part_ref, moved_ref))
    out_ref[...] = (res_ref[...] + choose(clip, tanh_ref[...]) * hat * gains_ref[3:4]).astype(bf16)
    add_clip_sums(clip, up_ref[...].astype(f32) * hat, sums_ref)


def middle_rows(
    clip_ref, res_ref, grad_part_ref, grad_moved_ref, up_ref, part_ref, moved_ref, tanh_ref,
    scale_ref, gains_ref, grad_res_ref, grad_attn_ref,
):
    clip = clip_ref[...]
    hat, inverse = rms_parts(res_ref[...])
    grad_hat = add_pair(grad_part_ref, grad_moved_ref) * gains_ref[2:3]
    grad_hat = grad_hat * choose(clip, scale_ref[...])
    grad_res = up_ref[...].astype(f32) + rms_back(grad_hat, hat, inverse)
    grad_res_ref[...] = grad_res
    hat, inverse = rms_parts(add_pair(part_ref, moved_ref))
    grad_hat = grad_res * gains_ref[1:2] * choose(clip, tanh_ref[...])
    grad_attn_ref[...] = rms_back(grad_hat, hat, inverse).astype(bf16)


def sum_rows(
    clip_ref, res_ref, grad_part_ref, grad_moved_ref, grad_res_ref, part_ref, moved_ref, _,
    res_sums_ref, attn_sums_ref,
):
    clip = clip_ref[...]
    hat, _ = rms_parts(res_ref[...])
    add_clip_sums(clip, add_pair(grad_part_ref, grad_moved_ref) * hat, res_sums_ref)
    hat, _ = rms_parts(add_pair(part_ref, moved_ref))
    add_clip_sums(clip, grad_res_ref[...] * hat, attn_sums_ref)


def last_rows(
    clip_ref, hidden_ref, part_ref, moved_ref, grad_res_ref, scale_ref, gains_ref, high_ref, low_ref,
    sums_ref,
):
    clip = clip_ref[...]
    grad = add_pair(part_ref, moved_ref)
    hat, inverse = rms_parts(hidden_ref[...].astype(f32))
    add_clip_sums(clip, grad * hat, sums_ref)
    grad_hat = grad * gains_ref[0:1] * choose(clip, scale_ref[...])
    total = grad_res_ref[...] + rms_back(grad_hat, hat, inverse)
    high = total.astype(bf16)
    high_ref[...] = high
    low_ref[...] = (total - high.astype(f32)).astype(bf16)


def row_call(body, name, arrays, tables, outs, sums):
    count, width = arrays[1].shape
    rows = count // 4

    def by_rows(array):
        return pl.BlockSpec((rows, array.shape[1]), lambda i: (i, 0))

    def whole(array):
        return pl.BlockSpec(array.shape, lambda i: (0, 0))

    out_shapes = [jax.ShapeDtypeStruct((count, width), kind) for kind in outs]
    sum_shapes = [jax.ShapeDtypeStruct((tables[0].shape[0], width), f32)] * sums
    return pl.pallas_call(
        body,
        grid=(4,),
        in_specs=[by_rows(array) for array in arrays] + [whole(table) for table in tables],
        out_specs=[by_rows(shape) for shape in out_shapes] + [whole(shape) for shape in sum_shapes],
        out_shape=out_shapes + sum_shapes,
        cost_estimate=pl.CostEstimate(flops=1, bytes_accessed=1, transcendentals=0),
        compiler_params=pltpu.CompilerParams(vmem_limit_bytes=48 * 1024 * 1024),
        name=name,
    )(*arrays, *tables)


def head_means(values):
    first = lax.broadcasted_iota(jnp.int32, values.shape, 1) < HD
    front = jnp.sum(jnp.where(first, values, 0.0), axis=1, keepdims=True)
    back = jnp.sum(jnp.where(first, 0.0, values), axis=1, keepdims=True)
    return jnp.where(first, front, back) * (1.0 / HD)


def turn_lanes(values, cosine, sine):
    lane = lax.broadcasted_iota(jnp.int32, values.shape, 1) % HD
    ahead = pltpu.roll(values, 2 * HD - HD // 2, 1)
    behind = pltpu.roll(values, HD // 2, 1)
    return values * cosine + jnp.where(lane < HD // 2, -ahead, behind) * sine


def norm_heads(values_ref, gain_ref, cos_ref, sin_ref, out_ref):
    cosine, sine = cos_ref[...], sin_ref[...]
    for start in range(0, out_ref.shape[1], 2 * HD):
        part = slice(start, start + 2 * HD)
        values = values_ref[:, part]
        hat = values * lax.rsqrt(head_means(values * values) + epsilon)
        out_ref[:, part] = turn_lanes(hat * gain_ref[:, part], cosine, sine).astype(bf16)


def norm_heads_back(*refs):
    values_ref, gain_ref, cos_ref, sin_ref, *grad_refs, out_ref, sums_ref = refs
    cosine, sine = cos_ref[...], sin_ref[...]

    @pl.when(pl.program_id(0) == 0)
    def _():
        sums_ref[...] = jnp.zeros_like(sums_ref)

    for start in range(0, out_ref.shape[1], 2 * HD):
        part = slice(start, start + 2 * HD)
        values = values_ref[:, part]
        inverse = lax.rsqrt(head_means(values * values) + epsilon)
        hat = values * inverse
        grad = grad_refs[0][:, part]
        for grad_ref in grad_refs[1:]:
            grad = grad + grad_ref[:, part]
        grad = turn_lanes(grad, cosine, -sine)
        sums_ref[:, part] += jnp.sum(grad * hat, axis=0, keepdims=True)
        grad = grad * gain_ref[:, part]
        out_ref[:, part] = (inverse * (grad - hat * head_means(grad * hat))).astype(bf16)


def head_call(body, name, values, column, gain, turns, grads=()):
    count, width = turns[0].shape[0], gain.shape[1]
    rows = count // 4
    by_rows = pl.BlockSpec((rows, width), lambda i: (i, 0))
    whole = pl.BlockSpec((1, width), lambda i: (0, 0))
    turn = pl.BlockSpec((rows, 2 * HD), lambda i: (i, 0))
    out_shape = [jax.ShapeDtypeStruct((count, width), bf16)]
    out_specs = [by_rows]
    if grads:
        out_shape.append(jax.ShapeDtypeStruct((1, width), f32))
        out_specs.append(whole)
    results = pl.pallas_call(
        body,
        grid=(4,),
        in_specs=[pl.BlockSpec((rows, width), lambda i: (i, column)), whole, turn, turn]
        + [by_rows] * len(grads),
        out_specs=out_specs,
        out_shape=out_shape,
        cost_estimate=pl.CostEstimate(flops=1, bytes_accessed=1, transcendentals=0),
        compiler_params=pltpu.CompilerParams(vmem_limit_bytes=48 * 1024 * 1024),
        name=name,
    )(values, gain, *turns, *grads)
    return results if grads else results[0]


def attend_heads(clip_ref, key_clip_ref, query_ref, key_ref, value_ref, out_ref, total_ref):
    visible = clip_ref[...] == key_clip_ref[...]
    for start in range(0, 2 * HD, HD):
        head = slice(start, start + HD)
        scores = contract_cols(query_ref[:, head], key_ref[:, head]) * HD ** (-0.5)
        scores = jnp.where(visible, scores, negative)
        peak = jnp.max(scores, axis=1, keepdims=True)
        exponent = jnp.exp(scores - peak)
        total = jnp.sum(exponent, axis=1, keepdims=True)
        out_ref[:, head] = dot((exponent / total).astype(bf16), value_ref[:, head])
        total_ref[:, head] = jnp.broadcast_to(peak + jnp.log(total), (total_ref.shape[0], HD))


def attend_heads_back(
    clip_ref, key_clip_ref, query_ref, key_ref, value_ref, grad_ref, out_ref, total_ref,
    grad_query_ref, grad_key_ref, grad_value_ref,
):
    visible = clip_ref[...] == key_clip_ref[...]
    for start in range(0, 2 * HD, HD):
        head = slice(start, start + HD)
        query, key = query_ref[:, head], key_ref[:, head]
        grad = grad_ref[:, head]
        scores = contract_cols(query, key) * HD ** (-0.5)
        weights = jnp.where(visible, jnp.exp(scores - total_ref[:, start : start + 1]), 0.0)
        delta = jnp.sum(grad.astype(f32) * out_ref[:, head], axis=1, keepdims=True)
        grad_scores = weights * (contract_cols(grad, value_ref[:, head]) - delta)
        grad_scores = grad_scores.astype(bf16)
        grad_query_ref[:, head] = dot(grad_scores, key) * HD ** (-0.5)
        grad_key = contract_rows(grad_scores, query) * HD ** (-0.5)
        grad_key_ref[:, head] = grad_key.astype(grad_key_ref.dtype)
        grad_value = contract_rows(weights.astype(bf16), grad)
        grad_value_ref[:, head] = grad_value.astype(grad_value_ref.dtype)


def attend_call(name, clips, key_clips, query, key, value, value_column=0, back=(), kind=f32):
    count, keys, width = query.shape[0], key.shape[0], query.shape[1]
    first = value_column // (2 * HD)
    queries = pl.BlockSpec((count, 2 * HD), lambda i: (0, i))
    seen = pl.BlockSpec((keys, 2 * HD), lambda i: (0, i))
    whole = [pl.BlockSpec(array.shape, lambda i: (0, 0)) for array in (clips, key_clips)]
    out_shape = [jax.ShapeDtypeStruct((count, width), f32)]
    if back:
        out_shape += [jax.ShapeDtypeStruct((keys, width), kind)] * 2
        out_specs = [queries, seen, seen]
    else:
        out_shape += out_shape
        out_specs = [queries, queries]
    return pl.pallas_call(
        attend_heads_back if back else attend_heads,
        grid=(width // (2 * HD),),
        in_specs=whole
        + [queries, seen, pl.BlockSpec((keys, 2 * HD), lambda i: (0, first + i))]
        + [queries] * len(back),
        out_specs=out_specs,
        out_shape=out_shape,
        cost_estimate=pl.CostEstimate(flops=1, bytes_accessed=1, transcendentals=0),
        compiler_params=pltpu.CompilerParams(vmem_limit_bytes=48 * 1024 * 1024),
        name=name,
    )(clips, key_clips, query, key, value, *back)


def local(
    video_tokens,
    cotangent,
    condition,
    captions,
    long_caption,
    null_embed,
    query_key_value,
    out_weight,
    gate_weight,
    up_weight,
    down_weight,
    text_weight,
    ada_weight,
    ada_bias,
    norm_gains,
    head_gates,
    clip_lengths,
    null_mask,
    text_lengths,
):
    grid = Grid()
    seq_index = grid.index
    seq_count = grid.count
    txt_index = lax.axis_index("txt")
    first_half = txt_index == 0
    token_count, model_width = video_tokens.shape
    depth = query_key_value.shape[0]
    text_depth, text_width = text_weight.shape[0], captions.shape[2]
    half_width = model_width // 2
    own_heads = query_key_value.shape[2] // HD
    own_width = own_heads * HD
    head_start = txt_index * own_heads
    clip_total = condition.shape[0]
    short_clips = clip_lengths.shape[1]
    clip_local, position = layout(clip_lengths[0], seq_index, LONG_DEV, token_count - LONG_DEV)
    owners = grid.owners()
    text_rows = (short_clips + 1) * TXT_LEN

    half_text = text_width // 2
    text_block = text_weight.reshape(text_depth, 2 * own_width)

    qkv_block, condition = fence(query_key_value.reshape(depth, 3 * own_width), condition)
    qkv_near = gather_outer(grid, qkv_block)
    shifted = jax.nn.silu(condition.astype(f32)).astype(bf16)
    mod_part = dot(shifted, ada_weight) + ada_bias
    short_part = mod_part[: clip_total - 1].reshape(seq_count, short_clips, mod_part.shape[1])
    long_part = jnp.broadcast_to(
        mod_part[clip_total - 1 :][None], (seq_count, 1, mod_part.shape[1])
    )
    own_part = turn_seq(grid, jnp.concatenate([short_part, long_part], axis=1))
    other_part = swap_txt(own_part)
    own_null = lax.dynamic_slice_in_dim(null_mask, seq_index * short_clips, short_clips, 0) == 1
    short_feats = jnp.where(own_null[:, None, None], null_embed[None], captions)
    long_feats = jnp.where(null_mask[clip_total - 1] == 1, null_embed, long_caption)
    own_feats = jnp.concatenate([short_feats, long_feats[None]], axis=0).reshape(-1, text_width)
    own_feats = reorder_columns(own_feats, owners, True)

    columns = jnp.arange(model_width, dtype=jnp.int32)
    column_order = jnp.repeat(owners, depth) * depth + columns % depth
    one_hot = (columns[:, None] == column_order[None, :]).astype(bf16)
    hidden = dot(video_tokens, one_hot).astype(bf16)
    hidden_hat, _ = rms_parts(hidden.astype(f32))
    clip_column = clip_local[:, None]
    tkey_block, tval_block = text_block[:, :own_width], text_block[:, own_width:]
    qkv_near, own_part, other_part, own_feats, tkey_block, tval_block, out_weight = fence(
        qkv_near, own_part, other_part, own_feats, tkey_block, tval_block, out_weight
    )

    qkv_y = send_inner(grid, qkv_near)
    qkv_near_core = send_core(grid, [qkv_near])
    tkey_near = gather_outer(grid, tkey_block)
    out_near = gather_outer(grid, out_weight)
    other_feats = swap_txt(own_feats)
    own_mod = jnp.stack(
        [jnp.where(first_half, own_part, other_part), jnp.where(first_half, other_part, own_part)],
        axis=1,
    )
    own_mod = jnp.transpose(own_mod, (2, 0, 1, 3)).reshape((short_clips + 1) * 4, model_width)
    rows = exact_dot(jnp.concatenate([own_mod, norm_gains[:4]], axis=0), one_hot)
    gains = rows[-4:]
    own_mod = rows[:-4].reshape(short_clips + 1, 4, model_width)
    own_scales = 1.0 + own_mod[:, 0], 1.0 + own_mod[:, 2]
    own_tanhs = jnp.tanh(own_mod[:, 1]), jnp.tanh(own_mod[:, 3])
    selector = clip_local[:, None] == jnp.arange(short_clips + 1, dtype=jnp.int32)[None, :]

    def per_token(rows):
        chosen = rows[short_clips:]
        for clip in range(short_clips):
            chosen = jnp.where(selector[:, clip : clip + 1], rows[clip : clip + 1], chosen)
        return chosen

    normed_in = (hidden_hat * gains[0] * per_token(own_scales[0])).astype(bf16)
    query_gain, key_gain, text_gain = [
        lax.dynamic_slice(norm_gains, (row, head_start * HD), (1, own_width)) for row in (4, 5, 6)
    ]
    frequency = jnp.exp(
        jnp.arange(HD // 2, dtype=f32) * (-math.log(10000.0) / (HD // 2))
    )
    angles = jnp.tile(position.astype(f32)[:, None] * frequency, (1, 4))
    turns = jnp.cos(angles), jnp.sin(angles)
    text_turns = jnp.ones((text_rows, 2 * HD), f32), jnp.zeros((text_rows, 2 * HD), f32)
    normed_in, other_feats, tkey_near, out_near, tval_block, qkv_near_core, qkv_y = fence(
        normed_in, other_feats, tkey_near, out_near, tval_block, qkv_near_core, qkv_y
    )

    tkey_y = send_inner(grid, tkey_near)
    tkey_near_core = send_core(grid, [tkey_near])
    out_near_core = send_core(grid, [out_near])
    tval_near = gather_outer(grid, tval_block)
    qkv_core, normed_in = fence(send_core(grid, qkv_y), normed_in)
    qkv_own, qkv_other = stack([qkv_near] + qkv_y), stack(qkv_near_core + qkv_core)
    projected = dot(normed_in[:, :half_width], qkv_own) + dot(normed_in[:, half_width:], qkv_other)
    query_bf = head_call(norm_heads, "norm_queries", projected, 0, query_gain, turns)
    key_bf = head_call(norm_heads, "norm_keys", projected, 1, key_gain, turns)
    value_bf = projected[:, 2 * own_width :].astype(bf16)
    long_block = jnp.concatenate([key_bf[:LONG_DEV], value_bf[:LONG_DEV]], axis=1)
    (
        query_bf, key_bf, value_bf, long_block, tkey_y, tkey_near_core, out_near, out_near_core,
        tval_near, gate_weight,
    ) = fence(
        query_bf, key_bf, value_bf, long_block, tkey_y, tkey_near_core, out_near, out_near_core,
        tval_near, gate_weight,
    )

    tail = long_block.size // gate_weight.shape[1]
    gate_near = gather_outer(
        grid, jnp.concatenate([gate_weight, long_block.reshape(tail, -1)], axis=0)
    )
    tval_y = send_inner(grid, tval_near)
    tval_near_core = send_core(grid, [tval_near])
    short_query = query_bf[LONG_DEV:]
    short_key = key_bf[LONG_DEV:]
    short_value = value_bf[LONG_DEV:]
    short_clip = clip_column[LONG_DEV:]
    short_seen = clip_local[LONG_DEV:][None, :]
    short_out, short_lse = attend_call(
        "attend_short", short_clip, short_seen, short_query, short_key, short_value
    )
    out_y = send_inner(grid, out_near)
    tkey_core = send_core(grid, tkey_y)
    feats = jnp.concatenate(
        [
            jnp.where(first_half, own_feats, other_feats).reshape(-1, TXT_LEN // 2, text_width),
            jnp.where(first_half, other_feats, own_feats).reshape(-1, TXT_LEN // 2, text_width),
        ],
        axis=1,
    ).reshape(text_rows, text_width)
    tval_y, tval_near_core, gate_near, tkey_core, out_y, up_weight, feats, short_out = fence(
        tval_y, tval_near_core, gate_near, tkey_core, out_y, up_weight, feats, short_out
    )

    gate_near = gate_near.reshape(grid.outer_count, depth + tail, -1)
    long_near = gate_near[:, depth:].reshape(-1, 2 * own_width)
    gate_near = gate_near[:, :depth].reshape(grid.outer_count * depth, -1)
    long_y = send_inner(grid, long_near)
    long_near_core = send_core(grid, [long_near])
    gate_y = send_inner(grid, gate_near)
    gate_near_core = send_core(grid, [gate_near])
    up_near = gather_outer(grid, up_weight)
    tval_core = send_core(grid, tval_y)
    long_core = send_core(grid, long_y)
    out_core = send_core(grid, out_y)
    tkey_pieces = [tkey_near] + tkey_y + tkey_near_core + tkey_core
    text_raw = dot_pieces(feats, tkey_pieces)
    text_key_bf = head_call(norm_heads, "norm_text", text_raw, 0, text_gain, text_turns)

    out_own, out_other = stack([out_near] + out_y), stack(out_near_core + out_core)
    long_pairs = stack([long_near] + long_y + long_near_core + long_core)
    long_count = long_pairs.shape[0]
    long_query = query_bf[:LONG_DEV]
    long_clip = clip_column[:LONG_DEV]
    long_seen = jnp.full((1, long_count), short_clips, jnp.int32)
    long_out, long_lse = attend_call(
        "attend_long", long_clip, long_seen, long_query, long_pairs, long_pairs, own_width
    )
    tval_pieces = [tval_near] + tval_y + tval_near_core + tval_core
    text_value_bf = dot_pieces(feats, tval_pieces).astype(bf16)
    key_clip = jnp.arange(text_rows, dtype=jnp.int32) // TXT_LEN
    key_place = jnp.arange(text_rows, dtype=jnp.int32) % TXT_LEN
    limits = jnp.concatenate(
        [
            lax.dynamic_slice_in_dim(text_lengths, seq_index * short_clips, short_clips, 0),
            text_lengths[clip_total - 1 :],
        ]
    )
    clip_match = key_clip[:, None] == jnp.arange(short_clips + 1, dtype=jnp.int32)[None, :]
    key_limit = jnp.sum(jnp.where(clip_match, limits[None, :], 0), axis=1)
    cross_seen = jnp.where(key_place < key_limit, key_clip, -1)[None, :]
    cross_out, cross_lse = attend_call(
        "attend_cross", clip_column, cross_seen, query_bf, text_key_bf, text_value_bf
    )
    attended = jnp.concatenate([long_out, short_out], axis=0)
    own_gates = lax.dynamic_slice_in_dim(head_gates, head_start, own_heads, 0)
    gate_tanh = jnp.repeat(jnp.tanh(own_gates), HD)[None, :]
    combined_bf = (attended + gate_tanh * cross_out).astype(bf16)
    attn_part = rounded(
        jnp.concatenate(
            [contract_cols(combined_bf, out_own), contract_cols(combined_bf, out_other)], axis=1
        )
    ).astype(bf16)
    attn_part, gate_y, gate_near_core, up_near, down_weight = fence(
        attn_part, gate_y, gate_near_core, up_near, down_weight
    )

    attn_moved = swap_txt(attn_part)
    up_y = send_inner(grid, up_near)
    up_near_core = send_core(grid, [up_near])
    down_near = gather_outer(grid, down_weight)
    gate_core = send_core(grid, gate_y)
    attn_moved, up_y, up_near_core, down_near, gate_core = fence(
        attn_moved, up_y, up_near_core, down_near, gate_core
    )

    down_y = send_inner(grid, down_near)
    down_near_core = send_core(grid, [down_near])
    up_core = send_core(grid, up_y)
    gate_own, gate_other = stack([gate_near] + gate_y), stack(gate_near_core + gate_core)
    residual, ffn_in_bf = row_call(
        enter_rows,
        "enter_rows",
        [clip_column, hidden, attn_part, attn_moved],
        [own_tanhs[0], own_scales[1], gains],
        [f32, bf16],
        0,
    )
    gate_value = dot(ffn_in_bf[:, :half_width], gate_own) + dot(
        ffn_in_bf[:, half_width:], gate_other
    )
    up_core, gate_value = fence(up_core, gate_value)
    up_own, up_other = stack([up_near] + up_y), stack(up_near_core + up_core)
    up_value = dot(ffn_in_bf[:, :half_width], up_own) + dot(ffn_in_bf[:, half_width:], up_other)
    inner_bf = (gate_value * jax.nn.sigmoid(gate_value) * up_value).astype(bf16)
    inner_bf, down_y, down_near_core = fence(inner_bf, down_y, down_near_core)

    down_core = send_core(grid, down_y)
    down_core, inner_bf, cotangent = fence(down_core, inner_bf, cotangent)
    down_own, down_other = stack([down_near] + down_y), stack(down_near_core + down_core)
    ffn_part = rounded(
        jnp.concatenate(
            [contract_cols(inner_bf, down_own), contract_cols(inner_bf, down_other)], axis=1
        )
    ).astype(bf16)
    ffn_part, gate_value, cotangent = fence(ffn_part, gate_value, cotangent)

    ffn_moved = swap_txt(ffn_part)
    upstream = dot(cotangent, one_hot).astype(bf16)
    sigmoid_gate = jax.nn.sigmoid(gate_value)
    silu_gate = gate_value * sigmoid_gate
    gate_slope = up_value * (sigmoid_gate * (1.0 + gate_value * (1.0 - sigmoid_gate)))
    ffn_moved, ffn_part, upstream, silu_gate, gate_slope = fence(
        ffn_moved, ffn_part, upstream, silu_gate, gate_slope
    )

    (grad_ffn_out,) = row_call(
        leave_rows,
        "leave_rows",
        [clip_column, ffn_part, ffn_moved, upstream],
        [own_tanhs[1], gains],
        [bf16],
        0,
    )
    down_kept = contract_rows(grad_ffn_out[:, :half_width], inner_bf).astype(bf16)
    down_away = contract_rows(grad_ffn_out[:, half_width:], inner_bf).astype(bf16)
    grad_ffn_out, down_away, down_kept = fence(grad_ffn_out, down_away, down_kept)

    down_core = grid.send(down_away, core=1)
    grad_inner = dot(grad_ffn_out[:, :half_width], down_own) + dot(
        grad_ffn_out[:, half_width:], down_other
    )
    grad_gate_bf = (grad_inner * gate_slope).astype(bf16)
    grad_up_bf = (grad_inner * silu_gate).astype(bf16)
    ffn_in_part = rounded(
        jnp.concatenate(
            [
                contract_cols(grad_gate_bf, gate_own) + contract_cols(grad_up_bf, up_own),
                contract_cols(grad_gate_bf, gate_other) + contract_cols(grad_up_bf, up_other),
            ],
            axis=1,
        )
    ).astype(bf16)
    gate_away = contract_rows(ffn_in_bf[:, half_width:], grad_gate_bf).astype(bf16)
    down_away = core_away(grid, down_kept, down_core)
    down_core, down_away, ffn_in_part, gate_away, grad_gate_bf, grad_up_bf = fence(
        down_core, down_away, ffn_in_part, gate_away, grad_gate_bf, grad_up_bf
    )

    ffn_in_moved = swap_txt(ffn_in_part)
    down_moved = swap_inner(grid, down_away)
    gate_core = grid.send(gate_away, core=1)
    gate_kept = contract_rows(ffn_in_bf[:, :half_width], grad_gate_bf).astype(bf16)
    up_kept = contract_rows(ffn_in_bf[:, :half_width], grad_up_bf).astype(bf16)
    up_away = contract_rows(ffn_in_bf[:, half_width:], grad_up_bf).astype(bf16)
    block_out, ffn_sums = row_call(
        block_rows,
        "block_rows",
        [clip_column, residual, ffn_part, ffn_moved, upstream],
        [own_tanhs[1], gains],
        [bf16],
        1,
    )
    block_out = contract_cols(block_out, one_hot).astype(bf16)
    gate_away = core_away(grid, gate_kept, gate_core)
    block_out, ffn_in_moved, down_moved, up_kept, gate_kept, gate_away = fence(
        block_out, ffn_in_moved, down_moved, up_kept, gate_kept, gate_away
    )

    down_total = inner_total(grid, down_kept, down_core, down_moved)
    gate_moved = swap_inner(grid, gate_away)
    up_core = grid.send(up_away, core=1)
    ffn_in_moved, down_total = fence(ffn_in_moved, down_total)
    down_sum = sum_outer(grid, down_total)
    grad_residual, grad_attn_bf = row_call(
        middle_rows,
        "middle_rows",
        [clip_column, residual, ffn_in_part, ffn_in_moved, upstream, attn_part, attn_moved],
        [own_tanhs[0], own_scales[1], gains],
        [f32, bf16],
        0,
    )
    grad_combined = dot(grad_attn_bf[:, :half_width], out_own) + dot(
        grad_attn_bf[:, half_width:], out_other
    )
    grad_attended_bf = grad_combined.astype(bf16)
    grad_long_bf = grad_attended_bf[:LONG_DEV]
    grad_long_q, *long_parts = attend_call(
        "attend_long_back", long_clip, long_seen, long_query, long_pairs, long_pairs, own_width,
        (grad_long_bf, long_out, long_lse), bf16,
    )
    long_terms = jnp.concatenate(long_parts, axis=1)
    long_kept, long_away = long_terms[: long_count // 2], long_terms[long_count // 2 :]
    out_kept = contract_rows(grad_attn_bf[:, :half_width], combined_bf).astype(bf16)
    out_away = contract_rows(grad_attn_bf[:, half_width:], combined_bf).astype(bf16)
    up_away = core_away(grid, up_kept, up_core)
    (
        grad_combined, grad_attended_bf, gate_moved, up_core, up_away, long_kept, long_away, out_kept,
        out_away, grad_long_q,
    ) = fence(
        grad_combined, grad_attended_bf, gate_moved, up_core, up_away, long_kept, long_away, out_kept,
        out_away, grad_long_q,
    )

    up_moved = swap_inner(grid, up_away)
    long_core = grid.send(long_away, core=1)
    out_core = grid.send(out_away, core=1)
    gate_total = inner_total(grid, gate_kept, gate_core, gate_moved)
    grad_combined, gate_total = fence(grad_combined, gate_total)
    gate_sum = sum_outer(grid, gate_total)
    grad_cross_bf = (gate_tanh * grad_combined).astype(bf16)
    own_gate_grad = jnp.sum(
        jnp.sum(grad_combined * cross_out, axis=0).reshape(own_heads, HD), axis=1
    ) * (1.0 - jnp.tanh(own_gates) ** 2)
    grad_query, grad_text_key, grad_text_value = attend_call(
        "attend_cross_back", clip_column, cross_seen, query_bf, text_key_bf, text_value_bf, 0,
        (grad_cross_bf, cross_out, cross_lse),
    )
    grad_tkey, text_gain_grad = head_call(
        norm_heads_back, "norm_text_back", text_raw, 0, text_gain, text_turns, (grad_text_key,)
    )
    grad_tval = grad_text_value.astype(bf16)
    tkey_kept = contract_rows(feats[:, :half_text], grad_tkey).astype(bf16)
    tkey_away = contract_rows(feats[:, half_text:], grad_tkey).astype(bf16)
    long_away = core_away(grid, long_kept, long_core)
    out_away = core_away(grid, out_kept, out_core)
    (
        gate_sum, down_sum, up_moved, long_core, long_away, out_core, out_away, grad_query, grad_tkey,
        grad_tval, tkey_kept, tkey_away, grad_attended_bf,
    ) = fence(
        gate_sum, down_sum, up_moved, long_core, long_away, out_core, out_away, grad_query, grad_tkey,
        grad_tval, tkey_kept, tkey_away, grad_attended_bf,
    )

    long_moved = swap_inner(grid, long_away)
    out_moved = swap_inner(grid, out_away)
    tkey_core = grid.send(tkey_away, core=1)
    down_grad = down_sum.astype(f32)
    gate_grad = gate_sum.astype(f32)
    up_total = inner_total(grid, up_kept, up_core, up_moved)
    grad_attended_bf, up_total = fence(grad_attended_bf, up_total)
    up_sum = sum_outer(grid, up_total)
    grad_short_bf = grad_attended_bf[LONG_DEV:]
    grad_short_q, grad_short_k, grad_short_v = attend_call(
        "attend_short_back", short_clip, short_seen, short_query, short_key, short_value, 0,
        (grad_short_bf, short_out, short_lse),
    )
    tval_kept = contract_rows(feats[:, :half_text], grad_tval).astype(bf16)
    tval_away = contract_rows(feats[:, half_text:], grad_tval).astype(bf16)
    null_flags = jnp.concatenate([own_null, null_mask[clip_total - 1 :] == 1]).astype(f32)
    row_ids = jnp.arange(text_rows, dtype=jnp.int32)
    null_chosen = jnp.where(
        row_ids[None, :] % TXT_LEN == jnp.arange(TXT_LEN, dtype=jnp.int32)[:, None],
        jnp.repeat(null_flags, TXT_LEN)[None, :],
        0.0,
    ).astype(bf16)
    null_rows = jnp.concatenate(
        [dot(null_chosen, grad_tkey), dot(null_chosen, grad_tval)], axis=1
    ).astype(bf16)
    tkey_away = core_away(grid, tkey_kept, tkey_core)
    (
        up_sum, long_moved, out_moved, tkey_core, tkey_away, tval_kept, tval_away, grad_short_q,
        grad_short_k, grad_short_v, null_rows,
    ) = fence(
        up_sum, long_moved, out_moved, tkey_core, tkey_away, tval_kept, tval_away, grad_short_q,
        grad_short_k, grad_short_v, null_rows,
    )

    tkey_moved = swap_inner(grid, tkey_away)
    tval_core = grid.send(tval_away, core=1)
    null_moved = pair_sum(grid, null_rows, 1)
    up_grad = up_sum.astype(f32)
    both_total = join_sums(
        grid,
        [long_kept, long_core] + long_moved,
        [out_kept, out_core] + out_moved,
        LONG_DEV,
        depth,
    )
    both_sum = sum_outer(grid, both_total)
    grad_query_raw, query_gain_grad = head_call(
        norm_heads_back, "norm_queries_back", projected, 0, query_gain, turns,
        (grad_query, jnp.concatenate([grad_long_q, grad_short_q], axis=0)),
    )
    res_sums, attn_sums = row_call(
        sum_rows,
        "sum_rows",
        [clip_column, residual, ffn_in_part, ffn_in_moved, grad_residual, attn_part, attn_moved],
        [own_tanhs[0]],
        [],
        2,
    )
    tval_away = core_away(grid, tval_kept, tval_core)
    (
        both_sum, tkey_moved, tval_core, tval_away, null_moved, grad_query_raw, grad_short_k,
        grad_short_v, query_gain_grad, res_sums, attn_sums,
    ) = fence(
        both_sum, tkey_moved, tval_core, tval_away, null_moved, grad_query_raw, grad_short_k,
        grad_short_v, query_gain_grad, res_sums, attn_sums,
    )

    tval_moved = swap_inner(grid, tval_away)
    null_rows = null_rows + null_moved
    null_moved = pair_sum(grid, null_rows, 2)
    out_grad = both_sum[2 * LONG_DEV :].astype(f32)
    tkey_total = inner_total(grid, tkey_kept, tkey_core, tkey_moved)
    both_sum, tkey_total = fence(both_sum, tkey_total)
    tkey_sum = sum_outer(grid, tkey_total)
    own_terms = both_sum[: 2 * LONG_DEV].astype(f32)
    grad_key = jnp.concatenate([own_terms[:LONG_DEV], grad_short_k], axis=0)
    grad_value = jnp.concatenate([own_terms[LONG_DEV:], grad_short_v], axis=0)
    grad_key_raw, key_gain_grad = head_call(
        norm_heads_back, "norm_keys_back", projected, 1, key_gain, turns, (grad_key,)
    )
    grad_proj_bf = jnp.concatenate(
        [grad_query_raw, grad_key_raw, grad_value.astype(bf16)], axis=1
    )
    normed_part = rounded(
        jnp.concatenate(
            [contract_cols(grad_proj_bf, qkv_own), contract_cols(grad_proj_bf, qkv_other)], axis=1
        )
    ).astype(bf16)
    qkv_kept = contract_rows(normed_in[:, :half_width], grad_proj_bf).astype(bf16)
    qkv_away = contract_rows(normed_in[:, half_width:], grad_proj_bf).astype(bf16)
    first_rows = token_count // 2
    moved_first = swap_txt(normed_part[:first_rows])
    moved_last = swap_txt(normed_part[first_rows:])
    qkv_core = grid.send(qkv_away, core=1)
    qkv_away = core_away(grid, qkv_kept, qkv_core)
    (
        tkey_sum, tval_moved, null_moved, moved_first, qkv_kept, qkv_core, qkv_away, grad_residual,
    ) = fence(
        tkey_sum, tval_moved, null_moved, moved_first, qkv_kept, qkv_core, qkv_away, grad_residual,
    )

    qkv_moved = swap_inner(grid, qkv_away)
    null_rows = null_rows + null_moved
    tval_total = inner_total(grid, tval_kept, tval_core, tval_moved)
    tval_total, null_rows, moved_first, grad_residual = fence(
        tval_total, null_rows, moved_first, grad_residual
    )
    tval_sum = sum_outer(grid, tval_total)
    null_rows = null_rows + pair_sum(grid, null_rows, 4)
    null_moved = pair_sum(grid, null_rows, 8)
    normed_moved = jnp.concatenate([moved_first, moved_last], axis=0)
    video_high, video_low, hidden_sums = row_call(
        last_rows,
        "last_rows",
        [clip_column, hidden, normed_part, normed_moved, grad_residual],
        [own_scales[0], gains],
        [bf16, bf16],
        1,
    )
    hidden_sums, tval_sum, qkv_moved, null_rows, null_moved = fence(
        hidden_sums, tval_sum, qkv_moved, null_rows, null_moved
    )

    text_grad = jnp.stack([tkey_sum.astype(f32), tval_sum.astype(f32)], axis=1)
    qkv_total = inner_total(grid, qkv_kept, qkv_core, qkv_moved)
    hidden_sums, qkv_total = fence(hidden_sums, qkv_total)
    qkv_sum = sum_outer(grid, qkv_total)

    grad_mod = jnp.stack(
        [
            hidden_sums * gains[0],
            attn_sums * gains[1] * (1.0 - own_tanhs[0] * own_tanhs[0]),
            res_sums * gains[2],
            ffn_sums * gains[3] * (1.0 - own_tanhs[1] * own_tanhs[1]),
        ],
        axis=1,
    ).reshape(-1, model_width)
    gain_rows = jnp.stack(
        [
            jnp.sum(hidden_sums * own_scales[0], axis=0),
            jnp.sum(attn_sums * own_tanhs[0], axis=0),
            jnp.sum(res_sums * own_scales[1], axis=0),
            jnp.sum(ffn_sums * own_tanhs[1], axis=0),
        ],
        axis=0,
    )
    rows = contract_cols(
        jnp.concatenate(split_three(jnp.concatenate([grad_mod, gain_rows], axis=0)), axis=0),
        one_hot,
    )
    row_count = rows.shape[0] // 3
    rows = rows[:row_count] + rows[row_count : 2 * row_count] + rows[2 * row_count :]
    gain_rows = rows[-4:]
    own_grad_mod = rows[:-4].reshape(short_clips + 1, 4 * model_width)
    column_count = mod_part.shape[1]
    mod_blocks = lax.dynamic_index_in_dim(
        own_grad_mod.reshape(short_clips + 1, seq_count, 2, column_count),
        txt_index,
        2,
        keepdims=False,
    )
    mod_blocks = turn_seq(grid, jnp.transpose(mod_blocks, (1, 0, 2)))
    null_rows = sum_seq(grid, null_rows + null_moved, 16)
    null_part = jnp.concatenate(
        [
            contract_cols(null_rows[:, :own_width], key_piece)
            + contract_cols(null_rows[:, own_width:], value_piece)
            for key_piece, value_piece in zip(tkey_pieces, tval_pieces)
        ],
        axis=1,
    )
    null_part = rounded(null_part).astype(bf16)
    null_moved = swap_txt(null_part)
    video_grad = contract_cols(video_high, one_hot) + contract_cols(video_low, one_hot)
    slice_grad_mod = jnp.concatenate(
        [
            mod_blocks[:, :short_clips].reshape(clip_total - 1, column_count),
            jnp.sum(mod_blocks[:, short_clips], axis=0, keepdims=True),
        ],
        axis=0,
    )
    ada_weight_grad = lax.dot_general(
        shifted.astype(f32), slice_grad_mod, (((0,), (0,)), ((), ())), precision=highest
    )
    ada_bias_grad = jnp.sum(slice_grad_mod, axis=0)
    grad_shifted = lax.dot_general(
        slice_grad_mod, ada_weight.astype(f32), (((1,), (1,)), ((), ())), precision=highest
    )
    cond_value = condition.astype(f32)
    cond_sigmoid = jax.nn.sigmoid(cond_value)
    cond_part = grad_shifted * cond_sigmoid * (1.0 + cond_value * (1.0 - cond_sigmoid))

    head_rows = [
        lax.dynamic_update_slice(jnp.zeros((1, model_width), f32), rows, (0, head_start * HD))
        for rows in (query_gain_grad, key_gain_grad, text_gain_grad)
    ]
    gains_term = jnp.concatenate([jnp.where(first_half, gain_rows, 0.0)] + head_rows, axis=0)
    gates_term = lax.dynamic_update_slice_in_dim(jnp.zeros((H,), f32), own_gate_grad, head_start, 0)
    cond_count, gains_count = cond_part.size, gains_term.size
    packed = jnp.concatenate([cond_part.reshape(-1), gains_term.reshape(-1), gates_term])
    packed = jnp.pad(packed, (0, -packed.shape[0] % 1024)).reshape(-1, 1024)
    packed = packed + pair_sum(grid, packed, 1)
    packed = packed + pair_sum(grid, packed, 2)
    packed = packed + swap_txt(packed)
    packed, qkv_sum = fence(packed, qkv_sum)
    packed = packed + pair_sum(grid, packed, 4)
    packed, null_moved = fence(packed, null_moved)
    null_grad = reorder_columns(
        null_part.astype(f32) + null_moved.astype(f32), owners, False
    )
    qkv_grad = qkv_sum.astype(f32).reshape(depth, 3, own_width)
    packed = sum_seq(grid, packed, 8)
    packed = packed.reshape(-1)
    condition_grad = packed[:cond_count].reshape(cond_part.shape)
    norm_gains_grad = packed[cond_count : cond_count + gains_count].reshape(gains_term.shape)
    head_gates_grad = packed[cond_count + gains_count : cond_count + gains_count + H]
    return (
        block_out,
        video_grad,
        condition_grad,
        qkv_grad,
        out_grad,
        gate_grad,
        up_grad,
        down_grad,
        text_grad,
        ada_weight_grad,
        ada_bias_grad,
        null_grad,
        norm_gains_grad,
        head_gates_grad,
    )


def solution(mesh):
    placed = (
        P("seq", None),
        P("seq", None),
        P(),
        P("seq", "txt", None),
        P("txt", None),
        P("txt", None),
        P("seq", None, "txt"),
        P("seq", "txt"),
        P("seq", "txt"),
        P("seq", "txt"),
        P("seq", "txt"),
        P("seq", None, "txt"),
        P(None, ("seq", "txt")),
        P(("seq", "txt")),
        P(),
        P(),
        P("seq", None),
        P(),
        P(),
    )
    return jax.shard_map(
        local,
        mesh=mesh,
        in_specs=placed,
        out_specs=(
            P("seq", None),
            P("seq", None),
            P(),
            P("seq", None, "txt"),
            P("seq", "txt"),
            P("seq", "txt"),
            P("seq", "txt"),
            P("seq", "txt"),
            P("seq", None, "txt"),
            P(None, ("seq", "txt")),
            P(("seq", "txt")),
            P(),
            P(),
            P(),
        ),
        check_vma=False,
    )
```

```python
import functools
import math

import jax
import jax.numpy as jnp
from jax import lax
from jax.experimental import pallas as pl
from jax.experimental.pallas import tpu as pltpu
from jax.sharding import PartitionSpec as P

H = 24
HD = 64
TXT_LEN = 64
LONG_DEV = 64

epsilon = 1e-05
negative = -1e30
highest = lax.Precision.HIGHEST
bf16 = jnp.bfloat16
f32 = jnp.float32


def layout(lengths_row, seq_index, long_rows, short_rows):
    clip_count = lengths_row.shape[0]
    clip_ends = jnp.cumsum(lengths_row)
    clip_starts = clip_ends - lengths_row
    row_ids = jnp.arange(short_rows, dtype=jnp.int32)
    local_clip = jnp.sum(
        (row_ids[:, None] >= clip_ends[None, : clip_count - 1]).astype(jnp.int32), axis=1
    )
    chosen = local_clip[:, None] == jnp.arange(clip_count, dtype=jnp.int32)[None, :]
    clip_begin = jnp.sum(jnp.where(chosen, clip_starts[None, :], 0), axis=1)
    clip_local = jnp.concatenate([jnp.full((long_rows,), clip_count, jnp.int32), local_clip])
    long_place = seq_index * long_rows + jnp.arange(long_rows, dtype=jnp.int32)
    position = jnp.concatenate([long_place, row_ids - clip_begin])
    return (clip_local, position)


def rms_parts(values):
    inverse = lax.rsqrt(jnp.mean(values * values, axis=-1, keepdims=True) + epsilon)
    return (values * inverse, inverse)


def rms_back(grad_hat, normed, inverse):
    return inverse * (grad_hat - normed * jnp.mean(grad_hat * normed, axis=-1, keepdims=True))


def dot(left_side, right_side):
    return jnp.dot(left_side, right_side, preferred_element_type=f32)


def dot_pieces(left_side, pieces):
    depth = pieces[0].shape[0]
    total = 0.0
    for place, piece in enumerate(pieces):
        total = total + dot(left_side[:, place * depth : (place + 1) * depth], piece)
    return total


def contract_rows(left_side, right_side):
    return lax.dot_general(
        left_side, right_side, (((0,), (0,)), ((), ())), preferred_element_type=f32
    )


def contract_cols(left_side, right_side):
    return lax.dot_general(
        left_side, right_side, (((1,), (1,)), ((), ())), preferred_element_type=f32
    )


def swap_txt(values):
    return lax.ppermute(values, "txt", [(0, 1), (1, 0)])


def rounded(values):
    return lax.reduce_precision(values, exponent_bits=8, mantissa_bits=7)


def fence(*values):
    return lax.optimization_barrier(values)


class Grid:
    def __init__(self):
        self.count = lax.axis_size("seq")
        self.outer_count = 4
        self.inner_count = self.count // 8
        self.index = lax.axis_index("seq")
        self.core = self.index % 2
        self.inner = (self.index // 2) % self.inner_count
        self.outer = self.index // (2 * self.inner_count)

    def send(self, values, outer=0, inner=0, core=0):
        pairs = []
        for index in range(self.count):
            to_core = (index + core) % 2
            to_inner = (index // 2 + inner) % self.inner_count
            to_outer = (index // (2 * self.inner_count) + outer) % self.outer_count
            pairs.append((index, (to_outer * self.inner_count + to_inner) * 2 + to_core))
        return lax.ppermute(values, "seq", pairs)

    def lines(self):
        step = 2 * self.inner_count
        return [[first + step * k for k in range(self.outer_count)] for first in range(step)]

    def owners(self):
        place = jnp.arange(self.count, dtype=jnp.int32)
        outer = place % self.outer_count
        inner = (self.inner - (place // self.outer_count) % self.inner_count) % self.inner_count
        core = (self.core + place // (self.outer_count * self.inner_count)) % 2
        return (outer * self.inner_count + inner) * 2 + core


def gather_outer(grid, block):
    return lax.all_gather(block, "seq", axis=0, tiled=True, axis_index_groups=grid.lines())


def send_inner(grid, near):
    return [grid.send(near, inner=step) for step in range(1, grid.inner_count)]


def send_core(grid, pieces):
    return [grid.send(piece, core=1) for piece in pieces]


def stack(pieces):
    return jnp.concatenate(pieces, axis=0) if len(pieces) > 1 else pieces[0]


def add_blocks(*refs):
    *sources, target = refs
    total = sources[0][...].astype(f32)
    for source in sources[1:]:
        total = total + source[...].astype(f32)
    target[...] = total.astype(target.dtype)


def add_rows(arrays, starts, rows):
    cols = arrays[0].shape[1]
    block = 256 if rows % 256 == 0 else 128 if rows % 128 == 0 else rows

    def from_row(start):
        return pl.BlockSpec((block, cols), lambda i: (start // block + i, 0))

    return pl.pallas_call(
        add_blocks,
        grid=(rows // block,),
        in_specs=[from_row(start) for start in starts],
        out_specs=from_row(0),
        out_shape=jax.ShapeDtypeStruct((rows, cols), bf16),
        cost_estimate=pl.CostEstimate(flops=1, bytes_accessed=1, transcendentals=0),
        compiler_params=pltpu.CompilerParams(vmem_limit_bytes=48 * 1024 * 1024),
        name="add_rows",
    )(*arrays)


def join_blocks(*refs):
    *sources, target = refs
    half = len(sources) // 2
    totals = []
    for part in (sources[:half], sources[half:]):
        total = part[0][...].astype(f32)
        for source in part[1:]:
            total = total + source[...].astype(f32)
        totals.append(total.astype(bf16))
    rows, width = totals[0].shape[0], totals[1].shape[1]
    target[0, :rows, :] = totals[0][:, :width]
    target[0, rows : 2 * rows, :] = totals[0][:, width:]
    target[0, 2 * rows :, :] = totals[1]


def join_sums(grid, long_parts, out_parts, long_rows, out_rows):
    width = out_parts[0].shape[1]
    rows = 2 * long_rows + out_rows
    long_spec = pl.BlockSpec((long_rows, 2 * width), lambda i: (i, 0))
    out_spec = pl.BlockSpec((out_rows, width), lambda i: (i, 0))
    joined = pl.pallas_call(
        join_blocks,
        grid=(grid.outer_count,),
        in_specs=[long_spec] * len(long_parts) + [out_spec] * len(out_parts),
        out_specs=pl.BlockSpec((1, rows, width), lambda i: (i, 0, 0)),
        out_shape=jax.ShapeDtypeStruct((grid.outer_count, rows, width), bf16),
        cost_estimate=pl.CostEstimate(flops=1, bytes_accessed=1, transcendentals=0),
        name="join_sums",
    )(*long_parts, *out_parts)
    return joined.reshape(grid.outer_count * rows, width)


def core_away(grid, kept, moved):
    rows = kept.shape[0] // grid.inner_count
    return [
        add_rows([kept, moved], [step * rows] * 2, rows) for step in range(1, grid.inner_count)
    ]


def inner_total(grid, kept, moved, arrived):
    rows = kept.shape[0] // grid.inner_count
    return add_rows([kept, moved] + arrived, [0] * (2 + len(arrived)), rows)


def swap_inner(grid, away):
    return [grid.send(part, inner=-step) for step, part in enumerate(away, 1)]


def sum_outer(grid, total):
    return lax.psum_scatter(
        total, "seq", scatter_dimension=0, tiled=True, axis_index_groups=grid.lines()
    )


def pair_sum(grid, values, bit):
    pairs = [(index, index ^ bit) for index in range(grid.count)]
    return lax.ppermute(values, "seq", pairs)


def turn_stage(values, axis, size, own, send):
    moved = [lax.dynamic_index_in_dim(values, own, axis, keepdims=False)]
    for step in range(1, size):
        piece = lax.dynamic_index_in_dim(values, (own + step) % size, axis, keepdims=False)
        moved.append(send(piece, step))
    stacked = jnp.stack(moved, axis=axis)
    order = (own - jnp.arange(size, dtype=jnp.int32)) % size
    return jnp.take(stacked, order, axis=axis)


def turn_seq(grid, values):
    rest = values.shape[1:]
    values = values.reshape((grid.outer_count, grid.inner_count, 2) + rest)
    values = turn_stage(
        values, 0, grid.outer_count, grid.outer, lambda v, k: grid.send(v, outer=k)
    )
    values = turn_stage(
        values, 1, grid.inner_count, grid.inner, lambda v, k: grid.send(v, inner=k)
    )
    values = turn_stage(values, 2, 2, grid.core, lambda v, k: grid.send(v, core=k))
    return values.reshape((grid.count,) + rest)


def sum_seq(grid, values, bit):
    while bit < grid.count:
        values = values + pair_sum(grid, values, bit)
        bit *= 2
    return values


def copy_blocks(to_order, count, order_ref, source_ref, target_ref):
    width = source_ref.shape[1] // count
    for block in range(count):
        moved = pl.ds(pl.multiple_of(order_ref[block] * width, width), width)
        plain = pl.ds(block * width, width)
        if to_order:
            target_ref[:, plain] = source_ref[:, moved]
        else:
            target_ref[:, moved] = source_ref[:, plain]


def reorder_columns(values, order, to_order):
    rows, cols = values.shape
    count = order.shape[0]
    width = cols // count
    if width % 128:
        taken = order if to_order else jnp.argsort(order)
        return jnp.take(values.reshape(rows, count, width), taken, axis=1).reshape(rows, cols)
    return pl.pallas_call(
        functools.partial(copy_blocks, to_order, count),
        out_shape=jax.ShapeDtypeStruct(values.shape, values.dtype),
        in_specs=[
            pl.BlockSpec(memory_space=pltpu.SMEM),
            pl.BlockSpec(memory_space=pltpu.VMEM),
        ],
        out_specs=pl.BlockSpec(memory_space=pltpu.VMEM),
        name="reorder_columns",
    )(order, values)


def split_three(values):
    high = rounded(values)
    rest = values - high
    middle = rounded(rest)
    return high.astype(bf16), middle.astype(bf16), (rest - middle).astype(bf16)


def exact_dot(values, one_hot):
    rows = values.shape[0]
    parts = dot(jnp.concatenate(split_three(values), axis=0), one_hot)
    return parts[:rows] + parts[rows : 2 * rows] + parts[2 * rows :]


def choose(clip, rows):
    chosen = rows[-1:]
    for index in range(rows.shape[0] - 1):
        chosen = jnp.where(clip == index, rows[index : index + 1], chosen)
    return chosen


def add_clip_sums(clip, values, sums_ref):
    @pl.when(pl.program_id(0) == 0)
    def _():
        sums_ref[...] = jnp.zeros_like(sums_ref)

    for index in range(sums_ref.shape[0]):
        part = jnp.sum(jnp.where(clip == index, values, 0.0), axis=0, keepdims=True)
        sums_ref[index : index + 1, :] += part


def add_pair(own_ref, moved_ref):
    return own_ref[...].astype(f32) + moved_ref[...].astype(f32)


def enter_rows(clip_ref, hidden_ref, part_ref, moved_ref, tanh_ref, scale_ref, gains_ref, res_ref, in_ref):
    clip = clip_ref[...]
    attn_hat, _ = rms_parts(add_pair(part_ref, moved_ref))
    tanh_tok = choose(clip, tanh_ref[...])
    residual = hidden_ref[...].astype(f32) + tanh_tok * attn_hat * gains_ref[1:2]
    res_hat, _ = rms_parts(residual)
    res_ref[...] = residual
    in_ref[...] = (res_hat * gains_ref[2:3] * choose(clip, scale_ref[...])).astype(bf16)


def leave_rows(clip_ref, part_ref, moved_ref, up_ref, tanh_ref, gains_ref, grad_ref):
    hat, inverse = rms_parts(add_pair(part_ref, moved_ref))
    grad_hat = up_ref[...].astype(f32) * choose(clip_ref[...], tanh_ref[...]) * gains_ref[3:4]
    grad_ref[...] = rms_back(grad_hat, hat, inverse).astype(bf16)


def block_rows(clip_ref, res_ref, part_ref, moved_ref, up_ref, tanh_ref, gains_ref, out_ref, sums_ref):
    clip = clip_ref[...]
    hat, _ = rms_parts(add_pair(part_ref, moved_ref))
    out_ref[...] = (res_ref[...] + choose(clip, tanh_ref[...]) * hat * gains_ref[3:4]).astype(bf16)
    add_clip_sums(clip, up_ref[...].astype(f32) * hat, sums_ref)


def middle_rows(
    clip_ref, res_ref, grad_part_ref, grad_moved_ref, up_ref, part_ref, moved_ref, tanh_ref,
    scale_ref, gains_ref, grad_res_ref, grad_attn_ref,
):
    clip = clip_ref[...]
    hat, inverse = rms_parts(res_ref[...])
    grad_hat = add_pair(grad_part_ref, grad_moved_ref) * gains_ref[2:3]
    grad_hat = grad_hat * choose(clip, scale_ref[...])
    grad_res = up_ref[...].astype(f32) + rms_back(grad_hat, hat, inverse)
    grad_res_ref[...] = grad_res
    hat, inverse = rms_parts(add_pair(part_ref, moved_ref))
    grad_hat = grad_res * gains_ref[1:2] * choose(clip, tanh_ref[...])
    grad_attn_ref[...] = rms_back(grad_hat, hat, inverse).astype(bf16)


def sum_rows(
    clip_ref, res_ref, grad_part_ref, grad_moved_ref, grad_res_ref, part_ref, moved_ref, _,
    res_sums_ref, attn_sums_ref,
):
    clip = clip_ref[...]
    hat, _ = rms_parts(res_ref[...])
    add_clip_sums(clip, add_pair(grad_part_ref, grad_moved_ref) * hat, res_sums_ref)
    hat, _ = rms_parts(add_pair(part_ref, moved_ref))
    add_clip_sums(clip, grad_res_ref[...] * hat, attn_sums_ref)


def last_rows(
    clip_ref, hidden_ref, part_ref, moved_ref, grad_res_ref, scale_ref, gains_ref, high_ref, low_ref,
    sums_ref,
):
    clip = clip_ref[...]
    grad = add_pair(part_ref, moved_ref)
    hat, inverse = rms_parts(hidden_ref[...].astype(f32))
    add_clip_sums(clip, grad * hat, sums_ref)
    grad_hat = grad * gains_ref[0:1] * choose(clip, scale_ref[...])
    total = grad_res_ref[...] + rms_back(grad_hat, hat, inverse)
    high = total.astype(bf16)
    high_ref[...] = high
    low_ref[...] = (total - high.astype(f32)).astype(bf16)


def row_call(body, name, arrays, tables, outs, sums):
    count, width = arrays[1].shape
    rows = count // 4

    def by_rows(array):
        return pl.BlockSpec((rows, array.shape[1]), lambda i: (i, 0))

    def whole(array):
        return pl.BlockSpec(array.shape, lambda i: (0, 0))

    out_shapes = [jax.ShapeDtypeStruct((count, width), kind) for kind in outs]
    sum_shapes = [jax.ShapeDtypeStruct((tables[0].shape[0], width), f32)] * sums
    return pl.pallas_call(
        body,
        grid=(4,),
        in_specs=[by_rows(array) for array in arrays] + [whole(table) for table in tables],
        out_specs=[by_rows(shape) for shape in out_shapes] + [whole(shape) for shape in sum_shapes],
        out_shape=out_shapes + sum_shapes,
        cost_estimate=pl.CostEstimate(flops=1, bytes_accessed=1, transcendentals=0),
        compiler_params=pltpu.CompilerParams(vmem_limit_bytes=48 * 1024 * 1024),
        name=name,
    )(*arrays, *tables)


def head_means(values):
    first = lax.broadcasted_iota(jnp.int32, values.shape, 1) < HD
    front = jnp.sum(jnp.where(first, values, 0.0), axis=1, keepdims=True)
    back = jnp.sum(jnp.where(first, 0.0, values), axis=1, keepdims=True)
    return jnp.where(first, front, back) * (1.0 / HD)


def turn_lanes(values, cosine, sine):
    lane = lax.broadcasted_iota(jnp.int32, values.shape, 1) % HD
    ahead = pltpu.roll(values, 2 * HD - HD // 2, 1)
    behind = pltpu.roll(values, HD // 2, 1)
    return values * cosine + jnp.where(lane < HD // 2, -ahead, behind) * sine


def norm_heads(values_ref, gain_ref, cos_ref, sin_ref, out_ref):
    cosine, sine = cos_ref[...], sin_ref[...]
    for start in range(0, out_ref.shape[1], 2 * HD):
        part = slice(start, start + 2 * HD)
        values = values_ref[:, part]
        hat = values * lax.rsqrt(head_means(values * values) + epsilon)
        out_ref[:, part] = turn_lanes(hat * gain_ref[:, part], cosine, sine).astype(bf16)


def norm_heads_back(*refs):
    values_ref, gain_ref, cos_ref, sin_ref, *grad_refs, out_ref, sums_ref = refs
    cosine, sine = cos_ref[...], sin_ref[...]

    @pl.when(pl.program_id(0) == 0)
    def _():
        sums_ref[...] = jnp.zeros_like(sums_ref)

    for start in range(0, out_ref.shape[1], 2 * HD):
        part = slice(start, start + 2 * HD)
        values = values_ref[:, part]
        inverse = lax.rsqrt(head_means(values * values) + epsilon)
        hat = values * inverse
        grad = grad_refs[0][:, part]
        for grad_ref in grad_refs[1:]:
            grad = grad + grad_ref[:, part]
        grad = turn_lanes(grad, cosine, -sine)
        sums_ref[:, part] += jnp.sum(grad * hat, axis=0, keepdims=True)
        grad = grad * gain_ref[:, part]
        out_ref[:, part] = (inverse * (grad - hat * head_means(grad * hat))).astype(bf16)


def head_call(body, name, values, column, gain, turns, grads=()):
    count, width = turns[0].shape[0], gain.shape[1]
    rows = count // 4
    by_rows = pl.BlockSpec((rows, width), lambda i: (i, 0))
    whole = pl.BlockSpec((1, width), lambda i: (0, 0))
    turn = pl.BlockSpec((rows, 2 * HD), lambda i: (i, 0))
    out_shape = [jax.ShapeDtypeStruct((count, width), bf16)]
    out_specs = [by_rows]
    if grads:
        out_shape.append(jax.ShapeDtypeStruct((1, width), f32))
        out_specs.append(whole)
    results = pl.pallas_call(
        body,
        grid=(4,),
        in_specs=[pl.BlockSpec((rows, width), lambda i: (i, column)), whole, turn, turn]
        + [by_rows] * len(grads),
        out_specs=out_specs,
        out_shape=out_shape,
        cost_estimate=pl.CostEstimate(flops=1, bytes_accessed=1, transcendentals=0),
        compiler_params=pltpu.CompilerParams(vmem_limit_bytes=48 * 1024 * 1024),
        name=name,
    )(values, gain, *turns, *grads)
    return results if grads else results[0]


def attend_heads(clip_ref, key_clip_ref, query_ref, key_ref, value_ref, out_ref, total_ref):
    visible = clip_ref[...] == key_clip_ref[...]
    for start in range(0, 2 * HD, HD):
        head = slice(start, start + HD)
        scores = contract_cols(query_ref[:, head], key_ref[:, head]) * HD ** (-0.5)
        scores = jnp.where(visible, scores, negative)
        peak = jnp.max(scores, axis=1, keepdims=True)
        exponent = jnp.exp(scores - peak)
        total = jnp.sum(exponent, axis=1, keepdims=True)
        out_ref[:, head] = dot((exponent / total).astype(bf16), value_ref[:, head])
        total_ref[:, head] = jnp.broadcast_to(peak + jnp.log(total), (total_ref.shape[0], HD))


def attend_heads_back(
    clip_ref, key_clip_ref, query_ref, key_ref, value_ref, grad_ref, out_ref, total_ref,
    grad_query_ref, grad_key_ref, grad_value_ref,
):
    visible = clip_ref[...] == key_clip_ref[...]
    for start in range(0, 2 * HD, HD):
        head = slice(start, start + HD)
        query, key = query_ref[:, head], key_ref[:, head]
        grad = grad_ref[:, head]
        scores = contract_cols(query, key) * HD ** (-0.5)
        weights = jnp.where(visible, jnp.exp(scores - total_ref[:, start : start + 1]), 0.0)
        delta = jnp.sum(grad.astype(f32) * out_ref[:, head], axis=1, keepdims=True)
        grad_scores = weights * (contract_cols(grad, value_ref[:, head]) - delta)
        grad_scores = grad_scores.astype(bf16)
        grad_query_ref[:, head] = dot(grad_scores, key) * HD ** (-0.5)
        grad_key = contract_rows(grad_scores, query) * HD ** (-0.5)
        grad_key_ref[:, head] = grad_key.astype(grad_key_ref.dtype)
        grad_value = contract_rows(weights.astype(bf16), grad)
        grad_value_ref[:, head] = grad_value.astype(grad_value_ref.dtype)


def attend_call(name, clips, key_clips, query, key, value, value_column=0, back=(), kind=f32):
    count, keys, width = query.shape[0], key.shape[0], query.shape[1]
    first = value_column // (2 * HD)
    queries = pl.BlockSpec((count, 2 * HD), lambda i: (0, i))
    seen = pl.BlockSpec((keys, 2 * HD), lambda i: (0, i))
    whole = [pl.BlockSpec(array.shape, lambda i: (0, 0)) for array in (clips, key_clips)]
    out_shape = [jax.ShapeDtypeStruct((count, width), f32)]
    if back:
        out_shape += [jax.ShapeDtypeStruct((keys, width), kind)] * 2
        out_specs = [queries, seen, seen]
    else:
        out_shape += out_shape
        out_specs = [queries, queries]
    return pl.pallas_call(
        attend_heads_back if back else attend_heads,
        grid=(width // (2 * HD),),
        in_specs=whole
        + [queries, seen, pl.BlockSpec((keys, 2 * HD), lambda i: (0, first + i))]
        + [queries] * len(back),
        out_specs=out_specs,
        out_shape=out_shape,
        cost_estimate=pl.CostEstimate(flops=1, bytes_accessed=1, transcendentals=0),
        compiler_params=pltpu.CompilerParams(vmem_limit_bytes=48 * 1024 * 1024),
        name=name,
    )(clips, key_clips, query, key, value, *back)


def local(
    video_tokens,
    cotangent,
    condition,
    captions,
    long_caption,
    null_embed,
    query_key_value,
    out_weight,
    gate_weight,
    up_weight,
    down_weight,
    text_weight,
    ada_weight,
    ada_bias,
    norm_gains,
    head_gates,
    clip_lengths,
    null_mask,
    text_lengths,
):
    grid = Grid()
    seq_index = grid.index
    seq_count = grid.count
    txt_index = lax.axis_index("txt")
    first_half = txt_index == 0
    token_count, model_width = video_tokens.shape
    depth = query_key_value.shape[0]
    text_depth, text_width = text_weight.shape[0], captions.shape[2]
    half_width = model_width // 2
    own_heads = query_key_value.shape[2] // HD
    own_width = own_heads * HD
    head_start = txt_index * own_heads
    clip_total = condition.shape[0]
    short_clips = clip_lengths.shape[1]
    clip_local, position = layout(clip_lengths[0], seq_index, LONG_DEV, token_count - LONG_DEV)
    owners = grid.owners()
    text_rows = (short_clips + 1) * TXT_LEN

    half_text = text_width // 2
    text_block = text_weight.reshape(text_depth, 2 * own_width)

    qkv_block, condition = fence(query_key_value.reshape(depth, 3 * own_width), condition)
    qkv_near = gather_outer(grid, qkv_block)
    shifted = jax.nn.silu(condition.astype(f32)).astype(bf16)
    mod_part = dot(shifted, ada_weight) + ada_bias
    short_part = mod_part[: clip_total - 1].reshape(seq_count, short_clips, mod_part.shape[1])
    long_part = jnp.broadcast_to(
        mod_part[clip_total - 1 :][None], (seq_count, 1, mod_part.shape[1])
    )
    own_part = turn_seq(grid, jnp.concatenate([short_part, long_part], axis=1))
    other_part = swap_txt(own_part)
    own_null = lax.dynamic_slice_in_dim(null_mask, seq_index * short_clips, short_clips, 0) == 1
    short_feats = jnp.where(own_null[:, None, None], null_embed[None], captions)
    long_feats = jnp.where(null_mask[clip_total - 1] == 1, null_embed, long_caption)
    own_feats = jnp.concatenate([short_feats, long_feats[None]], axis=0).reshape(-1, text_width)
    own_feats = reorder_columns(own_feats, owners, True)

    columns = jnp.arange(model_width, dtype=jnp.int32)
    column_order = jnp.repeat(owners, depth) * depth + columns % depth
    one_hot = (columns[:, None] == column_order[None, :]).astype(bf16)
    hidden = dot(video_tokens, one_hot).astype(bf16)
    hidden_hat, _ = rms_parts(hidden.astype(f32))
    clip_column = clip_local[:, None]
    tkey_block, tval_block = text_block[:, :own_width], text_block[:, own_width:]
    qkv_near, own_part, other_part, own_feats, tkey_block, tval_block, out_weight = fence(
        qkv_near, own_part, other_part, own_feats, tkey_block, tval_block, out_weight
    )

    qkv_y = send_inner(grid, qkv_near)
    qkv_near_core = send_core(grid, [qkv_near])
    tkey_near = gather_outer(grid, tkey_block)
    out_near = gather_outer(grid, out_weight)
    other_feats = swap_txt(own_feats)
    own_mod = jnp.stack(
        [jnp.where(first_half, own_part, other_part), jnp.where(first_half, other_part, own_part)],
        axis=1,
    )
    own_mod = jnp.transpose(own_mod, (2, 0, 1, 3)).reshape((short_clips + 1) * 4, model_width)
    rows = exact_dot(jnp.concatenate([own_mod, norm_gains[:4]], axis=0), one_hot)
    gains = rows[-4:]
    own_mod = rows[:-4].reshape(short_clips + 1, 4, model_width)
    own_scales = 1.0 + own_mod[:, 0], 1.0 + own_mod[:, 2]
    own_tanhs = jnp.tanh(own_mod[:, 1]), jnp.tanh(own_mod[:, 3])
    selector = clip_local[:, None] == jnp.arange(short_clips + 1, dtype=jnp.int32)[None, :]

    def per_token(rows):
        chosen = rows[short_clips:]
        for clip in range(short_clips):
            chosen = jnp.where(selector[:, clip : clip + 1], rows[clip : clip + 1], chosen)
        return chosen

    normed_in = (hidden_hat * gains[0] * per_token(own_scales[0])).astype(bf16)
    query_gain, key_gain, text_gain = [
        lax.dynamic_slice(norm_gains, (row, head_start * HD), (1, own_width)) for row in (4, 5, 6)
    ]
    frequency = jnp.exp(
        jnp.arange(HD // 2, dtype=f32) * (-math.log(10000.0) / (HD // 2))
    )
    angles = jnp.tile(position.astype(f32)[:, None] * frequency, (1, 4))
    turns = jnp.cos(angles), jnp.sin(angles)
    text_turns = jnp.ones((text_rows, 2 * HD), f32), jnp.zeros((text_rows, 2 * HD), f32)
    normed_in, other_feats, tkey_near, out_near, tval_block, qkv_near_core, qkv_y = fence(
        normed_in, other_feats, tkey_near, out_near, tval_block, qkv_near_core, qkv_y
    )

    tkey_y = send_inner(grid, tkey_near)
    tkey_near_core = send_core(grid, [tkey_near])
    out_near_core = send_core(grid, [out_near])
    tval_near = gather_outer(grid, tval_block)
    qkv_core, normed_in = fence(send_core(grid, qkv_y), normed_in)
    qkv_own, qkv_other = stack([qkv_near] + qkv_y), stack(qkv_near_core + qkv_core)
    projected = dot(normed_in[:, :half_width], qkv_own) + dot(normed_in[:, half_width:], qkv_other)
    query_bf = head_call(norm_heads, "norm_queries", projected, 0, query_gain, turns)
    key_bf = head_call(norm_heads, "norm_keys", projected, 1, key_gain, turns)
    value_bf = projected[:, 2 * own_width :].astype(bf16)
    long_block = jnp.concatenate([key_bf[:LONG_DEV], value_bf[:LONG_DEV]], axis=1)
    (
        query_bf, key_bf, value_bf, long_block, tkey_y, tkey_near_core, out_near, out_near_core,
        tval_near, gate_weight,
    ) = fence(
        query_bf, key_bf, value_bf, long_block, tkey_y, tkey_near_core, out_near, out_near_core,
        tval_near, gate_weight,
    )

    tail = long_block.size // gate_weight.shape[1]
    gate_near = gather_outer(
        grid, jnp.concatenate([gate_weight, long_block.reshape(tail, -1)], axis=0)
    )
    tval_y = send_inner(grid, tval_near)
    tval_near_core = send_core(grid, [tval_near])
    short_query = query_bf[LONG_DEV:]
    short_key = key_bf[LONG_DEV:]
    short_value = value_bf[LONG_DEV:]
    short_clip = clip_column[LONG_DEV:]
    short_seen = clip_local[LONG_DEV:][None, :]
    short_out, short_lse = attend_call(
        "attend_short", short_clip, short_seen, short_query, short_key, short_value
    )
    out_y = send_inner(grid, out_near)
    tkey_core = send_core(grid, tkey_y)
    feats = jnp.concatenate(
        [
            jnp.where(first_half, own_feats, other_feats).reshape(-1, TXT_LEN // 2, text_width),
            jnp.where(first_half, other_feats, own_feats).reshape(-1, TXT_LEN // 2, text_width),
        ],
        axis=1,
    ).reshape(text_rows, text_width)
    tval_y, tval_near_core, gate_near, tkey_core, out_y, up_weight, feats, short_out = fence(
        tval_y, tval_near_core, gate_near, tkey_core, out_y, up_weight, feats, short_out
    )

    gate_near = gate_near.reshape(grid.outer_count, depth + tail, -1)
    long_near = gate_near[:, depth:].reshape(-1, 2 * own_width)
    gate_near = gate_near[:, :depth].reshape(grid.outer_count * depth, -1)
    long_y = send_inner(grid, long_near)
    long_near_core = send_core(grid, [long_near])
    gate_y = send_inner(grid, gate_near)
    gate_near_core = send_core(grid, [gate_near])
    up_near = gather_outer(grid, up_weight)
    tval_core = send_core(grid, tval_y)
    long_core = send_core(grid, long_y)
    out_core = send_core(grid, out_y)
    tkey_pieces = [tkey_near] + tkey_y + tkey_near_core + tkey_core
    text_raw = dot_pieces(feats, tkey_pieces)
    text_key_bf = head_call(norm_heads, "norm_text", text_raw, 0, text_gain, text_turns)

    out_own, out_other = stack([out_near] + out_y), stack(out_near_core + out_core)
    long_pairs = stack([long_near] + long_y + long_near_core + long_core)
    long_count = long_pairs.shape[0]
    long_query = query_bf[:LONG_DEV]
    long_clip = clip_column[:LONG_DEV]
    long_seen = jnp.full((1, long_count), short_clips, jnp.int32)
    long_out, long_lse = attend_call(
        "attend_long", long_clip, long_seen, long_query, long_pairs, long_pairs, own_width
    )
    tval_pieces = [tval_near] + tval_y + tval_near_core + tval_core
    text_value_bf = dot_pieces(feats, tval_pieces).astype(bf16)
    key_clip = jnp.arange(text_rows, dtype=jnp.int32) // TXT_LEN
    key_place = jnp.arange(text_rows, dtype=jnp.int32) % TXT_LEN
    limits = jnp.concatenate(
        [
            lax.dynamic_slice_in_dim(text_lengths, seq_index * short_clips, short_clips, 0),
            text_lengths[clip_total - 1 :],
        ]
    )
    clip_match = key_clip[:, None] == jnp.arange(short_clips + 1, dtype=jnp.int32)[None, :]
    key_limit = jnp.sum(jnp.where(clip_match, limits[None, :], 0), axis=1)
    cross_seen = jnp.where(key_place < key_limit, key_clip, -1)[None, :]
    cross_out, cross_lse = attend_call(
        "attend_cross", clip_column, cross_seen, query_bf, text_key_bf, text_value_bf
    )
    attended = jnp.concatenate([long_out, short_out], axis=0)
    own_gates = lax.dynamic_slice_in_dim(head_gates, head_start, own_heads, 0)
    gate_tanh = jnp.repeat(jnp.tanh(own_gates), HD)[None, :]
    combined_bf = (attended + gate_tanh * cross_out).astype(bf16)
    attn_part = rounded(
        jnp.concatenate(
            [contract_cols(combined_bf, out_own), contract_cols(combined_bf, out_other)], axis=1
        )
    ).astype(bf16)
    attn_part, gate_y, gate_near_core, up_near, down_weight = fence(
        attn_part, gate_y, gate_near_core, up_near, down_weight
    )

    attn_moved = swap_txt(attn_part)
    up_y = send_inner(grid, up_near)
    up_near_core = send_core(grid, [up_near])
    down_near = gather_outer(grid, down_weight)
    gate_core = send_core(grid, gate_y)
    attn_moved, up_y, up_near_core, down_near, gate_core = fence(
        attn_moved, up_y, up_near_core, down_near, gate_core
    )

    down_y = send_inner(grid, down_near)
    down_near_core = send_core(grid, [down_near])
    up_core = send_core(grid, up_y)
    gate_own, gate_other = stack([gate_near] + gate_y), stack(gate_near_core + gate_core)
    residual, ffn_in_bf = row_call(
        enter_rows,
        "enter_rows",
        [clip_column, hidden, attn_part, attn_moved],
        [own_tanhs[0], own_scales[1], gains],
        [f32, bf16],
        0,
    )
    gate_value = dot(ffn_in_bf[:, :half_width], gate_own) + dot(
        ffn_in_bf[:, half_width:], gate_other
    )
    up_core, gate_value = fence(up_core, gate_value)
    up_own, up_other = stack([up_near] + up_y), stack(up_near_core + up_core)
    up_value = dot(ffn_in_bf[:, :half_width], up_own) + dot(ffn_in_bf[:, half_width:], up_other)
    inner_bf = (gate_value * jax.nn.sigmoid(gate_value) * up_value).astype(bf16)
    inner_bf, down_y, down_near_core = fence(inner_bf, down_y, down_near_core)

    down_core = send_core(grid, down_y)
    down_core, inner_bf, cotangent = fence(down_core, inner_bf, cotangent)
    down_own, down_other = stack([down_near] + down_y), stack(down_near_core + down_core)
    ffn_part = rounded(
        jnp.concatenate(
            [contract_cols(inner_bf, down_own), contract_cols(inner_bf, down_other)], axis=1
        )
    ).astype(bf16)
    ffn_part, gate_value, cotangent = fence(ffn_part, gate_value, cotangent)

    ffn_moved = swap_txt(ffn_part)
    upstream = dot(cotangent, one_hot).astype(bf16)
    sigmoid_gate = jax.nn.sigmoid(gate_value)
    silu_gate = gate_value * sigmoid_gate
    gate_slope = up_value * (sigmoid_gate * (1.0 + gate_value * (1.0 - sigmoid_gate)))
    ffn_moved, ffn_part, upstream, silu_gate, gate_slope = fence(
        ffn_moved, ffn_part, upstream, silu_gate, gate_slope
    )

    (grad_ffn_out,) = row_call(
        leave_rows,
        "leave_rows",
        [clip_column, ffn_part, ffn_moved, upstream],
        [own_tanhs[1], gains],
        [bf16],
        0,
    )
    down_kept = contract_rows(grad_ffn_out[:, :half_width], inner_bf).astype(bf16)
    down_away = contract_rows(grad_ffn_out[:, half_width:], inner_bf).astype(bf16)
    grad_ffn_out, down_away, down_kept = fence(grad_ffn_out, down_away, down_kept)

    down_core = grid.send(down_away, core=1)
    grad_inner = dot(grad_ffn_out[:, :half_width], down_own) + dot(
        grad_ffn_out[:, half_width:], down_other
    )
    grad_gate_bf = (grad_inner * gate_slope).astype(bf16)
    grad_up_bf = (grad_inner * silu_gate).astype(bf16)
    ffn_in_part = rounded(
        jnp.concatenate(
            [
                contract_cols(grad_gate_bf, gate_own) + contract_cols(grad_up_bf, up_own),
                contract_cols(grad_gate_bf, gate_other) + contract_cols(grad_up_bf, up_other),
            ],
            axis=1,
        )
    ).astype(bf16)
    gate_away = contract_rows(ffn_in_bf[:, half_width:], grad_gate_bf).astype(bf16)
    down_away = core_away(grid, down_kept, down_core)
    down_core, down_away, ffn_in_part, gate_away, grad_gate_bf, grad_up_bf = fence(
        down_core, down_away, ffn_in_part, gate_away, grad_gate_bf, grad_up_bf
    )

    ffn_in_moved = swap_txt(ffn_in_part)
    down_moved = swap_inner(grid, down_away)
    gate_core = grid.send(gate_away, core=1)
    gate_kept = contract_rows(ffn_in_bf[:, :half_width], grad_gate_bf).astype(bf16)
    up_kept = contract_rows(ffn_in_bf[:, :half_width], grad_up_bf).astype(bf16)
    up_away = contract_rows(ffn_in_bf[:, half_width:], grad_up_bf).astype(bf16)
    block_out, ffn_sums = row_call(
        block_rows,
        "block_rows",
        [clip_column, residual, ffn_part, ffn_moved, upstream],
        [own_tanhs[1], gains],
        [bf16],
        1,
    )
    block_out = contract_cols(block_out, one_hot).astype(bf16)
    gate_away = core_away(grid, gate_kept, gate_core)
    block_out, ffn_in_moved, down_moved, up_kept, gate_kept, gate_away = fence(
        block_out, ffn_in_moved, down_moved, up_kept, gate_kept, gate_away
    )

    down_total = inner_total(grid, down_kept, down_core, down_moved)
    gate_moved = swap_inner(grid, gate_away)
    up_core = grid.send(up_away, core=1)
    ffn_in_moved, down_total = fence(ffn_in_moved, down_total)
    down_sum = sum_outer(grid, down_total)
    grad_residual, grad_attn_bf = row_call(
        middle_rows,
        "middle_rows",
        [clip_column, residual, ffn_in_part, ffn_in_moved, upstream, attn_part, attn_moved],
        [own_tanhs[0], own_scales[1], gains],
        [f32, bf16],
        0,
    )
    grad_combined = dot(grad_attn_bf[:, :half_width], out_own) + dot(
        grad_attn_bf[:, half_width:], out_other
    )
    grad_attended_bf = grad_combined.astype(bf16)
    grad_long_bf = grad_attended_bf[:LONG_DEV]
    grad_long_q, *long_parts = attend_call(
        "attend_long_back", long_clip, long_seen, long_query, long_pairs, long_pairs, own_width,
        (grad_long_bf, long_out, long_lse), bf16,
    )
    long_terms = jnp.concatenate(long_parts, axis=1)
    long_kept, long_away = long_terms[: long_count // 2], long_terms[long_count // 2 :]
    out_kept = contract_rows(grad_attn_bf[:, :half_width], combined_bf).astype(bf16)
    out_away = contract_rows(grad_attn_bf[:, half_width:], combined_bf).astype(bf16)
    up_away = core_away(grid, up_kept, up_core)
    (
        grad_combined, grad_attended_bf, gate_moved, up_core, up_away, long_kept, long_away, out_kept,
        out_away, grad_long_q,
    ) = fence(
        grad_combined, grad_attended_bf, gate_moved, up_core, up_away, long_kept, long_away, out_kept,
        out_away, grad_long_q,
    )

    up_moved = swap_inner(grid, up_away)
    long_core = grid.send(long_away, core=1)
    out_core = grid.send(out_away, core=1)
    gate_total = inner_total(grid, gate_kept, gate_core, gate_moved)
    grad_combined, gate_total = fence(grad_combined, gate_total)
    gate_sum = sum_outer(grid, gate_total)
    grad_cross_bf = (gate_tanh * grad_combined).astype(bf16)
    own_gate_grad = jnp.sum(
        jnp.sum(grad_combined * cross_out, axis=0).reshape(own_heads, HD), axis=1
    ) * (1.0 - jnp.tanh(own_gates) ** 2)
    grad_query, grad_text_key, grad_text_value = attend_call(
        "attend_cross_back", clip_column, cross_seen, query_bf, text_key_bf, text_value_bf, 0,
        (grad_cross_bf, cross_out, cross_lse),
    )
    grad_tkey, text_gain_grad = head_call(
        norm_heads_back, "norm_text_back", text_raw, 0, text_gain, text_turns, (grad_text_key,)
    )
    grad_tval = grad_text_value.astype(bf16)
    tkey_kept = contract_rows(feats[:, :half_text], grad_tkey).astype(bf16)
    tkey_away = contract_rows(feats[:, half_text:], grad_tkey).astype(bf16)
    long_away = core_away(grid, long_kept, long_core)
    out_away = core_away(grid, out_kept, out_core)
    (
        gate_sum, down_sum, up_moved, long_core, long_away, out_core, out_away, grad_query, grad_tkey,
        grad_tval, tkey_kept, tkey_away, grad_attended_bf,
    ) = fence(
        gate_sum, down_sum, up_moved, long_core, long_away, out_core, out_away, grad_query, grad_tkey,
        grad_tval, tkey_kept, tkey_away, grad_attended_bf,
    )

    long_moved = swap_inner(grid, long_away)
    out_moved = swap_inner(grid, out_away)
    tkey_core = grid.send(tkey_away, core=1)
    down_grad = down_sum.astype(f32)
    gate_grad = gate_sum.astype(f32)
    up_total = inner_total(grid, up_kept, up_core, up_moved)
    grad_attended_bf, up_total = fence(grad_attended_bf, up_total)
    up_sum = sum_outer(grid, up_total)
    grad_short_bf = grad_attended_bf[LONG_DEV:]
    grad_short_q, grad_short_k, grad_short_v = attend_call(
        "attend_short_back", short_clip, short_seen, short_query, short_key, short_value, 0,
        (grad_short_bf, short_out, short_lse),
    )
    tval_kept = contract_rows(feats[:, :half_text], grad_tval).astype(bf16)
    tval_away = contract_rows(feats[:, half_text:], grad_tval).astype(bf16)
    null_flags = jnp.concatenate([own_null, null_mask[clip_total - 1 :] == 1]).astype(f32)
    row_ids = jnp.arange(text_rows, dtype=jnp.int32)
    null_chosen = jnp.where(
        row_ids[None, :] % TXT_LEN == jnp.arange(TXT_LEN, dtype=jnp.int32)[:, None],
        jnp.repeat(null_flags, TXT_LEN)[None, :],
        0.0,
    ).astype(bf16)
    null_rows = jnp.concatenate(
        [dot(null_chosen, grad_tkey), dot(null_chosen, grad_tval)], axis=1
    ).astype(bf16)
    tkey_away = core_away(grid, tkey_kept, tkey_core)
    (
        up_sum, long_moved, out_moved, tkey_core, tkey_away, tval_kept, tval_away, grad_short_q,
        grad_short_k, grad_short_v, null_rows,
    ) = fence(
        up_sum, long_moved, out_moved, tkey_core, tkey_away, tval_kept, tval_away, grad_short_q,
        grad_short_k, grad_short_v, null_rows,
    )

    tkey_moved = swap_inner(grid, tkey_away)
    tval_core = grid.send(tval_away, core=1)
    null_moved = pair_sum(grid, null_rows, 1)
    up_grad = up_sum.astype(f32)
    both_total = join_sums(
        grid,
        [long_kept, long_core] + long_moved,
        [out_kept, out_core] + out_moved,
        LONG_DEV,
        depth,
    )
    both_sum = sum_outer(grid, both_total)
    grad_query_raw, query_gain_grad = head_call(
        norm_heads_back, "norm_queries_back", projected, 0, query_gain, turns,
        (grad_query, jnp.concatenate([grad_long_q, grad_short_q], axis=0)),
    )
    res_sums, attn_sums = row_call(
        sum_rows,
        "sum_rows",
        [clip_column, residual, ffn_in_part, ffn_in_moved, grad_residual, attn_part, attn_moved],
        [own_tanhs[0]],
        [],
        2,
    )
    tval_away = core_away(grid, tval_kept, tval_core)
    (
        both_sum, tkey_moved, tval_core, tval_away, null_moved, grad_query_raw, grad_short_k,
        grad_short_v, query_gain_grad, res_sums, attn_sums,
    ) = fence(
        both_sum, tkey_moved, tval_core, tval_away, null_moved, grad_query_raw, grad_short_k,
        grad_short_v, query_gain_grad, res_sums, attn_sums,
    )

    tval_moved = swap_inner(grid, tval_away)
    null_rows = null_rows + null_moved
    null_moved = pair_sum(grid, null_rows, 4)
    out_grad = both_sum[2 * LONG_DEV :].astype(f32)
    tkey_total = inner_total(grid, tkey_kept, tkey_core, tkey_moved)
    both_sum, tkey_total = fence(both_sum, tkey_total)
    tkey_sum = sum_outer(grid, tkey_total)
    own_terms = both_sum[: 2 * LONG_DEV].astype(f32)
    grad_key = jnp.concatenate([own_terms[:LONG_DEV], grad_short_k], axis=0)
    grad_value = jnp.concatenate([own_terms[LONG_DEV:], grad_short_v], axis=0)
    grad_key_raw, key_gain_grad = head_call(
        norm_heads_back, "norm_keys_back", projected, 1, key_gain, turns, (grad_key,)
    )
    grad_proj_bf = jnp.concatenate(
        [grad_query_raw, grad_key_raw, grad_value.astype(bf16)], axis=1
    )
    normed_part = rounded(
        jnp.concatenate(
            [contract_cols(grad_proj_bf, qkv_own), contract_cols(grad_proj_bf, qkv_other)], axis=1
        )
    ).astype(bf16)
    qkv_kept = contract_rows(normed_in[:, :half_width], grad_proj_bf).astype(bf16)
    qkv_away = contract_rows(normed_in[:, half_width:], grad_proj_bf).astype(bf16)
    first_rows = token_count // 2
    moved_first = swap_txt(normed_part[:first_rows])
    moved_last = swap_txt(normed_part[first_rows:])
    qkv_core = grid.send(qkv_away, core=1)
    qkv_away = core_away(grid, qkv_kept, qkv_core)
    (
        tkey_sum, tval_moved, null_moved, moved_first, qkv_kept, qkv_core, qkv_away, grad_residual,
    ) = fence(
        tkey_sum, tval_moved, null_moved, moved_first, qkv_kept, qkv_core, qkv_away, grad_residual,
    )

    qkv_moved = swap_inner(grid, qkv_away)
    null_rows = null_rows + null_moved
    tval_total = inner_total(grid, tval_kept, tval_core, tval_moved)
    tval_total, null_rows, moved_first, grad_residual = fence(
        tval_total, null_rows, moved_first, grad_residual
    )
    tval_sum = sum_outer(grid, tval_total)
    null_moved = pair_sum(grid, null_rows, 8)
    normed_moved = jnp.concatenate([moved_first, moved_last], axis=0)
    video_high, video_low, hidden_sums = row_call(
        last_rows,
        "last_rows",
        [clip_column, hidden, normed_part, normed_moved, grad_residual],
        [own_scales[0], gains],
        [bf16, bf16],
        1,
    )
    hidden_sums, tval_sum, qkv_moved, null_rows, null_moved = fence(
        hidden_sums, tval_sum, qkv_moved, null_rows, null_moved
    )

    text_grad = jnp.stack([tkey_sum.astype(f32), tval_sum.astype(f32)], axis=1)
    qkv_total = inner_total(grid, qkv_kept, qkv_core, qkv_moved)
    hidden_sums, qkv_total = fence(hidden_sums, qkv_total)
    qkv_sum = sum_outer(grid, qkv_total)

    grad_mod = jnp.stack(
        [
            hidden_sums * gains[0],
            attn_sums * gains[1] * (1.0 - own_tanhs[0] * own_tanhs[0]),
            res_sums * gains[2],
            ffn_sums * gains[3] * (1.0 - own_tanhs[1] * own_tanhs[1]),
        ],
        axis=1,
    ).reshape(-1, model_width)
    gain_rows = jnp.stack(
        [
            jnp.sum(hidden_sums * own_scales[0], axis=0),
            jnp.sum(attn_sums * own_tanhs[0], axis=0),
            jnp.sum(res_sums * own_scales[1], axis=0),
            jnp.sum(ffn_sums * own_tanhs[1], axis=0),
        ],
        axis=0,
    )
    rows = contract_cols(
        jnp.concatenate(split_three(jnp.concatenate([grad_mod, gain_rows], axis=0)), axis=0),
        one_hot,
    )
    row_count = rows.shape[0] // 3
    rows = rows[:row_count] + rows[row_count : 2 * row_count] + rows[2 * row_count :]
    gain_rows = rows[-4:]
    own_grad_mod = rows[:-4].reshape(short_clips + 1, 4 * model_width)
    column_count = mod_part.shape[1]
    mod_blocks = lax.dynamic_index_in_dim(
        own_grad_mod.reshape(short_clips + 1, seq_count, 2, column_count),
        txt_index,
        2,
        keepdims=False,
    )
    mod_blocks = turn_seq(grid, jnp.transpose(mod_blocks, (1, 0, 2)))
    null_rows = null_rows + null_moved
    null_rows = sum_seq(grid, null_rows + pair_sum(grid, null_rows, 2), 16)
    null_part = jnp.concatenate(
        [
            contract_cols(null_rows[:, :own_width], key_piece)
            + contract_cols(null_rows[:, own_width:], value_piece)
            for key_piece, value_piece in zip(tkey_pieces, tval_pieces)
        ],
        axis=1,
    )
    null_part = rounded(null_part).astype(bf16)
    null_moved = swap_txt(null_part)
    video_grad = contract_cols(video_high, one_hot) + contract_cols(video_low, one_hot)
    slice_grad_mod = jnp.concatenate(
        [
            mod_blocks[:, :short_clips].reshape(clip_total - 1, column_count),
            jnp.sum(mod_blocks[:, short_clips], axis=0, keepdims=True),
        ],
        axis=0,
    )
    ada_weight_grad = lax.dot_general(
        shifted.astype(f32), slice_grad_mod, (((0,), (0,)), ((), ())), precision=highest
    )
    ada_bias_grad = jnp.sum(slice_grad_mod, axis=0)
    grad_shifted = lax.dot_general(
        slice_grad_mod, ada_weight.astype(f32), (((1,), (1,)), ((), ())), precision=highest
    )
    cond_value = condition.astype(f32)
    cond_sigmoid = jax.nn.sigmoid(cond_value)
    cond_part = grad_shifted * cond_sigmoid * (1.0 + cond_value * (1.0 - cond_sigmoid))

    head_rows = [
        lax.dynamic_update_slice(jnp.zeros((1, model_width), f32), rows, (0, head_start * HD))
        for rows in (query_gain_grad, key_gain_grad, text_gain_grad)
    ]
    gains_term = jnp.concatenate([jnp.where(first_half, gain_rows, 0.0)] + head_rows, axis=0)
    gates_term = lax.dynamic_update_slice_in_dim(jnp.zeros((H,), f32), own_gate_grad, head_start, 0)
    cond_count, gains_count = cond_part.size, gains_term.size
    packed = jnp.concatenate([cond_part.reshape(-1), gains_term.reshape(-1), gates_term])
    packed = jnp.pad(packed, (0, -packed.shape[0] % 1024)).reshape(-1, 1024)
    packed = packed + pair_sum(grid, packed, 1)
    packed = packed + pair_sum(grid, packed, 2)
    packed = packed + swap_txt(packed)
    packed, qkv_sum = fence(packed, qkv_sum)
    packed = packed + pair_sum(grid, packed, 4)
    packed, null_moved = fence(packed, null_moved)
    null_grad = reorder_columns(
        null_part.astype(f32) + null_moved.astype(f32), owners, False
    )
    qkv_grad = qkv_sum.astype(f32).reshape(depth, 3, own_width)
    packed = sum_seq(grid, packed, 8)
    packed = packed.reshape(-1)
    condition_grad = packed[:cond_count].reshape(cond_part.shape)
    norm_gains_grad = packed[cond_count : cond_count + gains_count].reshape(gains_term.shape)
    head_gates_grad = packed[cond_count + gains_count : cond_count + gains_count + H]
    return (
        block_out,
        video_grad,
        condition_grad,
        qkv_grad,
        out_grad,
        gate_grad,
        up_grad,
        down_grad,
        text_grad,
        ada_weight_grad,
        ada_bias_grad,
        null_grad,
        norm_gains_grad,
        head_gates_grad,
    )


def solution(mesh):
    placed = (
        P("seq", None),
        P("seq", None),
        P(),
        P("seq", "txt", None),
        P("txt", None),
        P("txt", None),
        P("seq", None, "txt"),
        P("seq", "txt"),
        P("seq", "txt"),
        P("seq", "txt"),
        P("seq", "txt"),
        P("seq", None, "txt"),
        P(None, ("seq", "txt")),
        P(("seq", "txt")),
        P(),
        P(),
        P("seq", None),
        P(),
        P(),
    )
    return jax.shard_map(
        local,
        mesh=mesh,
        in_specs=placed,
        out_specs=(
            P("seq", None),
            P("seq", None),
            P(),
            P("seq", None, "txt"),
            P("seq", "txt"),
            P("seq", "txt"),
            P("seq", "txt"),
            P("seq", "txt"),
            P("seq", None, "txt"),
            P(None, ("seq", "txt")),
            P(("seq", "txt")),
            P(),
            P(),
            P(),
        ),
        check_vma=False,
    )
```
